32 devices in a mesh: dp: 2 (over core), tensor: 4 (over y, x), corpus: 4 (over z).
Axes of the slice: x: 2, y: 2, z: 4, core: 2. Of those that a mesh axis runs over, the one named last changes fastest.
Arguments:
- queries: bfloat16 [512, 2048], P(('dp', 'tensor', 'corpus')), may hold values from -24 to 24
- passages: bfloat16 [8192, 2048], P(('dp', 'corpus'), 'tensor'), may hold values from -6 to 6
- pos_ids: int32 [512], P(('dp', 'tensor', 'corpus')), may hold values from 0 to 8191, as said below
- neg_ids: int32 [512, 32], P(('dp', 'tensor', 'corpus')), may hold values from 0 to 8191, as said below
Outputs:
- grad_query: float32 [512, 2048], P(('dp', 'tensor', 'corpus'))
- losses: float32 [512], P(('dp', 'tensor', 'corpus'))
- grad_pass: float32 [8192, 2048], P(('dp', 'corpus'), 'tensor')
The draws below stay inside these ranges and needn't reach their ends.
Inputs may be any that keep to these rules, and one draw needn't show every extreme that they name: `pos_ids`: together with neg_ids: the ids named by the 16 queries of one device, positives and negatives together, fall at most 132 times into one block of 1024 passage rows (rows b * 1024 to (b + 1) * 1024 - 1), and exactly 132 times into one block that is the same for every device. Ids may repeat. `neg_ids`: counted together with pos_ids as stated there.
All inputs are finite; a program needn't handle non-finite values.
Results may differ from the reference program's by a relative error of at most 0.0035.
Values may be sent and summed in bfloat16 or wider, within the bound.
No kernel may reach another device: no remote copies, remote signals or barrier semaphores. Data moves between devices by JAX's collectives and lax.ppermute only.
A program may use at most 128 MiB of HBM per device.

```python
import jax
import jax.numpy as jnp
from jax import lax

D = 2048
K = 32
QD = 16
OWNERS = 8
PB = 1024
CAP = 132
Q = 512
P_SIZE = 8192
N_DP = 2
N_TENSOR = 4
N_CORPUS = 4


def request_ids(key):
    base_key = jax.random.fold_in(key, 11)
    pick_key, block_key = jax.random.split(base_key)
    busiest = jax.random.randint(pick_key, (), 0, OWNERS)
    slot_total = QD * (K + 1)

    def one_block(part_key):
        key_pool, key_mix, key_local = jax.random.split(part_key, 3)
        others = jnp.arange((OWNERS - 1) * CAP, dtype=jnp.int32) // CAP
        others = (others + busiest + 1) % OWNERS
        others = jax.random.permutation(key_pool, others)[:slot_total - CAP]
        owner_ids = jnp.concatenate([jnp.full((CAP,), busiest, jnp.int32), others.astype(jnp.int32)])
        owner_ids = jax.random.permutation(key_mix, owner_ids)
        local_ids = jax.random.randint(key_local, (slot_total,), 0, PB)
        return (owner_ids * PB + local_ids).reshape(QD, K + 1)
    block_keys = jax.random.split(block_key, Q // QD)
    return jax.vmap(one_block)(block_keys).reshape(Q, K + 1).astype(jnp.int32)


def passage_values(key):
    value_key = jax.random.fold_in(key, 23)
    return jnp.clip(jax.random.normal(value_key, (P_SIZE, D), jnp.float32), -6.0, 6.0)


def draw_passages(key, part):
    return passage_values(key).astype(jnp.bfloat16)


def draw_queries(key, part):
    noise_key = jax.random.fold_in(key, 31)
    values = jnp.clip(jax.random.normal(noise_key, (Q, D), jnp.float32), -6.0, 6.0)
    return values.astype(jnp.bfloat16)


def draw_pos_ids(key, part):
    return request_ids(key)[:, 0]


def draw_neg_ids(key, part):
    return request_ids(key)[:, 1:]


def setup_inputs(seed: int = 0) -> dict:
    key_of = jax.random.split(jax.random.key(seed), 5)
    return {
        "queries": draw_queries(jax.random.fold_in(key_of[4], 71), 0),
        "passages": draw_passages(jax.random.fold_in(key_of[4], 71), 0),
        "pos_ids": draw_pos_ids(jax.random.fold_in(key_of[4], 71), 0),
        "neg_ids": draw_neg_ids(jax.random.fold_in(key_of[4], 71), 0),
    }


def regroup(values):
    shaped = values.reshape((N_DP, N_TENSOR * N_CORPUS, QD) + values.shape[1:])
    shaped = jnp.swapaxes(shaped, 0, 1)
    return shaped.reshape((N_TENSOR * N_CORPUS, N_DP * QD) + values.shape[1:])


def ungroup(values):
    shaped = values.reshape((N_TENSOR * N_CORPUS, N_DP, QD) + values.shape[2:])
    shaped = jnp.swapaxes(shaped, 0, 1)
    return shaped.reshape((Q,) + values.shape[2:])


def reference(queries, passages, pos_ids, neg_ids):
    score_scale = D ** -0.5
    columns = N_DP * QD

    def group_step(grad_pass, group):
        query_rows, pos_group, neg_group = group
        pos_rows = jnp.take(passages, pos_group, axis=0)
        neg_rows = jnp.take(passages, neg_group, axis=0)
        in_scores = jnp.dot(query_rows, pos_rows.T, preferred_element_type=jnp.float32) * score_scale
        neg_scores = jnp.einsum("md,mkd->mk", query_rows.astype(jnp.float32), neg_rows.astype(jnp.float32)) * score_scale
        logits = jnp.concatenate([in_scores, neg_scores], axis=1)
        row_max = jnp.max(logits, axis=1, keepdims=True)
        exponent = jnp.exp(logits - row_max)
        denominator = jnp.sum(exponent, axis=1, keepdims=True)
        target = (jnp.arange(columns + K)[None, :] == jnp.arange(columns)[:, None]).astype(jnp.float32)
        losses = jnp.log(denominator[:, 0]) + row_max[:, 0] - jnp.sum(target * logits, axis=1)
        weights = (exponent / denominator - target).astype(jnp.bfloat16)
        in_weights = weights[:, :columns]
        neg_weights = weights[:, columns:]
        grad_query = jnp.dot(in_weights, pos_rows, preferred_element_type=jnp.float32)
        grad_query = grad_query + jnp.einsum("mk,mkd->md", neg_weights.astype(jnp.float32), neg_rows.astype(jnp.float32))
        grad_query = grad_query * score_scale
        pos_grad = jnp.dot(in_weights.T, query_rows, preferred_element_type=jnp.float32) * score_scale
        neg_grad = neg_weights.astype(jnp.float32)[:, :, None] * query_rows.astype(jnp.float32)[:, None, :] * score_scale
        row_grads = jnp.concatenate([pos_grad[:, None, :], neg_grad], axis=1).astype(jnp.bfloat16)
        row_grads = lax.optimization_barrier(row_grads).astype(jnp.float32)
        named_ids = jnp.concatenate([pos_group[:, None], neg_group], axis=1).reshape(-1)
        grad_pass = grad_pass.at[named_ids].add(row_grads.reshape(-1, D))
        return grad_pass, (grad_query, losses)

    grad_pass, outputs = lax.scan(group_step, jnp.zeros((P_SIZE, D), jnp.float32), (regroup(queries), regroup(pos_ids), regroup(neg_ids)))
    grad_query, losses = outputs
    return (ungroup(grad_query), ungroup(losses), grad_pass)
```

```python
import jax
import jax.numpy as jnp
from jax import lax
from jax.experimental import pallas as pl
from jax.experimental.pallas import tpu as pltpu
from jax.sharding import PartitionSpec as P

LANES = 128


def pairs(size, bit):
    return [(i, i ^ bit) for i in range(size)]


def swap(value, axis, bit):
    return lax.ppermute(value, axis, pairs(lax.axis_size(axis), bit))


def gather_pieces(pieces, axis):
    bit = 1
    while bit < lax.axis_size(axis):
        pieces = pieces + [swap(piece, axis, bit) for piece in pieces]
        bit *= 2
    return pieces


def scatter_sum(pieces, axis):
    bit = lax.axis_size(axis) // 2
    while bit:
        pieces = [
            mine + swap(theirs, axis, bit) for mine, theirs in zip(pieces[:bit], pieces[bit:])
        ]
        bit //= 2
    return pieces[0]


class Sizes:
    def __init__(self, queries, passages, neg_ids):
        self.own, self.feat = queries.shape
        self.block, self.width = passages.shape
        self.negs = neg_ids.shape[1]
        self.dp = lax.axis_size("dp")
        self.tensor = lax.axis_size("tensor")
        self.corpus = lax.axis_size("corpus")
        self.groups = self.tensor * self.corpus
        self.half = self.groups * self.own
        self.rows = self.dp * self.half
        self.columns = self.dp * self.own
        self.items = self.columns + self.negs
        self.lanes = -(-self.items // LANES) * LANES
        self.pack = max(1, LANES // self.items)
        self.packed = self.rows // self.pack
        self.part = self.packed // self.dp
        self.neg_at = self.columns % LANES
        self.pos_at = 0 if self.neg_at else self.negs
        self.chunks = self.block // LANES
        self.scale = self.feat ** (-0.5)
        self.vmem = min(60, 16 + 10 * self.rows // 1024) * 2**20


def score_kernel(z, *refs):
    arrived = refs[: z.dp]
    passage_ref = refs[z.dp]
    query_ref, index_ref = refs[z.dp + 1 : z.dp + 3]
    part_refs = refs[z.dp + 3 : 2 * z.dp + 3]
    id_ref, local_ref, logit_ref = refs[2 * z.dp + 3 :]
    d, t, c = (lax.axis_index(a) for a in ("dp", "tensor", "corpus"))
    for sd in range(z.dp):
        for sc in range(z.corpus):
            for st in range(z.tensor):
                source = pl.ds((sc * z.tensor + st) * z.own, z.own)
                place = (((d ^ sd) * z.tensor + (t ^ st)) * z.corpus + (c ^ sc)) * z.own
                place = pl.ds(pl.multiple_of(place, z.own), z.own)
                query_ref[place, :] = arrived[sd][source, : z.width]
                code = arrived[sd][source, z.width :].astype(jnp.float32)
                id_ref[place, :] = code * 256.0 + pltpu.roll(code, LANES // 2, 1)
    first = ((d * z.corpus + c) * z.block).astype(jnp.float32)
    wide = -(-z.columns // LANES) * LANES
    row = lax.broadcasted_iota(jnp.int32, (z.half, wide), 0) & (z.own - 1)
    col = lax.broadcasted_iota(jnp.int32, (z.half, wide), 1)
    group_ids = jnp.zeros((z.groups, wide), jnp.float32)
    for h in range(z.dp):
        ids = id_ref[pl.ds(h * z.half, z.half), :]
        pos = jnp.broadcast_to(ids[:, z.pos_at : z.pos_at + 1], (z.half, wide))
        kept = jnp.where(col == row + h * z.own, pos, 0.0)
        group_ids += jnp.sum(kept.reshape(z.groups, z.own, wide), axis=1)
    batch_ids = jnp.broadcast_to(group_ids[:, None, :], (z.groups, z.own, wide))
    batch_ids = batch_ids.reshape(z.half, wide)
    lane = lax.broadcasted_iota(jnp.int32, (z.half, LANES), 1)
    for h in range(z.dp):
        ids = id_ref[pl.ds(h * z.half, z.half), :]
        for base in range(0, z.lanes, LANES):
            named = ids
            if base < z.columns:
                named = jnp.where(lane + base < z.columns, batch_ids[:, base : base + LANES], ids)
            local = named - first
            inside = (local >= 0.0) & (local < float(z.block)) & (lane + base < z.items)
            local_ref[pl.ds(h * z.half, z.half), base : base + LANES] = jnp.where(
                inside, local, -float(2**20)
            ).astype(jnp.int32)
    step = min(z.rows, 256)

    def score(i, carry):
        at = pl.ds(pl.multiple_of(i * step, step), step)
        scores = lax.dot_general(
            query_ref[at, :], passage_ref[...], (((1,), (1,)), ((), ())),
            preferred_element_type=jnp.float32,
        )
        for base in range(0, z.lanes, LANES):
            local = local_ref[at, base : base + LANES]
            chunk, within = local >> 7, local & (LANES - 1)
            picked = jnp.zeros((step, LANES), jnp.float32)
            for j in range(z.chunks):
                found = jnp.take_along_axis(scores[:, j * LANES : (j + 1) * LANES], within, axis=1)
                picked = jnp.where(chunk == j, found, picked)
            logit_ref[at, base : base + LANES] = picked
        return carry

    lax.fori_loop(0, z.rows // step, score, 0)
    lane = lax.broadcasted_iota(jnp.int32, (z.packed, z.lanes), 1)
    index = local_ref[pl.ds(0, z.packed), :]
    for h in range(1, z.pack):
        other = pltpu.roll(local_ref[pl.ds(h * z.packed, z.packed), :], h * z.items, 1)
        index = jnp.where(lane < h * z.items, index, other)
    index_ref[...] = index
    for s in range(z.dp):
        at = pl.multiple_of((d ^ s) * z.part, z.part)
        total = logit_ref[pl.ds(at, z.part), :]
        for h in range(1, z.pack):
            more = logit_ref[pl.ds(pl.multiple_of(h * z.packed + at, z.part), z.part), :]
            total = total + pltpu.roll(more, h * z.items, 1)
        part_refs[s][...] = total


def weight_kernel(z, *refs):
    parts = refs[: z.dp]
    index_ref, passage_ref = refs[z.dp : z.dp + 2]
    dense_ref, loss_ref = refs[z.dp + 2 : z.dp + 4]
    grad_refs = refs[z.dp + 4 : 2 * z.dp + 4]
    logit_ref, tile_ref = refs[2 * z.dp + 4 :]
    d, t, c = (lax.axis_index(a) for a in ("dp", "tensor", "corpus"))
    for s in range(z.dp):
        at = pl.multiple_of((d ^ s) * z.part, z.part)
        logit_ref[pl.ds(at, z.part), :] = parts[s][...] * z.scale

    def softmax(logits, first_row):
        shape = logits.shape
        lane = lax.broadcasted_iota(jnp.int32, shape, 1)
        row = lax.broadcasted_iota(jnp.int32, shape, 0) + first_row
        weights = jnp.zeros(shape, jnp.float32)
        losses = []
        for h in range(z.pack):
            mask = (lane >= h * z.items) & (lane < (h + 1) * z.items)
            top = jnp.max(jnp.where(mask, logits, -jnp.inf), axis=1, keepdims=True)
            exponent = jnp.where(mask, jnp.exp(logits - top), 0.0)
            denominator = jnp.sum(exponent, axis=1, keepdims=True)
            query = row + h * z.packed
            own = (query // z.half) * z.own + (query & (z.own - 1)) + h * z.items
            target = jnp.where(lane == own, 1.0, 0.0)
            weights = jnp.where(mask, exponent / denominator - target, weights)
            chosen = jnp.sum(target * jnp.where(mask, logits, 0.0), axis=1, keepdims=True)
            losses.append(jnp.log(denominator) + top - chosen)
        return weights, losses

    mine = ((d * z.tensor + t) * z.corpus + c) * z.own
    first = pl.multiple_of(mine % z.packed, z.own)
    _, losses = softmax(logit_ref[pl.ds(first, z.own), :], first)
    loss = losses[0]
    for h in range(1, z.pack):
        loss = jnp.where(mine // z.packed == h, losses[h], loss)
    loss_ref[...] = jnp.broadcast_to(loss, (z.own, LANES))

    step = min(z.packed, 256)

    def weigh(i, carry):
        at = pl.ds(pl.multiple_of(i * step, step), step)
        weights, _ = softmax(logit_ref[at, :], i * step)
        logit_ref[at, :] = weights.astype(jnp.bfloat16).astype(jnp.float32)
        return carry

    lax.fori_loop(0, z.packed // step, weigh, 0)

    high = z.pack * z.chunks
    tall = lax.broadcasted_iota(jnp.int32, (high, z.lanes), 0)
    shift = lax.broadcasted_iota(jnp.int32, (1, z.lanes), 1) // z.items * z.chunks
    spread = lax.broadcasted_iota(jnp.int32, (LANES, z.lanes), 0).astype(jnp.bfloat16)

    def place(i, carry):
        for j in range(8):
            r = i * 8 + j
            local = index_ref[pl.ds(r, 1), :]
            chunk = (local >> 7) + shift
            within = (local & (LANES - 1)).astype(jnp.bfloat16)
            left = jnp.where(
                jnp.broadcast_to(chunk, (high, z.lanes)) == tall,
                jnp.broadcast_to(logit_ref[pl.ds(r, 1), :], (high, z.lanes)), 0.0,
            ).astype(jnp.bfloat16)
            right = jnp.where(
                jnp.broadcast_to(within, (LANES, z.lanes)) == spread,
                jnp.bfloat16(1), jnp.bfloat16(0),
            )
            tiles = lax.dot_general(
                left, right, (((1,), (1,)), ((), ())), preferred_element_type=jnp.float32
            )
            for h in range(z.pack):
                at = pl.multiple_of((h * z.packed + r) * z.chunks, z.chunks)
                tile_ref[pl.ds(at, z.chunks), :] = tiles[h * z.chunks : (h + 1) * z.chunks, :]
        return carry

    lax.fori_loop(0, z.packed // 8, place, 0)
    for j in range(z.chunks):
        dense_ref[:, j * LANES : (j + 1) * LANES] = tile_ref[
            pl.ds(j, z.rows, stride=z.chunks), :
        ].astype(jnp.bfloat16)
    for s in range(z.dp):
        at = pl.multiple_of((d ^ s) * z.half, z.half)
        grad_refs[s][...] = jnp.dot(
            dense_ref[pl.ds(at, z.half), :], passage_ref[...], preferred_element_type=jnp.float32
        )


def passage_kernel(z, dense_ref, query_ref, out_ref):
    def one(i, carry):
        at = pl.ds(pl.multiple_of(i * 256, 256), 256)
        out_ref[at, :] = z.scale * lax.dot_general(
            dense_ref[:, at], query_ref[...], (((0,), (0,)), ((), ())),
            preferred_element_type=jnp.float32,
        )
        return carry

    lax.fori_loop(0, z.block // 256, one, 0)


def query_kernel(z, arrived_ref, out_ref):
    for t in range(z.tensor):
        total = arrived_ref[t * z.corpus]
        for c in range(1, z.corpus):
            total = total + arrived_ref[t * z.corpus + c]
        out_ref[:, t * z.width : (t + 1) * z.width] = total * z.scale


def call(z, kernel, outs, scratch, args, flops):
    moved = sum(a.size * a.dtype.itemsize for a in args)
    moved += sum(o.size * jnp.dtype(o.dtype).itemsize for o in outs)
    return pl.pallas_call(
        lambda *refs: kernel(z, *refs),
        out_shape=outs,
        in_specs=[pl.BlockSpec(memory_space=pltpu.VMEM)] * len(args),
        out_specs=[pl.BlockSpec(memory_space=pltpu.VMEM)] * len(outs),
        scratch_shapes=scratch,
        compiler_params=pltpu.CompilerParams(vmem_limit_bytes=z.vmem),
        cost_estimate=pl.CostEstimate(flops=flops, bytes_accessed=moved, transcendentals=0),
    )(*args)


def body(queries, passages, pos_ids, neg_ids):
    z = Sizes(queries, passages, neg_ids)
    f32, bf16 = jnp.float32, jnp.bfloat16
    shape = jax.ShapeDtypeStruct
    t = lax.axis_index("tensor")

    pos = jnp.broadcast_to(pos_ids[:, None], (z.own, LANES // 2))
    ids = jnp.concatenate(
        [pos[:, : z.neg_at], neg_ids, pos[:, : LANES // 2 - z.neg_at - z.negs]], axis=1
    )
    code = jnp.concatenate([ids >> 8, ids & 255], axis=1).astype(bf16)
    plane = []
    for s in range(z.tensor):
        piece = lax.dynamic_slice_in_dim(queries, (t ^ s) * z.width, z.width, axis=1)
        piece = jnp.concatenate([piece, code], axis=1)
        plane.append(swap(piece, "tensor", s) if s else piece)
    plane = jnp.concatenate(plane, axis=0)
    chip = [plane] + [swap(plane, "corpus", s) for s in range(1, z.corpus)]
    arrived = gather_pieces([jnp.concatenate(chip, axis=0)], "dp")

    work = 2 * z.rows * z.block * z.width
    query_rows, index, *parts = call(
        z, score_kernel,
        [shape((z.rows, z.width), bf16), shape((z.packed, z.lanes), jnp.int32)]
        + [shape((z.part, z.lanes), f32)] * z.dp,
        [
            pltpu.VMEM((z.rows, LANES), f32),
            pltpu.VMEM((z.rows, z.lanes), jnp.int32),
            pltpu.VMEM((z.rows, z.lanes), f32),
        ],
        arrived + [passages], work,
    )
    total = scatter_sum(parts, "dp")
    bit = 1
    while bit < z.tensor:
        total = total + swap(total, "tensor", bit)
        bit *= 2
    total = sum([swap(total, "corpus", s) for s in range(1, z.corpus)], total)
    logits = gather_pieces([total], "dp")

    dense, loss, *grads = call(
        z, weight_kernel,
        [shape((z.rows, z.block), bf16), shape((z.own, LANES), f32)]
        + [shape((z.half, z.width), f32)] * z.dp,
        [
            pltpu.VMEM((z.packed, z.lanes), f32),
            pltpu.VMEM((z.rows * z.chunks, LANES), f32),
        ],
        logits + [index, passages], 2 * work,
    )
    (grad_pass,) = call(
        z, passage_kernel, [shape((z.block, z.width), f32)], [], [dense, query_rows], work
    )
    half = scatter_sum(grads, "dp")
    half = half.reshape(z.groups, z.own, z.width)
    half = lax.all_to_all(half, ("tensor", "corpus"), split_axis=0, concat_axis=0, tiled=True)
    (grad_query,) = call(
        z, query_kernel, [shape((z.own, z.feat), f32)], [], [half], half.size
    )
    return (grad_query, loss[:, 0], grad_pass)


def solution(mesh):
    spread = ("dp", "tensor", "corpus")
    in_specs = (P(spread, None), P(("dp", "corpus"), "tensor"), P(spread), P(spread, None))
    out_specs = (P(spread, None), P(spread), P(("dp", "corpus"), "tensor"))
    return jax.shard_map(body, mesh=mesh, in_specs=in_specs, out_specs=out_specs, check_vma=False)
```

```python
import jax
import jax.numpy as jnp
from jax import lax
from jax.experimental import pallas as pl
from jax.experimental.pallas import tpu as pltpu
from jax.sharding import PartitionSpec as P

LANES = 128


def pairs(size, bit):
    return [(i, i ^ bit) for i in range(size)]


def swap(value, axis, bit):
    return lax.ppermute(value, axis, pairs(lax.axis_size(axis), bit))


def gather_pieces(pieces, axis):
    bit = 1
    while bit < lax.axis_size(axis):
        pieces = pieces + [swap(piece, axis, bit) for piece in pieces]
        bit *= 2
    return pieces


def scatter_sum(pieces, axis):
    bit = lax.axis_size(axis) // 2
    while bit:
        pieces = [
            mine + swap(theirs, axis, bit) for mine, theirs in zip(pieces[:bit], pieces[bit:])
        ]
        bit //= 2
    return pieces[0]


def turn_order(size):
    return [1] + list(range(size - 1, 1, -1))


class Sizes:
    def __init__(self, queries, passages, neg_ids):
        self.own, self.feat = queries.shape
        self.block, self.width = passages.shape
        self.negs = neg_ids.shape[1]
        self.dp = lax.axis_size("dp")
        self.tensor = lax.axis_size("tensor")
        self.corpus = lax.axis_size("corpus")
        self.groups = self.tensor * self.corpus
        self.half = self.groups * self.own
        self.rows = self.dp * self.half
        self.columns = self.dp * self.own
        self.items = self.columns + self.negs
        self.lanes = -(-self.items // LANES) * LANES
        self.pack = max(1, LANES // self.items)
        self.packed = self.rows // self.pack
        self.part = self.packed // self.dp
        self.neg_at = self.columns % LANES
        self.pos_at = 0 if self.neg_at else self.negs
        self.chunks = self.block // LANES
        self.scale = self.feat ** (-0.5)
        self.deep = 2 * LANES
        self.seats = self.deep // self.negs
        self.nrows = self.rows // self.seats
        self.joint = max(1, self.deep // self.columns)
        self.run = self.joint * self.own
        self.sets = self.groups // self.joint
        self.vmem = min(60, 16 + 10 * self.rows // 1024) * 2**20


def message_kernel(z, pos_in, neg_in, query_in, *refs):
    piece_refs = refs[: z.tensor]
    pos_ref, neg_ref, query_ref, sems = refs[z.tensor :]
    t = lax.axis_index("tensor")
    moves = [
        pltpu.make_async_copy(source, target, sems.at[i])
        for i, (source, target) in enumerate(
            [(pos_in, pos_ref), (neg_in, neg_ref), (query_in, query_ref)]
        )
    ]
    for move in moves:
        move.start()
    for move in moves:
        move.wait()
    half = LANES // 2
    row = lax.broadcasted_iota(jnp.int32, (z.own, half), 0)
    pos = jnp.zeros((z.own, half), jnp.int32)
    for i in range(z.own):
        pos = jnp.where(row == i, pos_ref[i], pos)
    ids = [neg_ref[...], pos[:, : half - z.neg_at - z.negs]]
    ids = jnp.concatenate([part for part in [pos[:, : z.neg_at]] + ids if part.shape[1]], axis=1)
    ids = jnp.concatenate([ids >> 8, ids & 255], axis=1)
    code = ids.astype(jnp.float32).astype(jnp.bfloat16)
    for s in range(z.tensor):
        at = pl.ds(pl.multiple_of((t ^ s) * z.width, LANES), z.width)
        piece_refs[s][:, : z.width] = query_ref[:, at]
        piece_refs[s][:, z.width :] = code


def fetch_kernel(z, block_ref, passage_ref, sem):
    fetch = pltpu.make_async_copy(block_ref, passage_ref, sem)
    fetch.start()
    fetch.wait()


def seat_rows(z, out_ref, source):
    lane = lax.broadcasted_iota(jnp.int32, (z.nrows, LANES), 1)
    per = LANES // z.negs
    for chunk in range(z.deep // LANES):
        packed = None
        for k in range(per):
            ref, row, at = source(chunk * per + k)
            base = at // LANES * LANES
            piece = ref[pl.ds(row, z.nrows), base : base + LANES]
            turn = (k * z.negs - at) % LANES
            piece = pltpu.roll(piece, turn, 1) if turn else piece
            packed = piece if packed is None else jnp.where(lane < k * z.negs, packed, piece)
        out_ref[:, chunk * LANES : (chunk + 1) * LANES] = packed


def score_kernel(z, *refs):
    arrived = refs[: z.dp]
    passage_ref = refs[z.dp]
    query_ref, index_ref, pos_ref = refs[z.dp + 1 : z.dp + 4]
    part_refs = refs[z.dp + 4 : 2 * z.dp + 4]
    id_ref, local_ref, logit_ref = refs[2 * z.dp + 4 :]
    d, t, c = (lax.axis_index(a) for a in ("dp", "tensor", "corpus"))
    for sd in range(z.dp):
        for sc in range(z.corpus):
            for st in range(z.tensor):
                source = pl.ds((sc * z.tensor + st) * z.own, z.own)
                place = (((d ^ sd) * z.tensor + (t ^ st)) * z.corpus + (c ^ sc)) * z.own
                place = pl.ds(pl.multiple_of(place, z.own), z.own)
                query_ref[place, :] = arrived[sd][source, : z.width]
                code = arrived[sd][source, z.width :].astype(jnp.float32)
                id_ref[place, :] = code * 256.0 + pltpu.roll(code, LANES // 2, 1)
    first = ((d * z.corpus + c) * z.block).astype(jnp.float32)
    wide = -(-z.columns // LANES) * LANES
    row = lax.broadcasted_iota(jnp.int32, (z.half, wide), 0) & (z.own - 1)
    col = lax.broadcasted_iota(jnp.int32, (z.half, wide), 1)
    group_ids = jnp.zeros((z.groups, wide), jnp.float32)
    for h in range(z.dp):
        ids = id_ref[pl.ds(h * z.half, z.half), :]
        pos = jnp.broadcast_to(ids[:, z.pos_at : z.pos_at + 1], (z.half, wide))
        pos_ref[pl.ds(h * z.half, z.half), :] = (pos[:, :LANES] - first).astype(jnp.int32)
        kept = jnp.where(col == row + h * z.own, pos, 0.0)
        group_ids += jnp.sum(kept.reshape(z.groups, z.own, wide), axis=1)
    batch_ids = jnp.broadcast_to(group_ids[:, None, :], (z.groups, z.own, wide))
    batch_ids = batch_ids.reshape(z.half, wide)
    lane = lax.broadcasted_iota(jnp.int32, (z.half, LANES), 1)
    for h in range(z.dp):
        ids = id_ref[pl.ds(h * z.half, z.half), :]
        for base in range(0, z.lanes, LANES):
            named = ids
            if base < z.columns:
                named = jnp.where(lane + base < z.columns, batch_ids[:, base : base + LANES], ids)
            local = named - first
            inside = (local >= 0.0) & (local < float(z.block)) & (lane + base < z.items)
            local_ref[pl.ds(h * z.half, z.half), base : base + LANES] = jnp.where(
                inside, local, -float(2**20)
            ).astype(jnp.int32)
    step = min(z.rows, 256)

    def score(i, carry):
        at = pl.ds(pl.multiple_of(i * step, step), step)
        scores = lax.dot_general(
            query_ref[at, :], passage_ref[...], (((1,), (1,)), ((), ())),
            preferred_element_type=jnp.float32,
        )
        for base in range(0, z.lanes, LANES):
            local = local_ref[at, base : base + LANES]
            chunk, within = local >> 7, local & (LANES - 1)
            picked = jnp.zeros((step, LANES), jnp.float32)
            for j in range(z.chunks):
                found = jnp.take_along_axis(scores[:, j * LANES : (j + 1) * LANES], within, axis=1)
                picked = jnp.where(chunk == j, found, picked)
            logit_ref[at, base : base + LANES] = picked
        return carry

    lax.fori_loop(0, z.rows // step, score, 0)
    seat_rows(z, index_ref, lambda j: (local_ref, j * z.nrows, z.columns))
    for s in range(z.dp):
        at = pl.multiple_of((d ^ s) * z.part, z.part)
        total = logit_ref[pl.ds(at, z.part), :]
        for h in range(1, z.pack):
            more = logit_ref[pl.ds(pl.multiple_of(h * z.packed + at, z.part), z.part), :]
            total = total + pltpu.roll(more, h * z.items, 1)
        part_refs[s][...] = total


def weight_kernel(z, *refs):
    parts = refs[: z.dp]
    index_ref, hot_ref, passage_ref = refs[z.dp : z.dp + 3]
    dense_ref, loss_ref = refs[z.dp + 3 : z.dp + 5]
    grad_refs = refs[z.dp + 5 : 2 * z.dp + 5]
    logit_ref, seat_ref, tile_ref = refs[2 * z.dp + 5 :]
    d, t, c = (lax.axis_index(a) for a in ("dp", "tensor", "corpus"))
    for s in range(z.dp):
        at = pl.multiple_of((d ^ s) * z.part, z.part)
        logit_ref[pl.ds(at, z.part), :] = parts[s][...] * z.scale

    def softmax(logits, first_row):
        shape = logits.shape
        lane = lax.broadcasted_iota(jnp.int32, shape, 1)
        row = lax.broadcasted_iota(jnp.int32, shape, 0) + first_row
        weights = jnp.zeros(shape, jnp.float32)
        losses = []
        for h in range(z.pack):
            mask = (lane >= h * z.items) & (lane < (h + 1) * z.items)
            top = jnp.max(jnp.where(mask, logits, -jnp.inf), axis=1, keepdims=True)
            exponent = jnp.where(mask, jnp.exp(logits - top), 0.0)
            denominator = jnp.sum(exponent, axis=1, keepdims=True)
            query = row + h * z.packed
            own = (query // z.half) * z.own + (query & (z.own - 1)) + h * z.items
            target = jnp.where(lane == own, 1.0, 0.0)
            weights = jnp.where(mask, exponent / denominator - target, weights)
            chosen = jnp.sum(target * jnp.where(mask, logits, 0.0), axis=1, keepdims=True)
            losses.append(jnp.log(denominator) + top - chosen)
        return weights, losses

    mine = ((d * z.tensor + t) * z.corpus + c) * z.own
    first = pl.multiple_of(mine % z.packed, z.own)
    _, losses = softmax(logit_ref[pl.ds(first, z.own), :], first)
    loss = losses[0]
    for h in range(1, z.pack):
        loss = jnp.where(mine // z.packed == h, losses[h], loss)
    loss_ref[...] = jnp.broadcast_to(loss, (z.own, LANES))

    step = min(z.packed, 256)

    def weigh(i, carry):
        at = pl.ds(pl.multiple_of(i * step, step), step)
        weights, _ = softmax(logit_ref[at, :], i * step)
        logit_ref[at, :] = weights.astype(jnp.bfloat16).astype(jnp.float32)
        return carry

    lax.fori_loop(0, z.packed // step, weigh, 0)

    def seat(j):
        h, row = divmod(j * z.nrows, z.packed)
        return logit_ref, row, h * z.items + z.columns

    seat_rows(z, seat_ref, seat)
    high = z.seats * z.chunks
    tall = lax.broadcasted_iota(jnp.int32, (high, z.deep), 0)
    shift = lax.broadcasted_iota(jnp.int32, (1, z.deep), 1) // z.negs * z.chunks
    spread = lax.broadcasted_iota(jnp.int32, (LANES, z.deep), 0).astype(jnp.bfloat16)
    turns = 16

    def place(i, carry):
        for k in range(turns):
            r = i * turns + k
            local = index_ref[pl.ds(r, 1), :]
            chunk = (local >> 7) + shift
            within = (local & (LANES - 1)).astype(jnp.bfloat16)
            left = jnp.where(
                jnp.broadcast_to(chunk, (high, z.deep)) == tall,
                jnp.broadcast_to(seat_ref[pl.ds(r, 1), :], (high, z.deep)), 0.0,
            ).astype(jnp.bfloat16)
            right = jnp.where(
                jnp.broadcast_to(within, (LANES, z.deep)) == spread,
                jnp.bfloat16(1), jnp.bfloat16(0),
            )
            tiles = lax.dot_general(
                left, right, (((1,), (1,)), ((), ())), preferred_element_type=jnp.float32
            )
            for j in range(z.seats):
                at = pl.multiple_of((j * z.nrows + r) * z.chunks, z.chunks)
                tile_ref[pl.ds(at, z.chunks), :] = tiles[j * z.chunks : (j + 1) * z.chunks, :]
        return carry

    lax.fori_loop(0, z.nrows // turns, place, 0)
    lane = lax.broadcasted_iota(jnp.int32, (z.run, LANES), 1)
    group = lax.broadcasted_iota(jnp.int32, (z.run, LANES), 0) // z.own
    for n in range(z.sets):
        spans = [pl.ds(h * z.half + n * z.run, z.run) for h in range(z.dp)]
        hot = jnp.concatenate([hot_ref[span, :] for span in spans], axis=0)
        for h in range(z.dp):
            first_row = h * z.half + n * z.run
            side, row = divmod(first_row, z.packed)
            left = []
            for chunk in range(z.deep // LANES):
                if z.joint == 1:
                    part = logit_ref[pl.ds(row, z.run), chunk * LANES : (chunk + 1) * LANES]
                else:
                    at = chunk * LANES + lane
                    from_lane = side * z.items + at // z.run * z.own + at % z.own
                    part = jnp.take_along_axis(
                        logit_ref[pl.ds(row, z.run), :LANES], from_lane, axis=1
                    )
                    part = jnp.where(at // z.own % z.joint == group, part, 0.0)
                left.append(part.astype(jnp.bfloat16))
            shared = jnp.dot(
                jnp.concatenate(left, axis=1), hot, preferred_element_type=jnp.float32
            )
            for j in range(z.chunks):
                alone = tile_ref[pl.ds(first_row * z.chunks + j, z.run, stride=z.chunks), :]
                dense_ref[spans[h], j * LANES : (j + 1) * LANES] = (
                    alone + shared[:, j * LANES : (j + 1) * LANES]
                ).astype(jnp.bfloat16)
    for s in range(z.dp):
        at = pl.multiple_of((d ^ s) * z.half, z.half)
        grad_refs[s][...] = jnp.dot(
            dense_ref[pl.ds(at, z.half), :], passage_ref[...], preferred_element_type=jnp.float32
        )


def hot_kernel(z, pos_ref, hot_ref):
    lane = lax.broadcasted_iota(jnp.int32, (z.half, LANES), 1)
    for h in range(z.dp):
        at = pl.ds(h * z.half, z.half)
        for j in range(z.chunks):
            same = pos_ref[at, :] == lane + j * LANES
            hot_ref[at, j * LANES : (j + 1) * LANES] = jnp.where(same, 1.0, 0.0).astype(jnp.bfloat16)


def passage_kernel(z, dense_ref, query_ref, out_ref):
    def one(i, carry):
        at = pl.ds(pl.multiple_of(i * 256, 256), 256)
        out_ref[at, :] = z.scale * lax.dot_general(
            dense_ref[:, at], query_ref[...], (((0,), (0,)), ((), ())),
            preferred_element_type=jnp.float32,
        )
        return carry

    lax.fori_loop(0, z.block // 256, one, 0)


def query_kernel(z, arrived_ref, out_ref):
    for t in range(z.tensor):
        total = arrived_ref[t * z.corpus]
        for c in range(1, z.corpus):
            total = total + arrived_ref[t * z.corpus + c]
        out_ref[:, t * z.width : (t + 1) * z.width] = total * z.scale


def call(z, kernel, outs, scratch, args, flops, spaces=None, vmem=None):
    spaces = spaces or [pltpu.VMEM] * len(args)
    moved = sum(a.size * a.dtype.itemsize for a in args)
    moved += sum(o.size * jnp.dtype(o.dtype).itemsize for o in outs)
    return pl.pallas_call(
        lambda *refs: kernel(z, *refs),
        out_shape=outs,
        in_specs=[pl.BlockSpec(memory_space=space) for space in spaces],
        out_specs=[pl.BlockSpec(memory_space=pltpu.VMEM)] * len(outs),
        scratch_shapes=scratch,
        compiler_params=pltpu.CompilerParams(vmem_limit_bytes=vmem or z.vmem),
        cost_estimate=pl.CostEstimate(flops=flops, bytes_accessed=moved, transcendentals=0),
    )(*args)


def body(queries, passages, pos_ids, neg_ids):
    z = Sizes(queries, passages, neg_ids)
    f32, bf16 = jnp.float32, jnp.bfloat16
    shape = jax.ShapeDtypeStruct

    pieces = call(
        z, message_kernel, [shape((z.own, z.width + LANES), bf16)] * z.tensor,
        [
            pltpu.SMEM(pos_ids.shape, jnp.int32), pltpu.VMEM(neg_ids.shape, jnp.int32),
            pltpu.VMEM(queries.shape, bf16), pltpu.SemaphoreType.DMA((3,)),
        ],
        [pos_ids, neg_ids, queries], 0, [pltpu.HBM] * 3, 60 * 2**20,
    )
    passages, pieces = lax.optimization_barrier((passages, pieces))
    (passages,) = call(
        z, fetch_kernel, [shape(passages.shape, bf16)], [pltpu.SemaphoreType.DMA],
        [passages], 0, [pltpu.HBM],
    )
    plane = [None] * z.tensor
    for s in range(1, z.tensor):
        plane[s] = swap(pieces[s], "tensor", s)
    plane[0] = pieces[0]
    plane = jnp.concatenate(plane, axis=0)
    chip = [plane] * z.corpus
    for s in range(1, z.corpus):
        chip[s] = swap(plane, "corpus", s)
    arrived = gather_pieces([jnp.concatenate(chip, axis=0)], "dp")

    work = 2 * z.rows * z.block * z.width
    query_rows, index, pos_rows, *parts = call(
        z, score_kernel,
        [
            shape((z.rows, z.width), bf16), shape((z.nrows, z.deep), jnp.int32),
            shape((z.rows, LANES), jnp.int32),
        ]
        + [shape((z.part, z.lanes), f32)] * z.dp,
        [
            pltpu.VMEM((z.rows, LANES), f32),
            pltpu.VMEM((z.rows, z.lanes), jnp.int32),
            pltpu.VMEM((z.rows, z.lanes), f32),
        ],
        arrived + [passages], work,
    )
    (hot,) = call(z, hot_kernel, [shape((z.rows, z.block), bf16)], [], [pos_rows], z.rows * z.block)
    total = scatter_sum(parts, "dp")
    bit = 1
    while bit < z.tensor:
        total = total + swap(total, "tensor", bit)
        bit *= 2
    total = sum([swap(total, "corpus", s) for s in turn_order(z.corpus)], total)
    logits = gather_pieces([total], "dp")

    dense, loss, *grads = call(
        z, weight_kernel,
        [shape((z.rows, z.block), bf16), shape((z.own, LANES), f32)]
        + [shape((z.half, z.width), f32)] * z.dp,
        [
            pltpu.VMEM((z.packed, z.lanes), f32),
            pltpu.VMEM((z.nrows, z.deep), f32),
            pltpu.VMEM((z.rows * z.chunks, LANES), f32),
        ],
        logits + [index, hot, passages], 2 * work,
    )
    (grad_pass,) = call(
        z, passage_kernel, [shape((z.block, z.width), f32)], [], [dense, query_rows], work
    )
    half = scatter_sum(grads, "dp")
    half = half.reshape(z.groups, z.own, z.width)
    half = lax.all_to_all(half, ("tensor", "corpus"), split_axis=0, concat_axis=0, tiled=True)
    (grad_query,) = call(
        z, query_kernel, [shape((z.own, z.feat), f32)], [], [half], half.size
    )
    return (grad_query, loss[:, 0], grad_pass)


def solution(mesh):
    spread = ("dp", "tensor", "corpus")
    in_specs = (P(spread, None), P(("dp", "corpus"), "tensor"), P(spread), P(spread, None))
    out_specs = (P(spread, None), P(spread), P(("dp", "corpus"), "tensor"))
    return jax.shard_map(body, mesh=mesh, in_specs=in_specs, out_specs=out_specs, check_vma=False)
```

```python
import jax
import jax.numpy as jnp
from jax import lax
from jax.experimental import pallas as pl
from jax.experimental.pallas import tpu as pltpu
from jax.sharding import PartitionSpec as P

LANES = 128


def pairs(size, bit):
    return [(i, i ^ bit) for i in range(size)]


def swap(value, axis, bit):
    return lax.ppermute(value, axis, pairs(lax.axis_size(axis), bit))


def gather_pieces(pieces, axis):
    bit = 1
    while bit < lax.axis_size(axis):
        pieces = pieces + [swap(piece, axis, bit) for piece in pieces]
        bit *= 2
    return pieces


def scatter_sum(pieces, axis):
    bit = lax.axis_size(axis) // 2
    while bit:
        pieces = [
            mine + swap(theirs, axis, bit) for mine, theirs in zip(pieces[:bit], pieces[bit:])
        ]
        bit //= 2
    return pieces[0]


def turn_order(size):
    return [1] + list(range(size - 1, 1, -1))


PLANE, ZED = [0, 1, 2, 3], [0, 3, 2, 1]


class Sizes:
    def __init__(self, queries, passages, neg_ids):
        self.own, self.feat = queries.shape
        self.block, self.width = passages.shape
        self.negs = neg_ids.shape[1]
        self.dp = lax.axis_size("dp")
        self.tensor = lax.axis_size("tensor")
        self.corpus = lax.axis_size("corpus")
        self.groups = self.tensor * self.corpus
        self.half = self.groups * self.own
        self.rows = self.dp * self.half
        self.columns = self.dp * self.own
        self.items = self.columns + self.negs
        self.lanes = -(-self.items // LANES) * LANES
        self.pack = max(1, LANES // self.items)
        self.packed = self.rows // self.pack
        self.part = self.packed // self.dp
        self.neg_at = self.columns % LANES
        self.pos_at = 0 if self.neg_at else self.negs
        self.chunks = self.block // LANES
        self.scale = self.feat ** (-0.5)
        self.tensor_order = PLANE if self.tensor == 4 else list(range(self.tensor))
        self.corpus_order = ZED if self.corpus == 4 else list(range(self.corpus))
        self.deep = 2 * LANES
        self.seats = self.deep // self.negs
        self.nrows = self.rows // self.seats
        self.joint = max(1, self.deep // self.columns)
        self.run = self.joint * self.own
        self.sets = self.groups // self.joint
        self.vmem = min(60, 20 + 10 * self.rows // 1024) * 2**20


def message_kernel(z, pos_in, neg_in, query_in, *refs):
    piece_refs = refs[: z.tensor]
    pos_ref, neg_ref, query_ref, sems = refs[z.tensor :]
    t = lax.axis_index("tensor")
    moves = [
        pltpu.make_async_copy(source, target, sems.at[i])
        for i, (source, target) in enumerate(
            [(pos_in, pos_ref), (neg_in, neg_ref), (query_in, query_ref)]
        )
    ]
    for move in moves:
        move.start()
    for move in moves:
        move.wait()
    half = LANES // 2
    row = lax.broadcasted_iota(jnp.int32, (z.own, half), 0)
    pos = jnp.zeros((z.own, half), jnp.int32)
    for i in range(z.own):
        pos = jnp.where(row == i, pos_ref[i], pos)
    ids = [neg_ref[...], pos[:, : half - z.neg_at - z.negs]]
    ids = jnp.concatenate([part for part in [pos[:, : z.neg_at]] + ids if part.shape[1]], axis=1)
    ids = jnp.concatenate([ids >> 8, ids & 255], axis=1)
    code = ids.astype(jnp.float32).astype(jnp.bfloat16)
    for s in range(z.tensor):
        at = pl.ds(pl.multiple_of((t ^ s) * z.width, LANES), z.width)
        piece_refs[s][:, : z.width] = query_ref[:, at]
        piece_refs[s][:, z.width :] = code


def fetch_kernel(z, block_ref, passage_ref, sem):
    fetch = pltpu.make_async_copy(block_ref, passage_ref, sem)
    fetch.start()
    fetch.wait()


def seat_rows(z, out_ref, source):
    lane = lax.broadcasted_iota(jnp.int32, (z.nrows, LANES), 1)
    per = LANES // z.negs
    for chunk in range(z.deep // LANES):
        packed = None
        for k in range(per):
            ref, row, at = source(chunk * per + k)
            base = at // LANES * LANES
            piece = ref[pl.ds(row, z.nrows), base : base + LANES]
            turn = (k * z.negs - at) % LANES
            piece = pltpu.roll(piece, turn, 1) if turn else piece
            packed = piece if packed is None else jnp.where(lane < k * z.negs, packed, piece)
        out_ref[:, chunk * LANES : (chunk + 1) * LANES] = packed


def score_kernel(z, *refs):
    cuts = z.corpus if z.dp == 2 else 1
    arrived, refs = refs[: cuts * z.dp], refs[cuts * z.dp :]
    passage_ref, query_ref, index_ref, pos_ref = refs[:4]
    part_refs = refs[4 : z.dp + 4]
    id_ref, local_ref, logit_ref = refs[z.dp + 4 :]
    d, t, c = (lax.axis_index(a) for a in ("dp", "tensor", "corpus"))
    for sd in range(z.dp):
        for sc in range(z.corpus):
            for st in range(z.tensor):
                piece_ref = arrived[sd * cuts + sc % cuts]
                source = pl.ds((sc // cuts * z.tensor + st) * z.own, z.own)
                place = (d ^ sd) * z.tensor + (t ^ z.tensor_order[st])
                place = (place * z.corpus + (c ^ z.corpus_order[sc])) * z.own
                place = pl.ds(pl.multiple_of(place, z.own), z.own)
                query_ref[place, :] = piece_ref[source, : z.width]
                code = piece_ref[source, z.width :].astype(jnp.float32)
                id_ref[place, :] = code * 256.0 + pltpu.roll(code, LANES // 2, 1)
    first = ((d * z.corpus + c) * z.block).astype(jnp.float32)
    wide = -(-z.columns // LANES) * LANES
    row = lax.broadcasted_iota(jnp.int32, (z.half, wide), 0) & (z.own - 1)
    col = lax.broadcasted_iota(jnp.int32, (z.half, wide), 1)
    group_ids = jnp.zeros((z.groups, wide), jnp.float32)
    for h in range(z.dp):
        ids = id_ref[pl.ds(h * z.half, z.half), :]
        pos = jnp.broadcast_to(ids[:, z.pos_at : z.pos_at + 1], (z.half, wide))
        pos_ref[pl.ds(h * z.half, z.half), :] = (pos[:, :LANES] - first).astype(jnp.int32)
        kept = jnp.where(col == row + h * z.own, pos, 0.0)
        group_ids += jnp.sum(kept.reshape(z.groups, z.own, wide), axis=1)
    batch_ids = jnp.broadcast_to(group_ids[:, None, :], (z.groups, z.own, wide))
    batch_ids = batch_ids.reshape(z.half, wide)
    lane = lax.broadcasted_iota(jnp.int32, (z.half, LANES), 1)
    for h in range(z.dp):
        ids = id_ref[pl.ds(h * z.half, z.half), :]
        for base in range(0, z.lanes, LANES):
            named = ids
            if base < z.columns:
                named = jnp.where(lane + base < z.columns, batch_ids[:, base : base + LANES], ids)
            local = named - first
            inside = (local >= 0.0) & (local < float(z.block)) & (lane + base < z.items)
            local_ref[pl.ds(h * z.half, z.half), base : base + LANES] = jnp.where(
                inside, local, -float(2**20)
            ).astype(jnp.int32)
    step = min(z.rows, 256)

    def score(i, carry):
        at = pl.ds(pl.multiple_of(i * step, step), step)
        scores = lax.dot_general(
            query_ref[at, :], passage_ref[...], (((1,), (1,)), ((), ())),
            preferred_element_type=jnp.float32,
        )
        for base in range(0, z.lanes, LANES):
            local = local_ref[at, base : base + LANES]
            chunk, within = local >> 7, local & (LANES - 1)
            picked = jnp.zeros((step, LANES), jnp.float32)
            for j in range(z.chunks):
                found = jnp.take_along_axis(scores[:, j * LANES : (j + 1) * LANES], within, axis=1)
                picked = jnp.where(chunk == j, found, picked)
            logit_ref[at, base : base + LANES] = picked
        return carry

    lax.fori_loop(0, z.rows // step, score, 0)
    seat_rows(z, index_ref, lambda j: (local_ref, j * z.nrows, z.columns))
    for s in range(z.dp):
        at = pl.multiple_of((d ^ s) * z.part, z.part)
        total = logit_ref[pl.ds(at, z.part), :]
        for h in range(1, z.pack):
            more = logit_ref[pl.ds(pl.multiple_of(h * z.packed + at, z.part), z.part), :]
            total = total + pltpu.roll(more, h * z.items, 1)
        part_refs[s][...] = total


def weight_kernel(z, *refs):
    parts = refs[: z.dp]
    index_ref, hot_ref, passage_ref = refs[z.dp : z.dp + 3]
    dense_ref, loss_ref, size_ref = refs[z.dp + 3 : z.dp + 6]
    sizes_ref = refs[z.dp + 6]
    grad_refs = refs[z.dp + 7 : 2 * z.dp + 6]
    logit_ref, seat_ref, tile_ref = refs[2 * z.dp + 6 :]
    d, t, c = (lax.axis_index(a) for a in ("dp", "tensor", "corpus"))
    for s in range(z.dp):
        at = pl.multiple_of((d ^ s) * z.part, z.part)
        logit_ref[pl.ds(at, z.part), :] = parts[s][...] * z.scale

    def softmax(logits, first_row):
        shape = logits.shape
        lane = lax.broadcasted_iota(jnp.int32, shape, 1)
        row = lax.broadcasted_iota(jnp.int32, shape, 0) + first_row
        weights = jnp.zeros(shape, jnp.float32)
        losses, sizes = [], []
        for h in range(z.pack):
            mask = (lane >= h * z.items) & (lane < (h + 1) * z.items)
            top = jnp.max(jnp.where(mask, logits, -jnp.inf), axis=1, keepdims=True)
            exponent = jnp.where(mask, jnp.exp(logits - top), 0.0)
            denominator = jnp.sum(exponent, axis=1, keepdims=True)
            query = row + h * z.packed
            own = (query // z.half) * z.own + (query & (z.own - 1)) + h * z.items
            target = jnp.where(lane == own, 1.0, 0.0)
            weights = jnp.where(mask, exponent / denominator - target, weights)
            size = jnp.max(jnp.where(mask, jnp.abs(weights), 0.0), axis=1, keepdims=True)
            sizes.append(jnp.maximum(size, 1e-30))
            chosen = jnp.sum(target * jnp.where(mask, logits, 0.0), axis=1, keepdims=True)
            losses.append(jnp.log(denominator) + top - chosen)
        return weights, losses, sizes

    mine = ((d * z.tensor + t) * z.corpus + c) * z.own
    first = pl.multiple_of(mine % z.packed, z.own)
    _, losses, _ = softmax(logit_ref[pl.ds(first, z.own), :], first)
    loss = losses[0]
    for h in range(1, z.pack):
        loss = jnp.where(mine // z.packed == h, losses[h], loss)
    loss_ref[...] = jnp.broadcast_to(loss, (z.own, LANES))

    step = min(z.packed, 256)

    def weigh(i, carry):
        at = pl.ds(pl.multiple_of(i * step, step), step)
        weights, _, sizes = softmax(logit_ref[at, :], i * step)
        logit_ref[at, :] = weights.astype(jnp.bfloat16).astype(jnp.float32)
        for h in range(z.pack):
            place = pl.ds(pl.multiple_of(h * z.packed + i * step, step), step)
            sizes_ref[place, :] = jnp.broadcast_to(sizes[h], (step, LANES))
        return carry

    lax.fori_loop(0, z.packed // step, weigh, 0)
    size_ref[...] = sizes_ref[pl.ds(pl.multiple_of(mine, z.own), z.own), :]

    def seat(j):
        h, row = divmod(j * z.nrows, z.packed)
        return logit_ref, row, h * z.items + z.columns

    seat_rows(z, seat_ref, seat)
    high = z.seats * z.chunks
    tall = lax.broadcasted_iota(jnp.int32, (high, z.deep), 0)
    shift = lax.broadcasted_iota(jnp.int32, (1, z.deep), 1) // z.negs * z.chunks
    spread = lax.broadcasted_iota(jnp.int32, (LANES, z.deep), 0).astype(jnp.bfloat16)
    turns = 16

    def place(i, carry):
        for k in range(turns):
            r = i * turns + k
            local = index_ref[pl.ds(r, 1), :]
            chunk = (local >> 7) + shift
            within = (local & (LANES - 1)).astype(jnp.bfloat16)
            left = jnp.where(
                jnp.broadcast_to(chunk, (high, z.deep)) == tall,
                jnp.broadcast_to(seat_ref[pl.ds(r, 1), :], (high, z.deep)), 0.0,
            ).astype(jnp.bfloat16)
            right = jnp.where(
                jnp.broadcast_to(within, (LANES, z.deep)) == spread,
                jnp.bfloat16(1), jnp.bfloat16(0),
            )
            tiles = lax.dot_general(
                left, right, (((1,), (1,)), ((), ())), preferred_element_type=jnp.float32
            )
            for j in range(z.seats):
                at = pl.multiple_of((j * z.nrows + r) * z.chunks, z.chunks)
                tile_ref[pl.ds(at, z.chunks), :] = tiles[j * z.chunks : (j + 1) * z.chunks, :]
        return carry

    lax.fori_loop(0, z.nrows // turns, place, 0)
    lane = lax.broadcasted_iota(jnp.int32, (z.run, LANES), 1)
    group = lax.broadcasted_iota(jnp.int32, (z.run, LANES), 0) // z.own
    for n in range(z.sets):
        spans = [pl.ds(h * z.half + n * z.run, z.run) for h in range(z.dp)]
        hot = jnp.concatenate([hot_ref[span, :] for span in spans], axis=0)
        for h in range(z.dp):
            first_row = h * z.half + n * z.run
            side, row = divmod(first_row, z.packed)
            left = []
            for chunk in range(z.deep // LANES):
                if z.joint == 1:
                    part = logit_ref[pl.ds(row, z.run), chunk * LANES : (chunk + 1) * LANES]
                else:
                    at = chunk * LANES + lane
                    from_lane = side * z.items + at // z.run * z.own + at % z.own
                    part = jnp.take_along_axis(
                        logit_ref[pl.ds(row, z.run), :LANES], from_lane, axis=1
                    )
                    part = jnp.where(at // z.own % z.joint == group, part, 0.0)
                left.append(part.astype(jnp.bfloat16))
            shared = jnp.dot(
                jnp.concatenate(left, axis=1), hot, preferred_element_type=jnp.float32
            )
            for j in range(z.chunks):
                alone = tile_ref[pl.ds(first_row * z.chunks + j, z.run, stride=z.chunks), :]
                dense_ref[spans[h], j * LANES : (j + 1) * LANES] = (
                    alone + shared[:, j * LANES : (j + 1) * LANES]
                ).astype(jnp.bfloat16)
    for s in range(1, z.dp):
        query_grads(z, s, dense_ref, sizes_ref, passage_ref, grad_refs[s - 1])


def query_grads(z, s, dense_ref, sizes_ref, passage_ref, grad_ref):
    at = pl.ds(pl.multiple_of((lax.axis_index("dp") ^ s) * z.half, z.half), z.half)
    grads = jnp.dot(dense_ref[at, :], passage_ref[...], preferred_element_type=jnp.float32)
    grad_ref[...] = grads / sizes_ref[at, :1]


def own_kernel(z, dense_ref, sizes_ref, passage_ref, grad_ref):
    query_grads(z, 0, dense_ref, sizes_ref, passage_ref, grad_ref)


def hot_kernel(z, pos_ref, hot_ref):
    lane = lax.broadcasted_iota(jnp.int32, (z.half, LANES), 1)
    for h in range(z.dp):
        at = pl.ds(h * z.half, z.half)
        for j in range(z.chunks):
            same = pos_ref[at, :] == lane + j * LANES
            hot_ref[at, j * LANES : (j + 1) * LANES] = jnp.where(same, 1.0, 0.0).astype(jnp.bfloat16)


def passage_kernel(z, dense_ref, query_ref, out_ref):
    def one(i, carry):
        at = pl.ds(pl.multiple_of(i * 256, 256), 256)
        out_ref[at, :] = z.scale * lax.dot_general(
            dense_ref[:, at], query_ref[...], (((0,), (0,)), ((), ())),
            preferred_element_type=jnp.float32,
        )
        return carry

    lax.fori_loop(0, z.block // 256, one, 0)


def call(z, kernel, outs, scratch, args, flops, spaces=None, vmem=None):
    spaces = spaces or [pltpu.VMEM] * len(args)
    moved = sum(a.size * a.dtype.itemsize for a in args)
    moved += sum(o.size * jnp.dtype(o.dtype).itemsize for o in outs)
    return pl.pallas_call(
        lambda *refs: kernel(z, *refs),
        out_shape=outs,
        in_specs=[pl.BlockSpec(memory_space=space) for space in spaces],
        out_specs=[pl.BlockSpec(memory_space=pltpu.VMEM)] * len(outs),
        scratch_shapes=scratch,
        compiler_params=pltpu.CompilerParams(vmem_limit_bytes=vmem or z.vmem),
        cost_estimate=pl.CostEstimate(flops=flops, bytes_accessed=moved, transcendentals=0),
    )(*args)


def body(queries, passages, pos_ids, neg_ids):
    z = Sizes(queries, passages, neg_ids)
    f32, bf16 = jnp.float32, jnp.bfloat16
    shape = jax.ShapeDtypeStruct

    pieces = call(
        z, message_kernel, [shape((z.own, z.width + LANES), bf16)] * z.tensor,
        [
            pltpu.SMEM(pos_ids.shape, jnp.int32), pltpu.VMEM(neg_ids.shape, jnp.int32),
            pltpu.VMEM(queries.shape, bf16), pltpu.SemaphoreType.DMA((3,)),
        ],
        [pos_ids, neg_ids, queries], 0, [pltpu.HBM] * 3, 60 * 2**20,
    )
    passages, pieces = lax.optimization_barrier((passages, pieces))
    (passages,) = call(
        z, fetch_kernel, [shape(passages.shape, bf16)], [pltpu.SemaphoreType.DMA],
        [passages], 0, [pltpu.HBM],
    )
    plane = [swap(pieces[s], "tensor", s) if s else pieces[s] for s in z.tensor_order]
    plane = jnp.concatenate(plane, axis=0)
    plane, passages = lax.optimization_barrier((plane, passages))
    chip = [swap(plane, "corpus", s) if s else plane for s in z.corpus_order]
    if z.dp > 2:
        chip = [jnp.concatenate(chip, axis=0)]
    arrived = gather_pieces(chip, "dp")

    work = 2 * z.rows * z.block * z.width
    query_rows, index, pos_rows, *parts = call(
        z, score_kernel,
        [
            shape((z.rows, z.width), bf16), shape((z.nrows, z.deep), jnp.int32),
            shape((z.rows, LANES), jnp.int32),
        ]
        + [shape((z.part, z.lanes), f32)] * z.dp,
        [
            pltpu.VMEM((z.rows, LANES), f32),
            pltpu.VMEM((z.rows, z.lanes), jnp.int32),
            pltpu.VMEM((z.rows, z.lanes), f32),
        ],
        arrived + [passages], work,
    )
    (hot,) = call(z, hot_kernel, [shape((z.rows, z.block), bf16)], [], [pos_rows], z.rows * z.block)
    total = scatter_sum(parts, "dp")
    total = sum([swap(total, "tensor", s) for s in range(1, z.tensor)], total)
    total = sum([swap(total, "corpus", s) for s in turn_order(z.corpus)], total)
    logits = gather_pieces([total], "dp")

    dense, loss, size, sizes, *grads = call(
        z, weight_kernel,
        [shape((z.rows, z.block), bf16)] + [shape((z.own, LANES), f32)] * 2
        + [shape((z.rows, LANES), f32)] + [shape((z.half, z.width), f32)] * (z.dp - 1),
        [
            pltpu.VMEM((z.packed, z.lanes), f32),
            pltpu.VMEM((z.nrows, z.deep), f32),
            pltpu.VMEM((z.rows * z.chunks, LANES), f32),
        ],
        logits + [index, hot, passages], 2 * work,
    )
    (grad_pass,) = call(
        z, passage_kernel, [shape((z.block, z.width), f32)], [], [dense, query_rows], work
    )
    (own_grad,) = call(
        z, own_kernel, [shape((z.half, z.width), f32)], [], [dense, sizes, passages], work // 2
    )
    half = scatter_sum([own_grad] + grads, "dp")
    half = half.astype(jnp.float16).reshape(z.groups, z.own, z.width)
    half = lax.all_to_all(half, ("tensor", "corpus"), split_axis=0, concat_axis=0, tiled=True)
    half = half.astype(f32).reshape(z.tensor, z.corpus, z.own, z.width).sum(axis=1)
    grad_query = half.swapaxes(0, 1).reshape(z.own, z.feat) * (size[:, :1] * z.scale)
    return (grad_query, loss[:, 0], grad_pass)


def solution(mesh):
    spread = ("dp", "tensor", "corpus")
    in_specs = (P(spread, None), P(("dp", "corpus"), "tensor"), P(spread), P(spread, None))
    out_specs = (P(spread, None), P(spread), P(("dp", "corpus"), "tensor"))
    return jax.shard_map(body, mesh=mesh, in_specs=in_specs, out_specs=out_specs, check_vma=False)
```

```python
import jax
import jax.numpy as jnp
from jax import lax
from jax.experimental import pallas as pl
from jax.experimental.pallas import tpu as pltpu
from jax.sharding import PartitionSpec as P

LANES = 128
FAR = -(2**20)
LOW = -1e30
PLANE, ZED = [0, 1, 2, 3], [0, 3, 2, 1]


def swap(value, axis, bit):
    size = lax.axis_size(axis)
    return lax.ppermute(value, axis, [(i, i ^ bit) for i in range(size)])


def gather_pairs(pieces):
    bit = 2
    while bit < lax.axis_size("dp"):
        pieces = pieces + [swap(piece, "dp", bit) for piece in pieces]
        bit *= 2
    return pieces


def scatter_pairs(pieces):
    while len(pieces) > 1:
        n = len(pieces) // 2
        pieces = [
            mine + swap(theirs, "dp", 2 * n) for mine, theirs in zip(pieces[:n], pieces[n:])
        ]
    return pieces[0]


class Sizes:
    def __init__(self, queries, passages, neg_ids):
        self.own, self.feat = queries.shape
        self.block, self.width = passages.shape
        self.negs = neg_ids.shape[1]
        self.dp = lax.axis_size("dp")
        self.tensor = lax.axis_size("tensor")
        self.corpus = lax.axis_size("corpus")
        self.side = self.dp // 2
        self.groups = self.tensor * self.corpus
        self.half = self.groups * self.own
        self.rows = self.side * self.half
        self.named = self.dp * self.half
        self.columns = self.dp * self.own
        self.items = self.columns + self.negs
        self.lanes = -(-self.items // LANES) * LANES
        self.pack = max(1, LANES // self.items)
        self.packed = self.rows // self.pack
        self.neg_at = self.columns % LANES
        self.pos_at = 0 if self.neg_at else self.negs
        self.wide = 2 * self.block
        self.chunks = self.wide // LANES
        self.scale = self.feat ** (-0.5)
        self.tensor_order = PLANE if self.tensor == 4 else list(range(self.tensor))
        self.corpus_order = ZED if self.corpus == 4 else list(range(self.corpus))
        self.cuts = self.corpus if self.side == 1 else 1
        self.deep = 2 * LANES
        self.seats = self.deep // self.negs
        self.nrows = self.rows // self.seats
        self.joint = max(1, self.deep // self.columns)
        self.run = self.joint * self.own
        self.sets = self.groups // self.joint
        self.high = -(-3 * self.pack // 8) * 8
        self.vmem = min(61, 20 + 20 * self.rows // 1024) * 2**20


def places():
    return [lax.axis_index(axis) for axis in ("dp", "tensor", "corpus")]


def rows_at(start, size):
    return pl.ds(pl.multiple_of(start, size), size)


def message_kernel(z, pos_in, neg_in, query_in, *refs):
    piece_refs = refs[: z.tensor]
    pos_ref, neg_ref, query_ref, sems = refs[z.tensor :]
    t = lax.axis_index("tensor")
    moves = [
        pltpu.make_async_copy(source, target, sems.at[i])
        for i, (source, target) in enumerate(
            [(pos_in, pos_ref), (neg_in, neg_ref), (query_in, query_ref)]
        )
    ]
    for move in moves:
        move.start()
    for move in moves:
        move.wait()
    half = LANES // 2
    row = lax.broadcasted_iota(jnp.int32, (z.own, half), 0)
    pos = jnp.zeros((z.own, half), jnp.int32)
    for i in range(z.own):
        pos = jnp.where(row == i, pos_ref[i], pos)
    ids = [neg_ref[...], pos[:, : half - z.neg_at - z.negs]]
    ids = jnp.concatenate([part for part in [pos[:, : z.neg_at]] + ids if part.shape[1]], axis=1)
    ids = jnp.concatenate([ids >> 8, ids & 255], axis=1)
    code = ids.astype(jnp.float32).astype(jnp.bfloat16)
    for s in range(z.tensor):
        at = pl.ds(pl.multiple_of((t ^ s) * z.width, LANES), z.width)
        piece_refs[s][:, : z.width] = query_ref[:, at]
        piece_refs[s][:, z.width :] = code


def fetch_kernel(z, block_ref, passage_ref, sem):
    fetch = pltpu.make_async_copy(block_ref, passage_ref, sem)
    fetch.start()
    fetch.wait()


def seat_rows(z, out_ref, source):
    lane = lax.broadcasted_iota(jnp.int32, (z.nrows, LANES), 1)
    per = LANES // z.negs
    for chunk in range(z.deep // LANES):
        packed = None
        for k in range(per):
            ref, row, at = source(chunk * per + k)
            base = at // LANES * LANES
            piece = ref[pl.ds(row, z.nrows), base : base + LANES]
            turn = (k * z.negs - at) % LANES
            piece = pltpu.roll(piece, turn, 1) if turn else piece
            packed = piece if packed is None else jnp.where(lane < k * z.negs, packed, piece)
        out_ref[:, chunk * LANES : (chunk + 1) * LANES] = packed


def score_kernel(z, *refs):
    count = z.side * z.cuts
    arrived, others, refs = refs[:count], refs[count : 2 * count], refs[2 * count :]
    block_refs, (query_ref, index_ref, pos_ref, inside_ref, part_ref) = refs[:2], refs[2:7]
    id_ref, local_ref, logit_ref = refs[7:]
    d, t, c = places()
    for su in range(z.side):
        for sc in range(z.corpus):
            for st in range(z.tensor):
                piece = su * z.cuts + sc % z.cuts
                source = pl.ds((sc // z.cuts * z.tensor + st) * z.own, z.own)
                from_d = d ^ (2 * su)
                place = (t ^ z.tensor_order[st]) * z.corpus + (c ^ z.corpus_order[sc])
                row = rows_at(((from_d >> 1) * z.groups + place) * z.own, z.own)
                query_ref[row, :] = arrived[piece][source, : z.width]
                codes = [arrived[piece][source, z.width :], others[piece][source, :]]
                for side, code in enumerate(codes):
                    code = code.astype(jnp.float32)
                    row = rows_at(((from_d ^ side) * z.groups + place) * z.own, z.own)
                    id_ref[row, :] = code * 256.0 + pltpu.roll(code, LANES // 2, 1)

    def localize(ids):
        found = jnp.full(ids.shape, float(FAR), jnp.float32)
        for side in range(2):
            local = ids - (((d ^ side) * z.corpus + c) * z.block).astype(jnp.float32)
            inside = (local >= 0.0) & (local < float(z.block))
            found = jnp.where(inside, local + float(side * z.block), found)
        return found

    wide = -(-z.columns // LANES) * LANES
    row = lax.broadcasted_iota(jnp.int32, (z.half, wide), 0) & (z.own - 1)
    col = lax.broadcasted_iota(jnp.int32, (z.half, wide), 1)
    group_ids = jnp.zeros((z.groups, wide), jnp.float32)
    for h in range(z.dp):
        at = pl.ds(h * z.half, z.half)
        pos = jnp.broadcast_to(id_ref[at, z.pos_at : z.pos_at + 1], (z.half, wide))
        pos_ref[at, :] = localize(pos[:, :LANES]).astype(jnp.int32)
        kept = jnp.where(col == row + h * z.own, pos, 0.0)
        group_ids += jnp.sum(kept.reshape(z.groups, z.own, wide), axis=1)
    batch_ids = jnp.broadcast_to(group_ids[:, None, :], (z.groups, z.own, wide))
    batch_ids = batch_ids.reshape(z.half, wide)
    lane = lax.broadcasted_iota(jnp.int32, (z.half, LANES), 1)
    for u in range(z.side):
        ids = id_ref[rows_at((2 * u + (d & 1)) * z.half, z.half), :]
        for base in range(0, z.lanes, LANES):
            named = ids
            if base < z.columns:
                named = jnp.where(lane + base < z.columns, batch_ids[:, base : base + LANES], ids)
            local = jnp.where(lane + base < z.items, localize(named), float(FAR))
            local_ref[pl.ds(u * z.half, z.half), base : base + LANES] = local.astype(jnp.int32)
    step = min(z.rows, 128)

    def score(i, carry):
        at = rows_at(i * step, step)
        scores = [
            lax.dot_general(
                query_ref[at, :], block_ref[...], (((1,), (1,)), ((), ())),
                preferred_element_type=jnp.float32,
            )
            for block_ref in block_refs
        ]
        each = z.block // LANES
        for base in range(0, z.lanes, LANES):
            local = local_ref[at, base : base + LANES]
            chunk, within = local >> 7, local & (LANES - 1)
            picked = jnp.zeros((step, LANES), jnp.float32)
            for j in range(z.chunks):
                k = j % each * LANES
                found = jnp.take_along_axis(scores[j // each][:, k : k + LANES], within, axis=1)
                picked = jnp.where(chunk == j, found, picked)
            logit_ref[at, base : base + LANES] = picked
        return carry

    lax.fori_loop(0, z.rows // step, score, 0)
    seat_rows(z, index_ref, lambda j: (local_ref, j * z.nrows, z.columns))
    for source_ref, target_ref in [(logit_ref, part_ref), (local_ref, inside_ref)]:
        lane = lax.broadcasted_iota(jnp.int32, (z.packed, z.lanes), 1)
        packed = source_ref[pl.ds(0, z.packed), :]
        for h in range(1, z.pack):
            other = pltpu.roll(source_ref[pl.ds(h * z.packed, z.packed), :], h * z.items, 1)
            packed = jnp.where(lane < h * z.items, packed, other)
        target_ref[...] = packed


def hot_kernel(z, pos_ref, hot_ref):
    lane = lax.broadcasted_iota(jnp.int32, (z.half, LANES), 1)
    for h in range(z.dp):
        at = pl.ds(h * z.half, z.half)
        for j in range(z.chunks):
            same = pos_ref[at, :] == lane + j * LANES
            hot_ref[at, j * LANES : (j + 1) * LANES] = jnp.where(same, 1.0, 0.0).astype(jnp.bfloat16)


def stat_kernel(z, total_ref, inside_ref, exponent_ref, stat_ref):
    step = min(z.packed, 256)
    side = lax.axis_index("dp") & 1

    def one(i, carry):
        at = rows_at(i * step, step)
        logits = total_ref[at, :] * z.scale
        lane = lax.broadcasted_iota(jnp.int32, logits.shape, 1)
        row = lax.broadcasted_iota(jnp.int32, logits.shape, 0) + i * step
        short = lax.broadcasted_iota(jnp.int32, (step, LANES), 1)
        named = inside_ref[at, :] >= 0
        exponents = jnp.zeros(logits.shape, jnp.float32)
        stats = jnp.zeros((step, LANES), jnp.float32)
        for h in range(z.pack):
            mask = named & (lane >= h * z.items) & (lane < (h + 1) * z.items)
            top = jnp.max(jnp.where(mask, logits, LOW), axis=1, keepdims=True)
            exponent = jnp.where(mask, jnp.exp(logits - top), 0.0)
            query = row + h * z.packed
            own = (2 * (query // z.half) + side) * z.own + (query & (z.own - 1)) + h * z.items
            chosen = jnp.where(mask & (lane == own), logits, 0.0)
            values = (
                top,
                jnp.sum(exponent, axis=1, keepdims=True),
                jnp.sum(chosen, axis=1, keepdims=True),
            )
            for k, value in enumerate(values):
                stats = jnp.where(short == 3 * h + k, value, stats)
            exponents = exponents + exponent
        exponent_ref[at, :] = exponents
        stat_ref[:, at] = stats.T[: z.high, :]
        return carry

    lax.fori_loop(0, z.packed // step, one, 0, unroll=z.packed == step)


def split(values):
    parts = []
    for _ in range(3):
        part = values.astype(jnp.bfloat16)
        parts.append(part)
        values = values - part.astype(jnp.float32)
    return parts


def join(tiles):
    n = tiles.shape[0] // 3
    return tiles[:n] + (tiles[n : 2 * n] + tiles[2 * n :])


def place_kernel(z, exponent_ref, index_ref, hot_ref, raw_ref, seat_ref, part_ref, tile_ref):
    def seat(j):
        h, row = divmod(j * z.nrows, z.packed)
        return exponent_ref, row, h * z.items + z.columns

    seat_rows(z, seat_ref, seat)
    for k, part in enumerate(split(seat_ref[...])):
        part_ref[k] = part.astype(jnp.float32)
    high = z.seats * z.chunks
    shape = (high, z.deep)
    tall = lax.broadcasted_iota(jnp.int32, shape, 0).astype(jnp.bfloat16)
    shift = lax.broadcasted_iota(jnp.int32, (1, z.deep), 1) // z.negs * z.chunks
    spread = lax.broadcasted_iota(jnp.int32, (LANES, z.deep), 0).astype(jnp.bfloat16)
    turns = min(16, z.nrows)
    none, unit = jnp.bfloat16(0), jnp.bfloat16(1)

    def place(i, carry):
        for k in range(turns):
            r = i * turns + k
            local = index_ref[pl.ds(r, 1), :]
            chunk = ((local >> 7) + shift).astype(jnp.bfloat16)
            within = (local & (LANES - 1)).astype(jnp.bfloat16)
            here = jnp.broadcast_to(chunk, shape) == tall
            left = [
                jnp.where(
                    here,
                    jnp.broadcast_to(part_ref[p, pl.ds(r, 1), :].astype(jnp.bfloat16), shape), none,
                )
                for p in range(3)
            ]
            right = jnp.where(jnp.broadcast_to(within, (LANES, z.deep)) == spread, unit, none)
            tiles = join(lax.dot_general(
                jnp.concatenate(left, axis=0), right, (((1,), (1,)), ((), ())),
                preferred_element_type=jnp.float32,
            ))
            for j in range(z.seats):
                at = rows_at((j * z.nrows + r) * z.chunks, z.chunks)
                tile_ref[at, :] = tiles[j * z.chunks : (j + 1) * z.chunks, :]
        return carry

    lax.fori_loop(0, z.nrows // turns, place, 0)
    lane = lax.broadcasted_iota(jnp.int32, (z.run, LANES), 1)
    group = lax.broadcasted_iota(jnp.int32, (z.run, LANES), 0) // z.own
    for n in range(z.sets):
        hot = [hot_ref[pl.ds(h * z.half + n * z.run, z.run), :] for h in range(z.dp)]
        hot = jnp.concatenate(hot, axis=0)
        for u in range(z.side):
            first_row = u * z.half + n * z.run
            side, row = divmod(first_row, z.packed)
            left = []
            for chunk in range(z.deep // LANES):
                if z.joint == 1:
                    part = exponent_ref[pl.ds(row, z.run), chunk * LANES : (chunk + 1) * LANES]
                else:
                    at = chunk * LANES + lane
                    from_lane = side * z.items + at // z.run * z.own + at % z.own
                    part = jnp.take_along_axis(
                        exponent_ref[pl.ds(row, z.run), :LANES], from_lane, axis=1
                    )
                    part = jnp.where(at // z.own % z.joint == group, part, 0.0)
                left.append(part)
            left = jnp.concatenate(split(jnp.concatenate(left, axis=1)), axis=0)
            shared = join(jnp.dot(left, hot, preferred_element_type=jnp.float32))
            for j in range(z.chunks):
                alone = tile_ref[pl.ds(first_row * z.chunks + j, z.run, stride=z.chunks), :]
                raw_ref[pl.ds(first_row, z.run), j * LANES : (j + 1) * LANES] = (
                    alone + shared[:, j * LANES : (j + 1) * LANES]
                )


def weight_kernel(z, *refs):
    count = z.side * z.cuts
    parts, refs = refs[:count], refs[count:]
    raw_ref, hot_ref, own_ref, other_ref = refs[:4]
    dense_refs, (loss_ref, size_ref) = refs[4:6], refs[6:8]
    grad_refs = refs[8 : 8 + z.side]
    stat_ref, row_ref, back_ref, sizes_ref = refs[8 + z.side :]
    d, t, c = places()
    for su in range(z.side):
        for sc in range(z.corpus):
            part = parts[su * z.cuts + sc % z.cuts][pl.ds(sc // z.cuts * z.high, z.high), :]
            stat_ref[((d >> 1) ^ su) * z.corpus + (c ^ z.corpus_order[sc])] = part
    planes = z.side * z.corpus
    row_ref[...] = jnp.zeros_like(row_ref)
    for h in range(z.pack):
        tops = [stat_ref[b, 3 * h : 3 * h + 1, :] for b in range(planes)]
        top = tops[0]
        for other in tops[1:]:
            top = jnp.maximum(top, other)
        total, chosen = jnp.zeros_like(top), jnp.zeros_like(top)
        for b in range(planes):
            total += stat_ref[b, 3 * h + 1 : 3 * h + 2, :] * jnp.exp(tops[b] - top)
            chosen += stat_ref[b, 3 * h + 2 : 3 * h + 3, :]
        mine = stat_ref[(d >> 1) * z.corpus + c, 3 * h : 3 * h + 1, :]
        rest = 1.0 - jnp.exp(chosen - top) / total
        row_ref[h : h + 1, :] = jnp.exp(mine - top) / total
        row_ref[z.pack + h : z.pack + h + 1, :] = jnp.maximum(rest, 2.0**-24)
        row_ref[2 * z.pack + h : 2 * z.pack + h + 1, :] = jnp.log(total) + top - chosen
    back_ref[...] = row_ref[...].T
    mine = (((d >> 1) * z.tensor + t) * z.corpus + c) * z.own
    place = rows_at(mine % z.packed, z.own)
    for k, target_ref in [(1, size_ref), (2, loss_ref)]:
        value = back_ref[place, k * z.pack : k * z.pack + 1]
        for h in range(1, z.pack):
            other = back_ref[place, k * z.pack + h : k * z.pack + h + 1]
            value = jnp.where(mine // z.packed == h, other, value)
        target_ref[...] = jnp.broadcast_to(value, (z.own, LANES))
    step = min(z.packed, 128)
    for h in range(z.pack):

        def one(i, carry):
            row = i * step
            query = h * z.packed + row
            at = rows_at(query, step)
            named = rows_at((2 * (query // z.half) + (d & 1)) * z.half + query % z.half, step)
            ratio = back_ref[rows_at(row, step), h : h + 1]
            weights = raw_ref[at, :] * ratio - hot_ref[named, :].astype(jnp.float32)
            weights = weights.astype(jnp.bfloat16)
            dense_refs[0][at, :] = weights[:, : z.block]
            dense_refs[1][at, :] = weights[:, z.block :]
            size = back_ref[rows_at(row, step), z.pack + h : z.pack + h + 1]
            sizes_ref[at, :] = jnp.broadcast_to(size, (step, LANES))
            return carry

        lax.fori_loop(0, z.packed // step, one, 0, unroll=z.packed == step)
    for s in range(z.side):
        at = rows_at(((d >> 1) ^ s) * z.half, z.half)
        grads = sum(
            jnp.dot(dense_ref[at, :], block_ref[...], preferred_element_type=jnp.float32)
            for dense_ref, block_ref in zip(dense_refs, (own_ref, other_ref))
        )
        grad_refs[s][...] = grads / sizes_ref[at, :1]


def passage_kernel(z, own_ref, query_ref, other_ref, other_query_ref, out_ref):
    def one(i, carry):
        at = rows_at(i * 256, 256)
        grads = [
            lax.dot_general(
                dense_ref[:, at], rows_ref[...], (((0,), (0,)), ((), ())),
                preferred_element_type=jnp.float32,
            )
            for dense_ref, rows_ref in [(own_ref, query_ref), (other_ref, other_query_ref)]
        ]
        out_ref[at, :] = z.scale * (grads[0] + grads[1])
        return carry

    lax.fori_loop(0, z.block // 256, one, 0)


def call(z, kernel, outs, scratch, args, flops, spaces=None, vmem=None):
    spaces = spaces or [pltpu.VMEM] * len(args)
    moved = sum(a.size * a.dtype.itemsize for a in args)
    moved += sum(o.size * jnp.dtype(o.dtype).itemsize for o in outs)
    return pl.pallas_call(
        lambda *refs: kernel(z, *refs),
        out_shape=outs,
        in_specs=[pl.BlockSpec(memory_space=space) for space in spaces],
        out_specs=[pl.BlockSpec(memory_space=pltpu.VMEM)] * len(outs),
        scratch_shapes=scratch,
        compiler_params=pltpu.CompilerParams(vmem_limit_bytes=vmem or z.vmem),
        cost_estimate=pl.CostEstimate(flops=flops, bytes_accessed=moved, transcendentals=0),
    )(*args)


def body(queries, passages, pos_ids, neg_ids):
    z = Sizes(queries, passages, neg_ids)
    f32, bf16, i32 = jnp.float32, jnp.bfloat16, jnp.int32
    shape = jax.ShapeDtypeStruct

    pieces = call(
        z, message_kernel, [shape((z.own, z.width + LANES), bf16)] * z.tensor,
        [
            pltpu.SMEM(pos_ids.shape, i32), pltpu.VMEM(neg_ids.shape, i32),
            pltpu.VMEM(queries.shape, bf16), pltpu.SemaphoreType.DMA((3,)),
        ],
        [pos_ids, neg_ids, queries], 0, [pltpu.HBM] * 3, 60 * 2**20,
    )
    passages, pieces = lax.optimization_barrier((passages, pieces))
    other_block = swap(passages, "dp", 1)
    (own_block,) = call(
        z, fetch_kernel, [shape(passages.shape, bf16)], [pltpu.SemaphoreType.DMA],
        [passages], 0, [pltpu.HBM],
    )
    plane = [swap(pieces[s], "tensor", s) if s else pieces[s] for s in z.tensor_order]
    plane = jnp.concatenate(plane, axis=0)
    plane, own_block, other_block = lax.optimization_barrier((plane, own_block, other_block))
    chip = [swap(plane, "corpus", s) if s else plane for s in z.corpus_order]
    if z.cuts == 1:
        chip = [jnp.concatenate(chip, axis=0)]
    arrived = gather_pairs(chip)
    others = [swap(piece[:, z.width :], "dp", 1) for piece in arrived]
    blocks = [own_block, other_block]

    work = 2 * z.rows * z.wide * z.width
    query_rows, index, pos_rows, inside, part = call(
        z, score_kernel,
        [
            shape((z.rows, z.width), bf16), shape((z.nrows, z.deep), i32),
            shape((z.named, LANES), i32), shape((z.packed, z.lanes), i32),
            shape((z.packed, z.lanes), f32),
        ],
        [
            pltpu.VMEM((z.named, LANES), f32), pltpu.VMEM((z.rows, z.lanes), i32),
            pltpu.VMEM((z.rows, z.lanes), f32),
        ],
        arrived + others + blocks, work,
    )
    (hot,) = call(z, hot_kernel, [shape((z.named, z.wide), bf16)], [], [pos_rows], work // 64)
    total = sum([swap(part, "tensor", s) for s in range(1, z.tensor)], part)
    exponent, stat = call(
        z, stat_kernel, [shape((z.packed, z.lanes), f32), shape((z.high, z.packed), f32)], [],
        [total, inside], total.size,
    )
    stats = [swap(stat, "corpus", s) if s else stat for s in z.corpus_order]
    (raw,) = call(
        z, place_kernel, [shape((z.rows, z.wide), f32)],
        [
            pltpu.VMEM((z.nrows, z.deep), f32), pltpu.VMEM((3, z.nrows, z.deep), f32),
            pltpu.VMEM((z.rows * z.chunks, LANES), f32),
        ],
        [exponent, index, hot], 3 * work,
    )
    if z.cuts == 1:
        stats = [jnp.concatenate(stats, axis=0)]
    stats = gather_pairs(stats)
    dense, other_dense, loss, size, *grads = call(
        z, weight_kernel,
        [shape((z.rows, z.block), bf16)] * 2 + [shape((z.own, LANES), f32)] * 2
        + [shape((z.half, z.width), f32)] * z.side,
        [
            pltpu.VMEM((z.side * z.corpus, z.high, z.packed), f32),
            pltpu.VMEM((LANES, z.packed), f32), pltpu.VMEM((z.packed, LANES), f32),
            pltpu.VMEM((z.rows, LANES), f32),
        ],
        stats + [raw, hot] + blocks, work,
    )
    half = scatter_pairs(grads).astype(jnp.float16).reshape(z.groups, z.own, z.width)
    half = lax.all_to_all(half, ("tensor", "corpus"), split_axis=0, concat_axis=0, tiled=True)
    (grad_pass,) = call(
        z, passage_kernel, [shape((z.block, z.width), f32)], [],
        [dense, query_rows, swap(other_dense, "dp", 1), swap(query_rows, "dp", 1)], work,
    )
    half, grad_pass = lax.optimization_barrier((half, grad_pass))
    half = half.astype(f32).reshape(z.tensor, z.corpus, z.own, z.width).sum(axis=1)
    grad_query = half.swapaxes(0, 1).reshape(z.own, z.feat) * (size[:, :1] * z.scale)
    return (grad_query, loss[:, 0], grad_pass)


def solution(mesh):
    spread = ("dp", "tensor", "corpus")
    in_specs = (P(spread, None), P(("dp", "corpus"), "tensor"), P(spread), P(spread, None))
    out_specs = (P(spread, None), P(spread), P(("dp", "corpus"), "tensor"))
    return jax.shard_map(body, mesh=mesh, in_specs=in_specs, out_specs=out_specs, check_vma=False)
```

```python
import jax
import jax.numpy as jnp
from jax import lax
from jax.experimental import pallas as pl
from jax.experimental.pallas import tpu as pltpu
from jax.sharding import PartitionSpec as P

LANES = 128
FAR = -(2**20)
LOW = -1e30
SUM, ZED = [3, 2, 1], [0, 2, 3, 1]


def swap(value, axis, bit):
    size = lax.axis_size(axis)
    return lax.ppermute(value, axis, [(i, i ^ bit) for i in range(size)])


def gather_pairs(pieces):
    bit = 2
    while bit < lax.axis_size("dp"):
        pieces = pieces + [swap(piece, "dp", bit) for piece in pieces]
        bit *= 2
    return pieces


def scatter_pairs(pieces):
    while len(pieces) > 1:
        n = len(pieces) // 2
        pieces = [
            mine + swap(theirs, "dp", 2 * n) for mine, theirs in zip(pieces[:n], pieces[n:])
        ]
    return pieces[0]


class Sizes:
    def __init__(self, queries, passages, neg_ids):
        self.own, self.feat = queries.shape
        self.block, self.width = passages.shape
        self.negs = neg_ids.shape[1]
        self.dp = lax.axis_size("dp")
        self.tensor = lax.axis_size("tensor")
        self.corpus = lax.axis_size("corpus")
        self.side = self.dp // 2
        self.groups = self.tensor * self.corpus
        self.half = self.groups * self.own
        self.rows = self.side * self.half
        self.named = self.dp * self.half
        self.columns = self.dp * self.own
        self.items = self.columns + self.negs
        self.lanes = -(-self.items // LANES) * LANES
        self.pack = max(1, LANES // self.items)
        self.packed = self.rows // self.pack
        self.neg_at = self.columns % LANES
        self.pos_at = 0 if self.neg_at else self.negs
        self.wide = 2 * self.block
        self.chunks = self.wide // LANES
        self.scale = self.feat ** (-0.5)
        self.tensor_order = SUM if self.tensor == 4 else list(range(1, self.tensor))
        self.corpus_order = ZED if self.corpus == 4 else list(range(self.corpus))
        self.cuts = self.corpus if self.side == 1 else 1
        self.deep = 2 * LANES
        self.seats = self.deep // self.negs
        self.nrows = self.rows // self.seats
        self.joint = max(1, self.deep // self.columns)
        self.run = self.joint * self.own
        self.sets = self.groups // self.joint
        self.high = -(-3 * self.pack // 8) * 8
        self.vmem = min(61, 20 + 20 * self.rows // 1024) * 2**20


def places():
    return [lax.axis_index(axis) for axis in ("dp", "tensor", "corpus")]


def rows_at(start, size):
    return pl.ds(pl.multiple_of(start, size), size)


def message_kernel(z, pos_in, neg_in, query_in, out_ref, pos_ref, neg_ref, query_ref, sems):
    moves = [
        pltpu.make_async_copy(source, target, sems.at[i])
        for i, (source, target) in enumerate(
            [(pos_in, pos_ref), (neg_in, neg_ref), (query_in, query_ref)]
        )
    ]
    for move in moves:
        move.start()
    for move in moves:
        move.wait()
    half = LANES // 2
    row = lax.broadcasted_iota(jnp.int32, (z.own, half), 0)
    pos = jnp.zeros((z.own, half), jnp.int32)
    for i in range(z.own):
        pos = jnp.where(row == i, pos_ref[i], pos)
    ids = [neg_ref[...], pos[:, : half - z.neg_at - z.negs]]
    ids = jnp.concatenate([part for part in [pos[:, : z.neg_at]] + ids if part.shape[1]], axis=1)
    ids = jnp.concatenate([ids >> 8, ids & 255], axis=1)
    code = ids.astype(jnp.float32).astype(jnp.bfloat16)
    for k in range(z.groups):
        t = k // z.corpus
        out_ref[k, :, : z.width] = query_ref[:, t * z.width : (t + 1) * z.width]
        out_ref[k, :, z.width :] = code


def fetch_kernel(z, block_ref, passage_ref, sem):
    fetch = pltpu.make_async_copy(block_ref, passage_ref, sem)
    fetch.start()
    fetch.wait()


def seat_rows(z, out_ref, source):
    lane = lax.broadcasted_iota(jnp.int32, (z.nrows, LANES), 1)
    per = LANES // z.negs
    for chunk in range(z.deep // LANES):
        packed = None
        for k in range(per):
            ref, row, at = source(chunk * per + k)
            base = at // LANES * LANES
            piece = ref[pl.ds(row, z.nrows), base : base + LANES]
            turn = (k * z.negs - at) % LANES
            piece = pltpu.roll(piece, turn, 1) if turn else piece
            packed = piece if packed is None else jnp.where(lane < k * z.negs, packed, piece)
        out_ref[:, chunk * LANES : (chunk + 1) * LANES] = packed


def score_kernel(z, *refs):
    arrived, block_refs = refs[: z.side], refs[z.side : z.side + 2]
    query_ref, score_ref = refs[z.side + 2 :]
    d = lax.axis_index("dp")
    for su in range(z.side):
        at = rows_at(((d ^ (2 * su)) >> 1) * z.half, z.half)
        query_ref[at, :] = arrived[su][:, : z.width]
    step = min(z.rows, 256)

    def score(i, carry):
        at = rows_at(i * step, step)
        for side, block_ref in enumerate(block_refs):
            score_ref[at, side * z.block : (side + 1) * z.block] = lax.dot_general(
                query_ref[at, :], block_ref[...], (((1,), (1,)), ((), ())),
                preferred_element_type=jnp.float32,
            )
        return carry

    lax.fori_loop(0, z.rows // step, score, 0, unroll=z.rows == step)


def localizer(z):
    d, _, c = places()

    def localize(ids):
        found = jnp.full(ids.shape, float(FAR), jnp.float32)
        for side in range(2):
            local = ids - (((d ^ side) * z.corpus + c) * z.block).astype(jnp.float32)
            inside = (local >= 0.0) & (local < float(z.block))
            found = jnp.where(inside, local + float(side * z.block), found)
        return found

    return localize


def pick_kernel(z, *refs):
    arrived, others, score_ref = refs[: z.side], refs[z.side : 2 * z.side], refs[2 * z.side]
    part_ref, local_ref, id_ref, logit_ref = refs[2 * z.side + 1 :]
    d = lax.axis_index("dp")
    localize = localizer(z)
    for su in range(z.side):
        from_d = d ^ (2 * su)
        for side, code in enumerate([arrived[su][:, z.width :], others[su][...]]):
            code = code.astype(jnp.float32)
            at = rows_at((from_d ^ side) * z.half, z.half)
            id_ref[at, :] = code * 256.0 + pltpu.roll(code, LANES // 2, 1)
    wide = -(-z.columns // LANES) * LANES
    row = lax.broadcasted_iota(jnp.int32, (z.half, wide), 0) & (z.own - 1)
    col = lax.broadcasted_iota(jnp.int32, (z.half, wide), 1)
    group_ids = jnp.zeros((z.groups, wide), jnp.float32)
    for h in range(z.dp):
        at = pl.ds(h * z.half, z.half)
        pos = jnp.broadcast_to(id_ref[at, z.pos_at : z.pos_at + 1], (z.half, wide))
        kept = jnp.where(col == row + h * z.own, pos, 0.0)
        group_ids += jnp.sum(kept.reshape(z.groups, z.own, wide), axis=1)
    batch_ids = jnp.broadcast_to(group_ids[:, None, :], (z.groups, z.own, wide))
    batch_ids = batch_ids.reshape(z.half, wide)
    lane = lax.broadcasted_iota(jnp.int32, (z.half, LANES), 1)
    for u in range(z.side):
        ids = id_ref[rows_at((2 * u + (d & 1)) * z.half, z.half), :]
        for base in range(0, z.lanes, LANES):
            named = ids
            if base < z.columns:
                named = jnp.where(lane + base < z.columns, batch_ids[:, base : base + LANES], ids)
            local = jnp.where(lane + base < z.items, localize(named), float(FAR))
            local_ref[pl.ds(u * z.half, z.half), base : base + LANES] = local.astype(jnp.int32)
    step = min(z.rows, 256)

    def pick(i, carry):
        at = rows_at(i * step, step)
        for base in range(0, z.lanes, LANES):
            local = local_ref[at, base : base + LANES]
            chunk, within = local >> 7, local & (LANES - 1)
            picked = jnp.zeros((step, LANES), jnp.float32)
            for j in range(z.chunks):
                found = jnp.take_along_axis(
                    score_ref[at, j * LANES : (j + 1) * LANES], within, axis=1
                )
                picked = jnp.where(chunk == j, found, picked)
            logit_ref[at, base : base + LANES] = picked
        return carry

    lax.fori_loop(0, z.rows // step, pick, 0, unroll=z.rows == step)
    pack_rows(z, logit_ref, part_ref)


def pack_rows(z, source_ref, target_ref):
    lane = lax.broadcasted_iota(jnp.int32, (z.packed, z.lanes), 1)
    packed = source_ref[pl.ds(0, z.packed), :]
    for h in range(1, z.pack):
        other = pltpu.roll(source_ref[pl.ds(h * z.packed, z.packed), :], h * z.items, 1)
        packed = jnp.where(lane < h * z.items, packed, other)
    target_ref[...] = packed


def index_kernel(z, local_ref, id_ref, index_ref, inside_ref, hot_ref):
    seat_rows(z, index_ref, lambda j: (local_ref, j * z.nrows, z.columns))
    pack_rows(z, local_ref, inside_ref)
    localize = localizer(z)
    lane = lax.broadcasted_iota(jnp.int32, (z.half, LANES), 1)
    for h in range(z.dp):
        at = pl.ds(h * z.half, z.half)
        pos = localize(jnp.broadcast_to(id_ref[at, z.pos_at : z.pos_at + 1], (z.half, LANES)))
        pos = pos.astype(jnp.int32)
        for j in range(z.chunks):
            same = jnp.where(pos == lane + j * LANES, 1.0, 0.0).astype(jnp.bfloat16)
            hot_ref[at, j * LANES : (j + 1) * LANES] = same


def stat_kernel(z, total_ref, inside_ref, exponent_ref, stat_ref):
    step = min(z.packed, 256)
    side = lax.axis_index("dp") & 1

    def one(i, carry):
        at = rows_at(i * step, step)
        logits = total_ref[at, :] * z.scale
        lane = lax.broadcasted_iota(jnp.int32, logits.shape, 1)
        row = lax.broadcasted_iota(jnp.int32, logits.shape, 0) + i * step
        short = lax.broadcasted_iota(jnp.int32, (step, LANES), 1)
        named = inside_ref[at, :] >= 0
        exponents = jnp.zeros(logits.shape, jnp.float32)
        stats = jnp.zeros((step, LANES), jnp.float32)
        for h in range(z.pack):
            mask = named & (lane >= h * z.items) & (lane < (h + 1) * z.items)
            top = jnp.max(jnp.where(mask, logits, LOW), axis=1, keepdims=True)
            exponent = jnp.where(mask, jnp.exp(logits - top), 0.0)
            query = row + h * z.packed
            own = (2 * (query // z.half) + side) * z.own + (query & (z.own - 1)) + h * z.items
            chosen = jnp.where(mask & (lane == own), logits, 0.0)
            values = (
                top,
                jnp.sum(exponent, axis=1, keepdims=True),
                jnp.sum(chosen, axis=1, keepdims=True),
            )
            for k, value in enumerate(values):
                stats = jnp.where(short == 3 * h + k, value, stats)
            exponents = exponents + exponent
        exponent_ref[at, :] = exponents
        stat_ref[:, at] = stats.T[: z.high, :]
        return carry

    lax.fori_loop(0, z.packed // step, one, 0, unroll=z.packed == step)


def split(values):
    parts = []
    for _ in range(3):
        part = values.astype(jnp.bfloat16)
        parts.append(part)
        values = values - part.astype(jnp.float32)
    return parts


def join(tiles):
    n = tiles.shape[0] // 3
    return tiles[:n] + (tiles[n : 2 * n] + tiles[2 * n :])


def place_kernel(z, exponent_ref, index_ref, hot_ref, raw_ref, seat_ref, part_ref, tile_ref):
    def seat(j):
        h, row = divmod(j * z.nrows, z.packed)
        return exponent_ref, row, h * z.items + z.columns

    seat_rows(z, seat_ref, seat)
    for k, part in enumerate(split(seat_ref[...])):
        part_ref[k] = part.astype(jnp.float32)
    high = z.seats * z.chunks
    shape = (high, z.deep)
    tall = lax.broadcasted_iota(jnp.int32, shape, 0).astype(jnp.bfloat16)
    shift = lax.broadcasted_iota(jnp.int32, (1, z.deep), 1) // z.negs * z.chunks
    spread = lax.broadcasted_iota(jnp.int32, (LANES, z.deep), 0).astype(jnp.bfloat16)
    turns = min(32, z.nrows)
    none, unit = jnp.bfloat16(0), jnp.bfloat16(1)

    def place(i, carry):
        for k in range(turns):
            r = i * turns + k
            local = index_ref[pl.ds(r, 1), :]
            chunk = ((local >> 7) + shift).astype(jnp.bfloat16)
            within = (local & (LANES - 1)).astype(jnp.bfloat16)
            here = jnp.broadcast_to(chunk, shape) == tall
            left = [
                jnp.where(
                    here,
                    jnp.broadcast_to(part_ref[p, pl.ds(r, 1), :].astype(jnp.bfloat16), shape), none,
                )
                for p in range(3)
            ]
            right = jnp.where(jnp.broadcast_to(within, (LANES, z.deep)) == spread, unit, none)
            tiles = join(lax.dot_general(
                jnp.concatenate(left, axis=0), right, (((1,), (1,)), ((), ())),
                preferred_element_type=jnp.float32,
            ))
            for j in range(z.seats):
                at = rows_at((j * z.nrows + r) * z.chunks, z.chunks)
                tile_ref[at, :] = tiles[j * z.chunks : (j + 1) * z.chunks, :]
        return carry

    lax.fori_loop(0, z.nrows // turns, place, 0, unroll=z.nrows == turns)
    lane = lax.broadcasted_iota(jnp.int32, (z.run, LANES), 1)
    group = lax.broadcasted_iota(jnp.int32, (z.run, LANES), 0) // z.own
    for n in range(z.sets):
        hot = [hot_ref[pl.ds(h * z.half + n * z.run, z.run), :] for h in range(z.dp)]
        hot = jnp.concatenate(hot, axis=0)
        for u in range(z.side):
            first_row = u * z.half + n * z.run
            side, row = divmod(first_row, z.packed)
            left = []
            for chunk in range(z.deep // LANES):
                if z.joint == 1:
                    part = exponent_ref[pl.ds(row, z.run), chunk * LANES : (chunk + 1) * LANES]
                else:
                    at = chunk * LANES + lane
                    from_lane = side * z.items + at // z.run * z.own + at % z.own
                    part = jnp.take_along_axis(
                        exponent_ref[pl.ds(row, z.run), :LANES], from_lane, axis=1
                    )
                    part = jnp.where(at // z.own % z.joint == group, part, 0.0)
                left.append(part)
            left = jnp.concatenate(split(jnp.concatenate(left, axis=1)), axis=0)
            shared = join(jnp.dot(left, hot, preferred_element_type=jnp.float32))
            for j in range(z.chunks):
                alone = tile_ref[pl.ds(first_row * z.chunks + j, z.run, stride=z.chunks), :]
                raw_ref[pl.ds(first_row, z.run), j * LANES : (j + 1) * LANES] = (
                    alone + shared[:, j * LANES : (j + 1) * LANES]
                )


def weight_kernel(z, *refs):
    count = z.side * z.cuts
    parts, refs = refs[:count], refs[count:]
    raw_ref, hot_ref, own_ref, other_ref = refs[:4]
    dense_refs, (loss_ref, size_ref) = refs[4:6], refs[6:8]
    grad_refs = refs[8 : 8 + z.side]
    stat_ref, row_ref, back_ref, sizes_ref = refs[8 + z.side :]
    d, t, c = places()
    for su in range(z.side):
        for sc in range(z.corpus):
            part = parts[su * z.cuts + sc % z.cuts][pl.ds(sc // z.cuts * z.high, z.high), :]
            stat_ref[((d >> 1) ^ su) * z.corpus + (c ^ z.corpus_order[sc])] = part
    planes = z.side * z.corpus
    row_ref[...] = jnp.zeros_like(row_ref)
    for h in range(z.pack):
        tops = [stat_ref[b, 3 * h : 3 * h + 1, :] for b in range(planes)]
        top = tops[0]
        for other in tops[1:]:
            top = jnp.maximum(top, other)
        total, chosen = jnp.zeros_like(top), jnp.zeros_like(top)
        for b in range(planes):
            total += stat_ref[b, 3 * h + 1 : 3 * h + 2, :] * jnp.exp(tops[b] - top)
            chosen += stat_ref[b, 3 * h + 2 : 3 * h + 3, :]
        mine = stat_ref[(d >> 1) * z.corpus + c, 3 * h : 3 * h + 1, :]
        rest = 1.0 - jnp.exp(chosen - top) / total
        row_ref[h : h + 1, :] = jnp.exp(mine - top) / total
        row_ref[z.pack + h : z.pack + h + 1, :] = jnp.maximum(rest, 2.0**-24)
        row_ref[2 * z.pack + h : 2 * z.pack + h + 1, :] = jnp.log(total) + top - chosen
    back_ref[...] = row_ref[...].T
    mine = (((d >> 1) * z.tensor + t) * z.corpus + c) * z.own
    place = rows_at(mine % z.packed, z.own)
    for k, target_ref in [(1, size_ref), (2, loss_ref)]:
        value = back_ref[place, k * z.pack : k * z.pack + 1]
        for h in range(1, z.pack):
            other = back_ref[place, k * z.pack + h : k * z.pack + h + 1]
            value = jnp.where(mine // z.packed == h, other, value)
        target_ref[...] = jnp.broadcast_to(value, (z.own, LANES))
    step = min(z.packed, 128)
    for h in range(z.pack):

        def one(i, carry):
            row = i * step
            query = h * z.packed + row
            at = rows_at(query, step)
            named = rows_at((2 * (query // z.half) + (d & 1)) * z.half + query % z.half, step)
            ratio = back_ref[rows_at(row, step), h : h + 1]
            weights = raw_ref[at, :] * ratio - hot_ref[named, :].astype(jnp.float32)
            weights = weights.astype(jnp.bfloat16)
            dense_refs[0][at, :] = weights[:, : z.block]
            dense_refs[1][at, :] = weights[:, z.block :]
            size = back_ref[rows_at(row, step), z.pack + h : z.pack + h + 1]
            sizes_ref[at, :] = jnp.broadcast_to(size, (step, LANES))
            return carry

        lax.fori_loop(0, z.packed // step, one, 0, unroll=z.packed == step)
    for s in range(z.side):
        at = rows_at(((d >> 1) ^ s) * z.half, z.half)
        grads = sum(
            jnp.dot(dense_ref[at, :], block_ref[...], preferred_element_type=jnp.float32)
            for dense_ref, block_ref in zip(dense_refs, (own_ref, other_ref))
        )
        grad_refs[s][...] = grads / sizes_ref[at, :1]


def passage_kernel(z, own_ref, query_ref, other_ref, other_query_ref, out_ref):
    def one(i, carry):
        at = rows_at(i * 256, 256)
        grads = [
            lax.dot_general(
                dense_ref[:, at], rows_ref[...], (((0,), (0,)), ((), ())),
                preferred_element_type=jnp.float32,
            )
            for dense_ref, rows_ref in [(own_ref, query_ref), (other_ref, other_query_ref)]
        ]
        out_ref[at, :] = z.scale * (grads[0] + grads[1])
        return carry

    lax.fori_loop(0, z.block // 256, one, 0)


def call(z, kernel, outs, scratch, args, flops, spaces=None, vmem=None):
    spaces = spaces or [pltpu.VMEM] * len(args)
    moved = sum(a.size * a.dtype.itemsize for a in args)
    moved += sum(o.size * jnp.dtype(o.dtype).itemsize for o in outs)
    return pl.pallas_call(
        lambda *refs: kernel(z, *refs),
        out_shape=outs,
        in_specs=[pl.BlockSpec(memory_space=space) for space in spaces],
        out_specs=[pl.BlockSpec(memory_space=pltpu.VMEM)] * len(outs),
        scratch_shapes=scratch,
        compiler_params=pltpu.CompilerParams(vmem_limit_bytes=vmem or z.vmem),
        cost_estimate=pl.CostEstimate(flops=flops, bytes_accessed=moved, transcendentals=0),
    )(*args)


def body(queries, passages, pos_ids, neg_ids):
    z = Sizes(queries, passages, neg_ids)
    f32, bf16, i32 = jnp.float32, jnp.bfloat16, jnp.int32
    shape = jax.ShapeDtypeStruct

    pieces = call(
        z, message_kernel, [shape((z.groups, z.own, z.width + LANES), bf16)],
        [
            pltpu.SMEM(pos_ids.shape, i32), pltpu.VMEM(neg_ids.shape, i32),
            pltpu.VMEM(queries.shape, bf16), pltpu.SemaphoreType.DMA((3,)),
        ],
        [pos_ids, neg_ids, queries], 0, [pltpu.HBM] * 3, 60 * 2**20,
    )
    passages, pieces = lax.optimization_barrier((passages, pieces))
    (own_block,) = call(
        z, fetch_kernel, [shape(passages.shape, bf16)], [pltpu.SemaphoreType.DMA],
        [passages], 0, [pltpu.HBM],
    )
    other_block = swap(passages, "dp", 1)
    chip = lax.all_to_all(pieces[0], ("tensor", "corpus"), split_axis=0, concat_axis=0, tiled=True)
    chip, own_block, other_block = lax.optimization_barrier((chip, own_block, other_block))
    arrived = gather_pairs([chip.reshape(z.half, z.width + LANES)])
    others = [swap(piece[:, z.width :], "dp", 1) for piece in arrived]
    blocks = [own_block, other_block]

    work = 2 * z.rows * z.wide * z.width
    query_rows, scores = call(
        z, score_kernel, [shape((z.rows, z.width), bf16), shape((z.rows, z.wide), f32)], [],
        arrived + blocks, work,
    )
    part, local, ids = call(
        z, pick_kernel,
        [
            shape((z.packed, z.lanes), f32), shape((z.rows, z.lanes), i32),
            shape((z.named, LANES), f32),
        ],
        [pltpu.VMEM((z.rows, z.lanes), f32)], arrived + others + [scores], work // 16,
    )
    index, inside, hot = call(
        z, index_kernel,
        [
            shape((z.nrows, z.deep), i32), shape((z.packed, z.lanes), i32),
            shape((z.named, z.wide), bf16),
        ],
        [], [local, ids], work // 64,
    )
    total = sum([swap(part, "tensor", s) for s in z.tensor_order], part)
    exponent, stat = call(
        z, stat_kernel, [shape((z.packed, z.lanes), f32), shape((z.high, z.packed), f32)], [],
        [total, inside], total.size,
    )
    stats = [swap(stat, "corpus", s) if s else stat for s in z.corpus_order]
    (raw,) = call(
        z, place_kernel, [shape((z.rows, z.wide), f32)],
        [
            pltpu.VMEM((z.nrows, z.deep), f32), pltpu.VMEM((3, z.nrows, z.deep), f32),
            pltpu.VMEM((z.rows * z.chunks, LANES), f32),
        ],
        [exponent, index, hot], 3 * work,
    )
    if z.cuts == 1:
        stats = [jnp.concatenate(stats, axis=0)]
    stats = gather_pairs(stats)
    dense, other_dense, loss, size, *grads = call(
        z, weight_kernel,
        [shape((z.rows, z.block), bf16)] * 2 + [shape((z.own, LANES), f32)] * 2
        + [shape((z.half, z.width), f32)] * z.side,
        [
            pltpu.VMEM((z.side * z.corpus, z.high, z.packed), f32),
            pltpu.VMEM((LANES, z.packed), f32), pltpu.VMEM((z.packed, LANES), f32),
            pltpu.VMEM((z.rows, LANES), f32),
        ],
        stats + [raw, hot] + blocks, work,
    )
    half = scatter_pairs(grads).astype(jnp.float16).reshape(z.groups, z.own, z.width)
    half = lax.all_to_all(half, ("tensor", "corpus"), split_axis=0, concat_axis=0, tiled=True)
    (grad_pass,) = call(
        z, passage_kernel, [shape((z.block, z.width), f32)], [],
        [dense, query_rows, swap(other_dense, "dp", 1), swap(query_rows, "dp", 1)], work,
    )
    half, grad_pass = lax.optimization_barrier((half, grad_pass))
    half = half.astype(f32).reshape(z.tensor, z.corpus, z.own, z.width).sum(axis=1)
    grad_query = half.swapaxes(0, 1).reshape(z.own, z.feat) * (size[:, :1] * z.scale)
    return (grad_query, loss[:, 0], grad_pass)


def solution(mesh):
    spread = ("dp", "tensor", "corpus")
    in_specs = (P(spread, None), P(("dp", "corpus"), "tensor"), P(spread), P(spread, None))
    out_specs = (P(spread, None), P(spread), P(("dp", "corpus"), "tensor"))
    return jax.shard_map(body, mesh=mesh, in_specs=in_specs, out_specs=out_specs, check_vma=False)
```

```python
import jax
import jax.numpy as jnp
from jax import lax
from jax.experimental import pallas as pl
from jax.experimental.pallas import tpu as pltpu
from jax.sharding import PartitionSpec as P

LANES = 128
FAR = -(2**20)
LOW = -1e30
SUM, ZED = [3, 2, 1], [0, 2, 3, 1]


def swap(value, axis, bit):
    size = lax.axis_size(axis)
    return lax.ppermute(value, axis, [(i, i ^ bit) for i in range(size)])


def gather_pairs(pieces):
    bit = 2
    while bit < lax.axis_size("dp"):
        pieces = pieces + [swap(piece, "dp", bit) for piece in pieces]
        bit *= 2
    return pieces


def scatter_pairs(pieces):
    while len(pieces) > 1:
        n = len(pieces) // 2
        pieces = [
            mine + swap(theirs, "dp", 2 * n) for mine, theirs in zip(pieces[:n], pieces[n:])
        ]
    return pieces[0]


class Sizes:
    def __init__(self, queries, passages, neg_ids):
        self.own, self.feat = queries.shape
        self.block, self.width = passages.shape
        self.negs = neg_ids.shape[1]
        self.dp = lax.axis_size("dp")
        self.tensor = lax.axis_size("tensor")
        self.corpus = lax.axis_size("corpus")
        self.side = self.dp // 2
        self.groups = self.tensor * self.corpus
        self.half = self.groups * self.own
        self.rows = self.side * self.half
        self.named = self.dp * self.half
        self.columns = self.dp * self.own
        self.items = self.columns + self.negs
        self.lanes = -(-self.items // LANES) * LANES
        self.pack = max(1, LANES // self.items)
        self.packed = self.rows // self.pack
        self.neg_at = self.columns % LANES
        self.pos_at = 0 if self.neg_at else self.negs
        self.wide = 2 * self.block
        self.chunks = self.wide // LANES
        self.scale = self.feat ** (-0.5)
        self.tensor_order = SUM if self.tensor == 4 else list(range(1, self.tensor))
        self.corpus_order = ZED if self.corpus == 4 else list(range(self.corpus))
        self.cuts = self.corpus if self.side == 1 else 1
        self.deep = 2 * LANES
        self.seats = self.deep // self.negs
        self.nrows = self.rows // self.seats
        self.joint = max(1, self.deep // self.columns)
        self.run = self.joint * self.own
        self.sets = self.groups // self.joint
        self.high = -(-3 * self.pack // 8) * 8
        self.dense_ids = self.block * self.dp * self.corpus <= 2**13 and self.own == 16
        self.fold = self.own // 2 if self.dense_ids else self.own
        self.message = 2 * self.width + LANES if self.dense_ids else self.width + LANES
        self.vmem = min(61, 20 + 20 * self.rows // 1024) * 2**20


def places():
    return [lax.axis_index(axis) for axis in ("dp", "tensor", "corpus")]


def rows_at(start, size):
    return pl.ds(pl.multiple_of(start, size), size)


def message_kernel(z, pos_in, neg_in, query_in, out_ref, pos_ref, neg_ref, query_ref, sems):
    moves = [
        pltpu.make_async_copy(source, target, sems.at[i])
        for i, (source, target) in enumerate(
            [(pos_in, pos_ref), (neg_in, neg_ref), (query_in, query_ref)]
        )
    ]
    for move in moves:
        move.start()
    for move in moves:
        move.wait()
    half = LANES // 2
    row = lax.broadcasted_iota(jnp.int32, (z.own, half), 0)
    pos = jnp.zeros((z.own, half), jnp.int32)
    for i in range(z.own):
        pos = jnp.where(row == i, pos_ref[i], pos)
    ids = [neg_ref[...], pos[:, : half - z.neg_at - z.negs]]
    ids = jnp.concatenate([part for part in [pos[:, : z.neg_at]] + ids if part.shape[1]], axis=1)
    if z.dense_ids:
        code = 1.0 + (ids & 127).astype(jnp.float32) / 128.0
        for bit in range(6):
            code = jnp.where((ids >> (7 + bit)) & 1 == 1, code * 2.0 ** (1 << bit), code)
        code = code * 2.0**-32
        code = jnp.concatenate([code[: z.fold], code[z.fold :]], axis=1)
        for t in range(z.tensor):
            rows = query_ref[:, t * z.width : (t + 1) * z.width].astype(jnp.float32)
            rows = jnp.concatenate([rows[: z.fold], rows[z.fold :], code], axis=1)
            rows = jnp.concatenate([rows, rows], axis=0).astype(jnp.bfloat16)
            for c in range(0, z.corpus, 2):
                out_ref[pl.ds((t * z.corpus + c) * z.fold, z.own), :] = rows
        return
    ids = jnp.concatenate([ids >> 8, ids & 255], axis=1)
    code = ids.astype(jnp.float32).astype(jnp.bfloat16)
    for k in range(z.groups):
        t = k // z.corpus
        at = pl.ds(k * z.own, z.own)
        out_ref[at, : z.width] = query_ref[:, t * z.width : (t + 1) * z.width]
        out_ref[at, z.width :] = code


def unfold(z, first, second):
    width = first.shape[-1]
    pair = [part.reshape(z.groups, z.fold, width) for part in (first, second)]
    return jnp.concatenate(pair, axis=1).reshape(z.half, width)


def decode(z, code):
    code = code.astype(jnp.float32)
    if not z.dense_ids:
        return code * 256.0 + pltpu.roll(code, LANES // 2, 1)
    code = code * 2.0**32
    high = jnp.zeros_like(code)
    for bit in range(5, -1, -1):
        big = code >= 2.0 ** (1 << bit)
        high = jnp.where(big, high + float(128 << bit), high)
        code = jnp.where(big, code * 2.0 ** -(1 << bit), code)
    ids = high + (code - 1.0) * 128.0
    return unfold(z, ids, pltpu.roll(ids, LANES // 2, 1))


def fetch_kernel(z, block_ref, passage_ref, sem):
    fetch = pltpu.make_async_copy(block_ref, passage_ref, sem)
    fetch.start()
    fetch.wait()


def seat_rows(z, out_ref, source):
    lane = lax.broadcasted_iota(jnp.int32, (z.nrows, LANES), 1)
    per = LANES // z.negs
    for chunk in range(z.deep // LANES):
        packed = None
        for k in range(per):
            ref, row, at = source(chunk * per + k)
            base = at // LANES * LANES
            piece = ref[pl.ds(row, z.nrows), base : base + LANES]
            turn = (k * z.negs - at) % LANES
            piece = pltpu.roll(piece, turn, 1) if turn else piece
            packed = piece if packed is None else jnp.where(lane < k * z.negs, packed, piece)
        out_ref[:, chunk * LANES : (chunk + 1) * LANES] = packed


def score_kernel(z, *refs):
    arrived, block_refs = refs[: z.side], refs[z.side : z.side + 2]
    query_ref, score_ref, own_ref, near_ref = refs[z.side + 2 :]
    d = lax.axis_index("dp")
    localize = localizer(z)
    for su in range(z.side):
        at = rows_at(((d ^ (2 * su)) >> 1) * z.half, z.half)
        rows = arrived[su][:, : z.message - LANES]
        if z.dense_ids:
            rows = rows.astype(jnp.float32)
            rows = unfold(z, rows[:, : z.width], rows[:, z.width :]).astype(jnp.bfloat16)
        query_ref[at, :] = rows
        ids = decode(z, arrived[su][:, z.message - LANES :])
        own_ref[at, :] = ids
        near_ref[at, :] = localize(ids)
    step = min(z.rows, 256)

    def score(i, carry):
        at = rows_at(i * step, step)
        for side, block_ref in enumerate(block_refs):
            score_ref[at, side * z.block : (side + 1) * z.block] = lax.dot_general(
                query_ref[at, :], block_ref[...], (((1,), (1,)), ((), ())),
                preferred_element_type=jnp.float32,
            )
        return carry

    lax.fori_loop(0, z.rows // step, score, 0, unroll=z.rows == step)


def localizer(z):
    d, _, c = places()

    def localize(ids):
        found = jnp.full(ids.shape, float(FAR), jnp.float32)
        for side in range(2):
            local = ids - (((d ^ side) * z.corpus + c) * z.block).astype(jnp.float32)
            inside = (local >= 0.0) & (local < float(z.block))
            found = jnp.where(inside, local + float(side * z.block), found)
        return found

    return localize


def pick_kernel(z, *refs):
    others, (score_ref, own_ref, near_ref) = refs[: z.side], refs[z.side : z.side + 3]
    part_ref, local_ref, id_ref, logit_ref = refs[z.side + 3 :]
    d = lax.axis_index("dp")
    for su in range(z.side):
        from_d = d ^ (2 * su)
        own = own_ref[rows_at((from_d >> 1) * z.half, z.half), :]
        id_ref[rows_at(from_d * z.half, z.half), :] = own
        id_ref[rows_at((from_d ^ 1) * z.half, z.half), :] = decode(z, others[su][...])
    wide = -(-z.columns // LANES) * LANES
    row = lax.broadcasted_iota(jnp.int32, (z.half, wide), 0) & (z.own - 1)
    col = lax.broadcasted_iota(jnp.int32, (z.half, wide), 1)
    group_ids = jnp.zeros((z.groups, wide), jnp.float32)
    for h in range(z.dp):
        at = pl.ds(h * z.half, z.half)
        pos = jnp.broadcast_to(id_ref[at, z.pos_at : z.pos_at + 1], (z.half, wide))
        kept = jnp.where(col == row + h * z.own, pos, 0.0)
        group_ids += jnp.sum(kept.reshape(z.groups, z.own, wide), axis=1)
    batch = jnp.broadcast_to(localizer(z)(group_ids)[:, None, :], (z.groups, z.own, wide))
    batch = batch.reshape(z.half, wide)
    lane = lax.broadcasted_iota(jnp.int32, (z.half, LANES), 1)
    for u in range(z.side):
        near = near_ref[pl.ds(u * z.half, z.half), :]
        for base in range(0, z.lanes, LANES):
            local = near
            if base < z.columns:
                local = jnp.where(lane + base < z.columns, batch[:, base : base + LANES], near)
            local = jnp.where(lane + base < z.items, local, float(FAR))
            local_ref[pl.ds(u * z.half, z.half), base : base + LANES] = local.astype(jnp.int32)
    step = min(z.rows, 256)

    def pick(i, carry):
        at = rows_at(i * step, step)
        for base in range(0, z.lanes, LANES):
            local = local_ref[at, base : base + LANES]
            chunk, within = local >> 7, local & (LANES - 1)
            picked = jnp.zeros((step, LANES), jnp.float32)
            for j in range(z.chunks):
                found = jnp.take_along_axis(
                    score_ref[at, j * LANES : (j + 1) * LANES], within, axis=1
                )
                picked = jnp.where(chunk == j, found, picked)
            logit_ref[at, base : base + LANES] = picked
        return carry

    lax.fori_loop(0, z.rows // step, pick, 0, unroll=z.rows == step)
    pack_rows(z, logit_ref, part_ref)


def pack_rows(z, source_ref, target_ref):
    lane = lax.broadcasted_iota(jnp.int32, (z.packed, z.lanes), 1)
    packed = source_ref[pl.ds(0, z.packed), :]
    for h in range(1, z.pack):
        other = pltpu.roll(source_ref[pl.ds(h * z.packed, z.packed), :], h * z.items, 1)
        packed = jnp.where(lane < h * z.items, packed, other)
    target_ref[...] = packed


def index_kernel(z, local_ref, id_ref, index_ref, inside_ref, hot_ref):
    seat_rows(z, index_ref, lambda j: (local_ref, j * z.nrows, z.columns))
    pack_rows(z, local_ref, inside_ref)
    localize = localizer(z)
    lane = lax.broadcasted_iota(jnp.int32, (z.half, LANES), 1)
    for h in range(z.dp):
        at = pl.ds(h * z.half, z.half)
        pos = localize(jnp.broadcast_to(id_ref[at, z.pos_at : z.pos_at + 1], (z.half, LANES)))
        pos = pos.astype(jnp.int32)
        for j in range(z.chunks):
            same = jnp.where(pos == lane + j * LANES, 1.0, 0.0).astype(jnp.bfloat16)
            hot_ref[at, j * LANES : (j + 1) * LANES] = same


def stat_kernel(z, total_ref, inside_ref, exponent_ref, stat_ref):
    step = min(z.packed, 256)
    side = lax.axis_index("dp") & 1

    def one(i, carry):
        at = rows_at(i * step, step)
        logits = total_ref[at, :] * z.scale
        lane = lax.broadcasted_iota(jnp.int32, logits.shape, 1)
        row = lax.broadcasted_iota(jnp.int32, logits.shape, 0) + i * step
        short = lax.broadcasted_iota(jnp.int32, (step, LANES), 1)
        named = inside_ref[at, :] >= 0
        exponents = jnp.zeros(logits.shape, jnp.float32)
        stats = jnp.zeros((step, LANES), jnp.float32)
        for h in range(z.pack):
            mask = named & (lane >= h * z.items) & (lane < (h + 1) * z.items)
            top = jnp.max(jnp.where(mask, logits, LOW), axis=1, keepdims=True)
            exponent = jnp.where(mask, jnp.exp(logits - top), 0.0)
            query = row + h * z.packed
            own = (2 * (query // z.half) + side) * z.own + (query & (z.own - 1)) + h * z.items
            chosen = jnp.where(mask & (lane == own), logits, 0.0)
            values = (
                top,
                jnp.sum(exponent, axis=1, keepdims=True),
                jnp.sum(chosen, axis=1, keepdims=True),
            )
            for k, value in enumerate(values):
                stats = jnp.where(short == 3 * h + k, value, stats)
            exponents = exponents + exponent
        exponent_ref[at, :] = exponents
        stat_ref[:, at] = stats.T[: z.high, :]
        return carry

    lax.fori_loop(0, z.packed // step, one, 0, unroll=z.packed == step)


def split(values):
    parts = []
    for _ in range(3):
        part = values.astype(jnp.bfloat16)
        parts.append(part)
        values = values - part.astype(jnp.float32)
    return parts


def join(tiles):
    n = tiles.shape[0] // 3
    return tiles[:n] + (tiles[n : 2 * n] + tiles[2 * n :])


def place_kernel(z, exponent_ref, index_ref, hot_ref, raw_ref, seat_ref, part_ref, tile_ref):
    def seat(j):
        h, row = divmod(j * z.nrows, z.packed)
        return exponent_ref, row, h * z.items + z.columns

    seat_rows(z, seat_ref, seat)
    for k, part in enumerate(split(seat_ref[...])):
        part_ref[k] = part.astype(jnp.float32)
    high = z.seats * z.chunks
    shape = (high, z.deep)
    tall = lax.broadcasted_iota(jnp.int32, shape, 0).astype(jnp.bfloat16)
    shift = lax.broadcasted_iota(jnp.int32, (1, z.deep), 1) // z.negs * z.chunks
    spread = lax.broadcasted_iota(jnp.int32, (LANES, z.deep), 0).astype(jnp.bfloat16)
    turns = min(32, z.nrows)
    none, unit = jnp.bfloat16(0), jnp.bfloat16(1)

    def place(i, carry):
        for k in range(turns):
            r = i * turns + k
            local = index_ref[pl.ds(r, 1), :]
            chunk = ((local >> 7) + shift).astype(jnp.bfloat16)
            within = (local & (LANES - 1)).astype(jnp.bfloat16)
            here = jnp.broadcast_to(chunk, shape) == tall
            left = [
                jnp.where(
                    here,
                    jnp.broadcast_to(part_ref[p, pl.ds(r, 1), :].astype(jnp.bfloat16), shape), none,
                )
                for p in range(3)
            ]
            right = jnp.where(jnp.broadcast_to(within, (LANES, z.deep)) == spread, unit, none)
            tiles = join(lax.dot_general(
                jnp.concatenate(left, axis=0), right, (((1,), (1,)), ((), ())),
                preferred_element_type=jnp.float32,
            ))
            for j in range(z.seats):
                at = rows_at((j * z.nrows + r) * z.chunks, z.chunks)
                tile_ref[at, :] = tiles[j * z.chunks : (j + 1) * z.chunks, :]
        return carry

    lax.fori_loop(0, z.nrows // turns, place, 0, unroll=z.nrows == turns)
    lane = lax.broadcasted_iota(jnp.int32, (z.run, LANES), 1)
    group = lax.broadcasted_iota(jnp.int32, (z.run, LANES), 0) // z.own
    for n in range(z.sets):
        hot = [hot_ref[pl.ds(h * z.half + n * z.run, z.run), :] for h in range(z.dp)]
        hot = jnp.concatenate(hot, axis=0)
        for u in range(z.side):
            first_row = u * z.half + n * z.run
            side, row = divmod(first_row, z.packed)
            left = []
            for chunk in range(z.deep // LANES):
                if z.joint == 1:
                    part = exponent_ref[pl.ds(row, z.run), chunk * LANES : (chunk + 1) * LANES]
                else:
                    at = chunk * LANES + lane
                    from_lane = side * z.items + at // z.run * z.own + at % z.own
                    part = jnp.take_along_axis(
                        exponent_ref[pl.ds(row, z.run), :LANES], from_lane, axis=1
                    )
                    part = jnp.where(at // z.own % z.joint == group, part, 0.0)
                left.append(part)
            left = jnp.concatenate(split(jnp.concatenate(left, axis=1)), axis=0)
            shared = join(jnp.dot(left, hot, preferred_element_type=jnp.float32))
            for j in range(z.chunks):
                alone = tile_ref[pl.ds(first_row * z.chunks + j, z.run, stride=z.chunks), :]
                raw_ref[pl.ds(first_row, z.run), j * LANES : (j + 1) * LANES] = (
                    alone + shared[:, j * LANES : (j + 1) * LANES]
                )


def weight_kernel(z, *refs):
    count = z.side * z.cuts
    parts, refs = refs[:count], refs[count:]
    raw_ref, hot_ref, own_ref, other_ref = refs[:4]
    dense_refs, (loss_ref, size_ref) = refs[4:6], refs[6:8]
    grad_refs = refs[8 : 8 + z.side]
    stat_ref, row_ref, back_ref, sizes_ref = refs[8 + z.side :]
    d, t, c = places()
    for su in range(z.side):
        for sc in range(z.corpus):
            part = parts[su * z.cuts + sc % z.cuts][pl.ds(sc // z.cuts * z.high, z.high), :]
            stat_ref[((d >> 1) ^ su) * z.corpus + (c ^ z.corpus_order[sc])] = part
    planes = z.side * z.corpus
    row_ref[...] = jnp.zeros_like(row_ref)
    for h in range(z.pack):
        tops = [stat_ref[b, 3 * h : 3 * h + 1, :] for b in range(planes)]
        top = tops[0]
        for other in tops[1:]:
            top = jnp.maximum(top, other)
        total, chosen = jnp.zeros_like(top), jnp.zeros_like(top)
        for b in range(planes):
            total += stat_ref[b, 3 * h + 1 : 3 * h + 2, :] * jnp.exp(tops[b] - top)
            chosen += stat_ref[b, 3 * h + 2 : 3 * h + 3, :]
        mine = stat_ref[(d >> 1) * z.corpus + c, 3 * h : 3 * h + 1, :]
        rest = 1.0 - jnp.exp(chosen - top) / total
        row_ref[h : h + 1, :] = jnp.exp(mine - top) / total
        row_ref[z.pack + h : z.pack + h + 1, :] = jnp.maximum(rest, 2.0**-24)
        row_ref[2 * z.pack + h : 2 * z.pack + h + 1, :] = jnp.log(total) + top - chosen
    back_ref[...] = row_ref[...].T
    mine = (((d >> 1) * z.tensor + t) * z.corpus + c) * z.own
    place = rows_at(mine % z.packed, z.own)
    for k, target_ref in [(1, size_ref), (2, loss_ref)]:
        value = back_ref[place, k * z.pack : k * z.pack + 1]
        for h in range(1, z.pack):
            other = back_ref[place, k * z.pack + h : k * z.pack + h + 1]
            value = jnp.where(mine // z.packed == h, other, value)
        target_ref[...] = jnp.broadcast_to(value, (z.own, LANES))
    step = min(z.packed, 128)
    for h in range(z.pack):

        def one(i, carry):
            row = i * step
            query = h * z.packed + row
            at = rows_at(query, step)
            named = rows_at((2 * (query // z.half) + (d & 1)) * z.half + query % z.half, step)
            ratio = back_ref[rows_at(row, step), h : h + 1]
            weights = raw_ref[at, :] * ratio - hot_ref[named, :].astype(jnp.float32)
            weights = weights.astype(jnp.bfloat16)
            dense_refs[0][at, :] = weights[:, : z.block]
            dense_refs[1][at, :] = weights[:, z.block :]
            size = back_ref[rows_at(row, step), z.pack + h : z.pack + h + 1]
            sizes_ref[at, :] = jnp.broadcast_to(size, (step, LANES))
            return carry

        lax.fori_loop(0, z.packed // step, one, 0, unroll=z.packed == step)
    for s in range(z.side):
        at = rows_at(((d >> 1) ^ s) * z.half, z.half)
        grads = sum(
            jnp.dot(dense_ref[at, :], block_ref[...], preferred_element_type=jnp.float32)
            for dense_ref, block_ref in zip(dense_refs, (own_ref, other_ref))
        )
        grad_refs[s][...] = grads / sizes_ref[at, :1]


def passage_kernel(z, own_ref, query_ref, other_ref, other_query_ref, out_ref):
    def one(i, carry):
        at = rows_at(i * 256, 256)
        grads = [
            lax.dot_general(
                dense_ref[:, at], rows_ref[...], (((0,), (0,)), ((), ())),
                preferred_element_type=jnp.float32,
            )
            for dense_ref, rows_ref in [(own_ref, query_ref), (other_ref, other_query_ref)]
        ]
        out_ref[at, :] = z.scale * (grads[0] + grads[1])
        return carry

    lax.fori_loop(0, z.block // 256, one, 0)


def call(z, kernel, outs, scratch, args, flops, spaces=None, vmem=None):
    spaces = spaces or [pltpu.VMEM] * len(args)
    moved = sum(a.size * a.dtype.itemsize for a in args)
    moved += sum(o.size * jnp.dtype(o.dtype).itemsize for o in outs)
    return pl.pallas_call(
        lambda *refs: kernel(z, *refs),
        out_shape=outs,
        in_specs=[pl.BlockSpec(memory_space=space) for space in spaces],
        out_specs=[pl.BlockSpec(memory_space=pltpu.VMEM)] * len(outs),
        scratch_shapes=scratch,
        compiler_params=pltpu.CompilerParams(vmem_limit_bytes=vmem or z.vmem),
        cost_estimate=pl.CostEstimate(flops=flops, bytes_accessed=moved, transcendentals=0),
    )(*args)


def body(queries, passages, pos_ids, neg_ids):
    z = Sizes(queries, passages, neg_ids)
    f32, bf16, i32 = jnp.float32, jnp.bfloat16, jnp.int32
    shape = jax.ShapeDtypeStruct

    pieces = call(
        z, message_kernel, [shape((z.groups * z.fold, z.message), bf16)],
        [
            pltpu.SMEM(pos_ids.shape, i32), pltpu.VMEM(neg_ids.shape, i32),
            pltpu.VMEM(queries.shape, bf16), pltpu.SemaphoreType.DMA((3,)),
        ],
        [pos_ids, neg_ids, queries], 0, [pltpu.HBM] * 3, 60 * 2**20,
    )
    passages, pieces = lax.optimization_barrier((passages, pieces))
    (own_block,) = call(
        z, fetch_kernel, [shape(passages.shape, bf16)], [pltpu.SemaphoreType.DMA],
        [passages], 0, [pltpu.HBM],
    )
    other_block = swap(passages, "dp", 1)
    chip = lax.all_to_all(pieces[0], ("tensor", "corpus"), split_axis=0, concat_axis=0, tiled=True)
    chip, own_block, other_block = lax.optimization_barrier((chip, own_block, other_block))
    arrived = gather_pairs([chip])
    others = [swap(piece[:, z.message - LANES :], "dp", 1) for piece in arrived]
    blocks = [own_block, other_block]

    work = 2 * z.rows * z.wide * z.width
    query_rows, scores, own_ids, near = call(
        z, score_kernel,
        [shape((z.rows, z.width), bf16), shape((z.rows, z.wide), f32)]
        + [shape((z.rows, LANES), f32)] * 2, [],
        arrived + blocks, work,
    )
    part, local, ids = call(
        z, pick_kernel,
        [
            shape((z.packed, z.lanes), f32), shape((z.rows, z.lanes), i32),
            shape((z.named, LANES), f32),
        ],
        [pltpu.VMEM((z.rows, z.lanes), f32)], others + [scores, own_ids, near], work // 16,
    )
    index, inside, hot = call(
        z, index_kernel,
        [
            shape((z.nrows, z.deep), i32), shape((z.packed, z.lanes), i32),
            shape((z.named, z.wide), bf16),
        ],
        [], [local, ids], work // 64,
    )
    total = sum([swap(part, "tensor", s) for s in z.tensor_order], part)
    exponent, stat = call(
        z, stat_kernel, [shape((z.packed, z.lanes), f32), shape((z.high, z.packed), f32)], [],
        [total, inside], total.size,
    )
    stats = [swap(stat, "corpus", s) if s else stat for s in z.corpus_order]
    (raw,) = call(
        z, place_kernel, [shape((z.rows, z.wide), f32)],
        [
            pltpu.VMEM((z.nrows, z.deep), f32), pltpu.VMEM((3, z.nrows, z.deep), f32),
            pltpu.VMEM((z.rows * z.chunks, LANES), f32),
        ],
        [exponent, index, hot], 3 * work,
    )
    if z.cuts == 1:
        stats = [jnp.concatenate(stats, axis=0)]
    stats = gather_pairs(stats)
    dense, other_dense, loss, size, *grads = call(
        z, weight_kernel,
        [shape((z.rows, z.block), bf16)] * 2 + [shape((z.own, LANES), f32)] * 2
        + [shape((z.half, z.width), f32)] * z.side,
        [
            pltpu.VMEM((z.side * z.corpus, z.high, z.packed), f32),
            pltpu.VMEM((LANES, z.packed), f32), pltpu.VMEM((z.packed, LANES), f32),
            pltpu.VMEM((z.rows, LANES), f32),
        ],
        stats + [raw, hot] + blocks, work,
    )
    half = scatter_pairs(grads).astype(jnp.float16)
    half = half.reshape(z.tensor, z.corpus, z.own, z.width).swapaxes(0, 1)
    half = half.reshape(z.groups, z.own, z.width)
    half = lax.all_to_all(half, ("corpus", "tensor"), split_axis=0, concat_axis=0, tiled=True)
    (grad_pass,) = call(
        z, passage_kernel, [shape((z.block, z.width), f32)], [],
        [dense, query_rows, swap(other_dense, "dp", 1), swap(query_rows, "dp", 1)], work,
    )
    half, grad_pass = lax.optimization_barrier((half, grad_pass))
    half = half.astype(f32).reshape(z.corpus, z.tensor, z.own, z.width).sum(axis=0)
    grad_query = half.swapaxes(0, 1).reshape(z.own, z.feat) * (size[:, :1] * z.scale)
    return (grad_query, loss[:, 0], grad_pass)


def solution(mesh):
    spread = ("dp", "tensor", "corpus")
    in_specs = (P(spread, None), P(("dp", "corpus"), "tensor"), P(spread), P(spread, None))
    out_specs = (P(spread, None), P(spread), P(("dp", "corpus"), "tensor"))
    return jax.shard_map(body, mesh=mesh, in_specs=in_specs, out_specs=out_specs, check_vma=False)
```

```python
import jax
import jax.numpy as jnp
from jax import lax
from jax.experimental import pallas as pl
from jax.experimental.pallas import tpu as pltpu
from jax.sharding import PartitionSpec as P

LANES = 128
FAR = -(2**20)
LOW = -1e30
SUM, ZED = [3, 2, 1], [0, 2, 3, 1]


def swap(value, axis, bit):
    size = lax.axis_size(axis)
    return lax.ppermute(value, axis, [(i, i ^ bit) for i in range(size)])


def gather_pairs(pieces):
    bit = 2
    while bit < lax.axis_size("dp"):
        pieces = pieces + [swap(piece, "dp", bit) for piece in pieces]
        bit *= 2
    return pieces


def scatter_pairs(pieces):
    while len(pieces) > 1:
        n = len(pieces) // 2
        pieces = [
            mine + swap(theirs, "dp", 2 * n) for mine, theirs in zip(pieces[:n], pieces[n:])
        ]
    return pieces[0]


class Sizes:
    def __init__(self, queries, passages, neg_ids):
        self.own, self.feat = queries.shape
        self.block, self.width = passages.shape
        self.negs = neg_ids.shape[1]
        self.dp = lax.axis_size("dp")
        self.tensor = lax.axis_size("tensor")
        self.corpus = lax.axis_size("corpus")
        self.side = self.dp // 2
        self.groups = self.tensor * self.corpus
        self.half = self.groups * self.own
        self.rows = self.side * self.half
        self.named = self.dp * self.half
        self.columns = self.dp * self.own
        self.items = self.columns + self.negs
        self.lanes = -(-self.items // LANES) * LANES
        self.pack = max(1, LANES // self.items)
        self.packed = self.rows // self.pack
        self.neg_at = self.columns % LANES
        self.pos_at = 0 if self.neg_at else self.negs
        self.wide = 2 * self.block
        self.chunks = self.wide // LANES
        self.scale = self.feat ** (-0.5)
        self.tensor_order = SUM if self.tensor == 4 else list(range(1, self.tensor))
        self.corpus_order = ZED if self.corpus == 4 else list(range(self.corpus))
        self.cuts = self.corpus if self.side == 1 else 1
        self.deep = 2 * LANES
        self.seats = self.deep // self.negs
        self.nrows = self.rows // self.seats
        self.joint = max(1, self.deep // self.columns)
        self.run = self.joint * self.own
        self.sets = self.groups // self.joint
        self.high = -(-3 * self.pack // 8) * 8
        self.dense_ids = self.block * self.dp * self.corpus <= 2**13 and self.own == 16
        self.fold = self.own // 2 if self.dense_ids else self.own
        self.message = 2 * self.width + LANES if self.dense_ids else self.width + LANES
        self.vmem = min(61, 20 + 20 * self.rows // 1024) * 2**20


def places():
    return [lax.axis_index(axis) for axis in ("dp", "tensor", "corpus")]


def rows_at(start, size):
    return pl.ds(pl.multiple_of(start, size), size)


def message_kernel(z, pos_in, neg_in, query_in, out_ref, pos_ref, neg_ref, query_ref, sems):
    moves = [
        pltpu.make_async_copy(source, target, sems.at[i])
        for i, (source, target) in enumerate(
            [(pos_in, pos_ref), (neg_in, neg_ref), (query_in, query_ref)]
        )
    ]
    for move in moves:
        move.start()
    for move in moves:
        move.wait()
    half = LANES // 2
    row = lax.broadcasted_iota(jnp.int32, (z.own, half), 0)
    pos = jnp.zeros((z.own, half), jnp.int32)
    for i in range(z.own):
        pos = jnp.where(row == i, pos_ref[i], pos)
    ids = [neg_ref[...], pos[:, : half - z.neg_at - z.negs]]
    ids = jnp.concatenate([part for part in [pos[:, : z.neg_at]] + ids if part.shape[1]], axis=1)
    if z.dense_ids:
        code = 1.0 + (ids & 127).astype(jnp.float32) / 128.0
        for bit in range(6):
            code = jnp.where((ids >> (7 + bit)) & 1 == 1, code * 2.0 ** (1 << bit), code)
        code = code * 2.0**-32
        code = jnp.concatenate([code[: z.fold], code[z.fold :]], axis=1)
        for t in range(z.tensor):
            rows = query_ref[:, t * z.width : (t + 1) * z.width].astype(jnp.float32)
            rows = jnp.concatenate([rows[: z.fold], rows[z.fold :], code], axis=1)
            rows = jnp.concatenate([rows, rows], axis=0).astype(jnp.bfloat16)
            for c in range(0, z.corpus, 2):
                out_ref[pl.ds((t * z.corpus + c) * z.fold, z.own), :] = rows
        return
    ids = jnp.concatenate([ids >> 8, ids & 255], axis=1)
    code = ids.astype(jnp.float32).astype(jnp.bfloat16)
    for k in range(z.groups):
        t = k // z.corpus
        at = pl.ds(k * z.own, z.own)
        out_ref[at, : z.width] = query_ref[:, t * z.width : (t + 1) * z.width]
        out_ref[at, z.width :] = code


def unfold(z, first, second):
    width = first.shape[-1]
    pair = [part.reshape(z.groups, z.fold, width) for part in (first, second)]
    return jnp.concatenate(pair, axis=1).reshape(z.half, width)


def decode(z, code):
    code = code.astype(jnp.float32)
    if not z.dense_ids:
        return code * 256.0 + pltpu.roll(code, LANES // 2, 1)
    code = code * 2.0**32
    high = jnp.zeros_like(code)
    for bit in range(5, -1, -1):
        big = code >= 2.0 ** (1 << bit)
        high = jnp.where(big, high + float(128 << bit), high)
        code = jnp.where(big, code * 2.0 ** -(1 << bit), code)
    ids = high + (code - 1.0) * 128.0
    return unfold(z, ids, pltpu.roll(ids, LANES // 2, 1))


def fetch_kernel(z, block_ref, passage_ref, sem):
    fetch = pltpu.make_async_copy(block_ref, passage_ref, sem)
    fetch.start()
    fetch.wait()


def seat_rows(z, out_ref, source):
    lane = lax.broadcasted_iota(jnp.int32, (z.nrows, LANES), 1)
    per = LANES // z.negs
    for chunk in range(z.deep // LANES):
        packed = None
        for k in range(per):
            ref, row, at = source(chunk * per + k)
            base = at // LANES * LANES
            piece = ref[pl.ds(row, z.nrows), base : base + LANES]
            turn = (k * z.negs - at) % LANES
            piece = pltpu.roll(piece, turn, 1) if turn else piece
            packed = piece if packed is None else jnp.where(lane < k * z.negs, packed, piece)
        out_ref[:, chunk * LANES : (chunk + 1) * LANES] = packed


def score_kernel(z, *refs):
    arrived, block_refs = refs[: z.side], refs[z.side : z.side + 2]
    query_ref, score_ref, own_ref, near_ref = refs[z.side + 2 :]
    d = lax.axis_index("dp")
    localize = localizer(z)
    for su in range(z.side):
        at = rows_at(((d ^ (2 * su)) >> 1) * z.half, z.half)
        rows = arrived[su][:, : z.message - LANES]
        if z.dense_ids:
            rows = rows.astype(jnp.float32)
            rows = unfold(z, rows[:, : z.width], rows[:, z.width :]).astype(jnp.bfloat16)
        query_ref[at, :] = rows
        ids = decode(z, arrived[su][:, z.message - LANES :])
        own_ref[at, :] = ids
        near_ref[at, :] = localize(ids)
    step = min(z.rows, 256)

    def score(i, carry):
        at = rows_at(i * step, step)
        for side, block_ref in enumerate(block_refs):
            score_ref[at, side * z.block : (side + 1) * z.block] = lax.dot_general(
                query_ref[at, :], block_ref[...], (((1,), (1,)), ((), ())),
                preferred_element_type=jnp.float32,
            )
        return carry

    lax.fori_loop(0, z.rows // step, score, 0, unroll=z.rows == step)


def localizer(z):
    d, _, c = places()

    def localize(ids):
        found = jnp.full(ids.shape, float(FAR), jnp.float32)
        for side in range(2):
            local = ids - (((d ^ side) * z.corpus + c) * z.block).astype(jnp.float32)
            inside = (local >= 0.0) & (local < float(z.block))
            found = jnp.where(inside, local + float(side * z.block), found)
        return found

    return localize


def pick_kernel(z, *refs):
    others, (score_ref, own_ref, near_ref) = refs[: z.side], refs[z.side : z.side + 3]
    part_ref, local_ref, id_ref, logit_ref = refs[z.side + 3 :]
    d = lax.axis_index("dp")
    for su in range(z.side):
        from_d = d ^ (2 * su)
        own = own_ref[rows_at((from_d >> 1) * z.half, z.half), :]
        id_ref[rows_at(from_d * z.half, z.half), :] = own
        id_ref[rows_at((from_d ^ 1) * z.half, z.half), :] = decode(z, others[su][...])
    wide = -(-z.columns // LANES) * LANES
    row = lax.broadcasted_iota(jnp.int32, (z.half, wide), 0) & (z.own - 1)
    col = lax.broadcasted_iota(jnp.int32, (z.half, wide), 1)
    group_ids = jnp.zeros((z.groups, wide), jnp.float32)
    for h in range(z.dp):
        at = pl.ds(h * z.half, z.half)
        pos = jnp.broadcast_to(id_ref[at, z.pos_at : z.pos_at + 1], (z.half, wide))
        kept = jnp.where(col == row + h * z.own, pos, 0.0)
        group_ids += jnp.sum(kept.reshape(z.groups, z.own, wide), axis=1)
    batch = jnp.broadcast_to(localizer(z)(group_ids)[:, None, :], (z.groups, z.own, wide))
    batch = batch.reshape(z.half, wide)
    lane = lax.broadcasted_iota(jnp.int32, (z.half, LANES), 1)
    for u in range(z.side):
        near = near_ref[pl.ds(u * z.half, z.half), :]
        for base in range(0, z.lanes, LANES):
            local = near
            if base < z.columns:
                local = jnp.where(lane + base < z.columns, batch[:, base : base + LANES], near)
            local = jnp.where(lane + base < z.items, local, float(FAR))
            local_ref[pl.ds(u * z.half, z.half), base : base + LANES] = local.astype(jnp.int32)
    step = min(z.rows, 256)

    def pick(i, carry):
        at = rows_at(i * step, step)
        for base in range(0, z.lanes, LANES):
            local = local_ref[at, base : base + LANES]
            chunk, within = local >> 7, local & (LANES - 1)
            picked = jnp.zeros((step, LANES), jnp.float32)
            for j in range(z.chunks):
                found = jnp.take_along_axis(
                    score_ref[at, j * LANES : (j + 1) * LANES], within, axis=1
                )
                picked = jnp.where(chunk == j, found, picked)
            logit_ref[at, base : base + LANES] = picked
        return carry

    lax.fori_loop(0, z.rows // step, pick, 0, unroll=z.rows == step)
    pack_rows(z, logit_ref, part_ref)


def pack_rows(z, source_ref, target_ref):
    lane = lax.broadcasted_iota(jnp.int32, (z.packed, z.lanes), 1)
    packed = source_ref[pl.ds(0, z.packed), :]
    for h in range(1, z.pack):
        other = pltpu.roll(source_ref[pl.ds(h * z.packed, z.packed), :], h * z.items, 1)
        packed = jnp.where(lane < h * z.items, packed, other)
    target_ref[...] = packed


def index_kernel(z, local_ref, id_ref, index_ref, inside_ref, hot_ref):
    seat_rows(z, index_ref, lambda j: (local_ref, j * z.nrows, z.columns))
    pack_rows(z, local_ref, inside_ref)
    localize = localizer(z)
    lane = lax.broadcasted_iota(jnp.int32, (z.half, LANES), 1)
    for h in range(z.dp):
        at = pl.ds(h * z.half, z.half)
        pos = localize(jnp.broadcast_to(id_ref[at, z.pos_at : z.pos_at + 1], (z.half, LANES)))
        pos = pos.astype(jnp.int32)
        for j in range(z.chunks):
            same = jnp.where(pos == lane + j * LANES, 1.0, 0.0).astype(jnp.bfloat16)
            hot_ref[at, j * LANES : (j + 1) * LANES] = same


def stat_kernel(z, total_ref, inside_ref, exponent_ref, stat_ref):
    step = min(z.packed, 256)
    side = lax.axis_index("dp") & 1

    def one(i, carry):
        at = rows_at(i * step, step)
        logits = total_ref[at, :] * z.scale
        lane = lax.broadcasted_iota(jnp.int32, logits.shape, 1)
        row = lax.broadcasted_iota(jnp.int32, logits.shape, 0) + i * step
        short = lax.broadcasted_iota(jnp.int32, (step, LANES), 1)
        named = inside_ref[at, :] >= 0
        exponents = jnp.zeros(logits.shape, jnp.float32)
        stats = jnp.zeros((step, LANES), jnp.float32)
        for h in range(z.pack):
            mask = named & (lane >= h * z.items) & (lane < (h + 1) * z.items)
            top = jnp.max(jnp.where(mask, logits, LOW), axis=1, keepdims=True)
            exponent = jnp.where(mask, jnp.exp(logits - top), 0.0)
            query = row + h * z.packed
            own = (2 * (query // z.half) + side) * z.own + (query & (z.own - 1)) + h * z.items
            chosen = jnp.where(mask & (lane == own), logits, 0.0)
            values = (
                top,
                jnp.sum(exponent, axis=1, keepdims=True),
                jnp.sum(chosen, axis=1, keepdims=True),
            )
            for k, value in enumerate(values):
                stats = jnp.where(short == 3 * h + k, value, stats)
            exponents = exponents + exponent
        exponent_ref[at, :] = exponents
        stat_ref[:, at] = stats.T[: z.high, :]
        return carry

    lax.fori_loop(0, z.packed // step, one, 0, unroll=z.packed == step)


def split(values):
    parts = []
    for _ in range(3):
        part = values.astype(jnp.bfloat16)
        parts.append(part)
        values = values - part.astype(jnp.float32)
    return parts


def join(tiles):
    n = tiles.shape[0] // 3
    return tiles[:n] + (tiles[n : 2 * n] + tiles[2 * n :])


def place_kernel(z, exponent_ref, index_ref, hot_ref, raw_ref, seat_ref, part_ref, tile_ref):
    def seat(j):
        h, row = divmod(j * z.nrows, z.packed)
        return exponent_ref, row, h * z.items + z.columns

    seat_rows(z, seat_ref, seat)
    for k, part in enumerate(split(seat_ref[...])):
        part_ref[k] = part.astype(jnp.float32)
    high = z.seats * z.chunks
    shape = (high, z.deep)
    tall = lax.broadcasted_iota(jnp.int32, shape, 0).astype(jnp.bfloat16)
    shift = lax.broadcasted_iota(jnp.int32, (1, z.deep), 1) // z.negs * z.chunks
    spread = lax.broadcasted_iota(jnp.int32, (LANES, z.deep), 0).astype(jnp.bfloat16)
    turns = min(32, z.nrows)
    none, unit = jnp.bfloat16(0), jnp.bfloat16(1)

    def place(i, carry):
        for k in range(turns):
            r = i * turns + k
            local = index_ref[pl.ds(r, 1), :]
            chunk = ((local >> 7) + shift).astype(jnp.bfloat16)
            within = (local & (LANES - 1)).astype(jnp.bfloat16)
            here = jnp.broadcast_to(chunk, shape) == tall
            left = [
                jnp.where(
                    here,
                    jnp.broadcast_to(part_ref[p, pl.ds(r, 1), :].astype(jnp.bfloat16), shape), none,
                )
                for p in range(3)
            ]
            right = jnp.where(jnp.broadcast_to(within, (LANES, z.deep)) == spread, unit, none)
            tiles = join(lax.dot_general(
                jnp.concatenate(left, axis=0), right, (((1,), (1,)), ((), ())),
                preferred_element_type=jnp.float32,
            ))
            for j in range(z.seats):
                at = rows_at((j * z.nrows + r) * z.chunks, z.chunks)
                tile_ref[at, :] = tiles[j * z.chunks : (j + 1) * z.chunks, :]
        return carry

    lax.fori_loop(0, z.nrows // turns, place, 0, unroll=z.nrows == turns)
    lane = lax.broadcasted_iota(jnp.int32, (z.run, LANES), 1)
    group = lax.broadcasted_iota(jnp.int32, (z.run, LANES), 0) // z.own
    for n in range(z.sets):
        hot = [hot_ref[pl.ds(h * z.half + n * z.run, z.run), :] for h in range(z.dp)]
        hot = jnp.concatenate(hot, axis=0)
        for u in range(z.side):
            first_row = u * z.half + n * z.run
            side, row = divmod(first_row, z.packed)
            left = []
            for chunk in range(z.deep // LANES):
                if z.joint == 1:
                    part = exponent_ref[pl.ds(row, z.run), chunk * LANES : (chunk + 1) * LANES]
                else:
                    at = chunk * LANES + lane
                    from_lane = side * z.items + at // z.run * z.own + at % z.own
                    part = jnp.take_along_axis(
                        exponent_ref[pl.ds(row, z.run), :LANES], from_lane, axis=1
                    )
                    part = jnp.where(at // z.own % z.joint == group, part, 0.0)
                left.append(part)
            left = jnp.concatenate(split(jnp.concatenate(left, axis=1)), axis=0)
            shared = join(jnp.dot(left, hot, preferred_element_type=jnp.float32))
            for j in range(z.chunks):
                alone = tile_ref[pl.ds(first_row * z.chunks + j, z.run, stride=z.chunks), :]
                raw_ref[pl.ds(first_row, z.run), j * LANES : (j + 1) * LANES] = (
                    alone + shared[:, j * LANES : (j + 1) * LANES]
                )


def weight_kernel(z, *refs):
    count = z.side * z.cuts
    parts, refs = refs[:count], refs[count:]
    raw_ref, hot_ref, own_ref, other_ref = refs[:4]
    dense_refs, (loss_ref, size_ref) = refs[4:6], refs[6:8]
    grad_refs = refs[8 : 8 + z.side]
    stat_ref, row_ref, back_ref, sizes_ref = refs[8 + z.side :]
    d, t, c = places()
    for su in range(z.side):
        for sc in range(z.corpus):
            part = parts[su * z.cuts + sc % z.cuts][pl.ds(sc // z.cuts * z.high, z.high), :]
            stat_ref[((d >> 1) ^ su) * z.corpus + (c ^ z.corpus_order[sc])] = part
    planes = z.side * z.corpus
    row_ref[...] = jnp.zeros_like(row_ref)
    for h in range(z.pack):
        tops = [stat_ref[b, 3 * h : 3 * h + 1, :] for b in range(planes)]
        top = tops[0]
        for other in tops[1:]:
            top = jnp.maximum(top, other)
        total, chosen = jnp.zeros_like(top), jnp.zeros_like(top)
        for b in range(planes):
            total += stat_ref[b, 3 * h + 1 : 3 * h + 2, :] * jnp.exp(tops[b] - top)
            chosen += stat_ref[b, 3 * h + 2 : 3 * h + 3, :]
        mine = stat_ref[(d >> 1) * z.corpus + c, 3 * h : 3 * h + 1, :]
        rest = 1.0 - jnp.exp(chosen - top) / total
        row_ref[h : h + 1, :] = jnp.exp(mine - top) / total
        row_ref[z.pack + h : z.pack + h + 1, :] = jnp.maximum(rest, 2.0**-24)
        row_ref[2 * z.pack + h : 2 * z.pack + h + 1, :] = jnp.log(total) + top - chosen
    back_ref[...] = row_ref[...].T
    mine = (((d >> 1) * z.tensor + t) * z.corpus + c) * z.own
    place = rows_at(mine % z.packed, z.own)
    for k, target_ref in [(1, size_ref), (2, loss_ref)]:
        value = back_ref[place, k * z.pack : k * z.pack + 1]
        for h in range(1, z.pack):
            other = back_ref[place, k * z.pack + h : k * z.pack + h + 1]
            value = jnp.where(mine // z.packed == h, other, value)
        target_ref[...] = jnp.broadcast_to(value, (z.own, LANES))
    step = min(z.packed, 128)
    for h in range(z.pack):

        def one(i, carry):
            row = i * step
            query = h * z.packed + row
            at = rows_at(query, step)
            named = rows_at((2 * (query // z.half) + (d & 1)) * z.half + query % z.half, step)
            ratio = back_ref[rows_at(row, step), h : h + 1]
            weights = raw_ref[at, :] * ratio - hot_ref[named, :].astype(jnp.float32)
            weights = weights.astype(jnp.bfloat16)
            dense_refs[0][at, :] = weights[:, : z.block]
            dense_refs[1][at, :] = weights[:, z.block :]
            size = back_ref[rows_at(row, step), z.pack + h : z.pack + h + 1]
            sizes_ref[at, :] = jnp.broadcast_to(size, (step, LANES))
            return carry

        lax.fori_loop(0, z.packed // step, one, 0, unroll=z.packed == step)
    for s in range(z.side):
        at = rows_at(((d >> 1) ^ s) * z.half, z.half)
        grads = sum(
            jnp.dot(dense_ref[at, :], block_ref[...], preferred_element_type=jnp.float32)
            for dense_ref, block_ref in zip(dense_refs, (own_ref, other_ref))
        )
        grad_refs[s][...] = grads / sizes_ref[at, :1]


def passage_kernel(z, own_ref, query_ref, other_ref, other_query_ref, out_ref):
    def one(i, carry):
        at = rows_at(i * 256, 256)
        grads = [
            lax.dot_general(
                dense_ref[:, at], rows_ref[...], (((0,), (0,)), ((), ())),
                preferred_element_type=jnp.float32,
            )
            for dense_ref, rows_ref in [(own_ref, query_ref), (other_ref, other_query_ref)]
        ]
        out_ref[at, :] = z.scale * (grads[0] + grads[1])
        return carry

    lax.fori_loop(0, z.block // 256, one, 0)


def call(z, kernel, outs, scratch, args, flops, spaces=None, vmem=None):
    spaces = spaces or [pltpu.VMEM] * len(args)
    moved = sum(a.size * a.dtype.itemsize for a in args)
    moved += sum(o.size * jnp.dtype(o.dtype).itemsize for o in outs)
    return pl.pallas_call(
        lambda *refs: kernel(z, *refs),
        out_shape=outs,
        in_specs=[pl.BlockSpec(memory_space=space) for space in spaces],
        out_specs=[pl.BlockSpec(memory_space=pltpu.VMEM)] * len(outs),
        scratch_shapes=scratch,
        compiler_params=pltpu.CompilerParams(vmem_limit_bytes=vmem or z.vmem),
        cost_estimate=pl.CostEstimate(flops=flops, bytes_accessed=moved, transcendentals=0),
    )(*args)


def body(queries, passages, pos_ids, neg_ids):
    z = Sizes(queries, passages, neg_ids)
    f32, bf16, i32 = jnp.float32, jnp.bfloat16, jnp.int32
    shape = jax.ShapeDtypeStruct

    pieces = call(
        z, message_kernel, [shape((z.groups * z.fold, z.message), bf16)],
        [
            pltpu.SMEM(pos_ids.shape, i32), pltpu.VMEM(neg_ids.shape, i32),
            pltpu.VMEM(queries.shape, bf16), pltpu.SemaphoreType.DMA((3,)),
        ],
        [pos_ids, neg_ids, queries], 0, [pltpu.HBM] * 3, 60 * 2**20,
    )
    passages, pieces = lax.optimization_barrier((passages, pieces))
    (own_block,) = call(
        z, fetch_kernel, [shape(passages.shape, bf16)], [pltpu.SemaphoreType.DMA],
        [passages], 0, [pltpu.HBM],
    )
    other_block = swap(passages, "dp", 1)
    chip = lax.all_to_all(pieces[0], ("tensor", "corpus"), split_axis=0, concat_axis=0, tiled=True)
    chip, own_block, other_block = lax.optimization_barrier((chip, own_block, other_block))
    arrived = gather_pairs([chip])
    others = [swap(piece[:, z.message - LANES :], "dp", 1) for piece in arrived]
    blocks = [own_block, other_block]

    work = 2 * z.rows * z.wide * z.width
    query_rows, scores, own_ids, near = call(
        z, score_kernel,
        [shape((z.rows, z.width), bf16), shape((z.rows, z.wide), f32)]
        + [shape((z.rows, LANES), f32)] * 2, [],
        arrived + blocks, work,
    )
    part, local, ids = call(
        z, pick_kernel,
        [
            shape((z.packed, z.lanes), f32), shape((z.rows, z.lanes), i32),
            shape((z.named, LANES), f32),
        ],
        [pltpu.VMEM((z.rows, z.lanes), f32)], others + [scores, own_ids, near], work // 16,
    )
    index, inside, hot = call(
        z, index_kernel,
        [
            shape((z.nrows, z.deep), i32), shape((z.packed, z.lanes), i32),
            shape((z.named, z.wide), bf16),
        ],
        [], [local, ids], work // 64,
    )
    total = sum([swap(part, "tensor", s) for s in z.tensor_order], part)
    exponent, stat = call(
        z, stat_kernel, [shape((z.packed, z.lanes), f32), shape((z.high, z.packed), f32)], [],
        [total, inside], total.size,
    )
    stats = [swap(stat, "corpus", s) if s else stat for s in z.corpus_order]
    (raw,) = call(
        z, place_kernel, [shape((z.rows, z.wide), f32)],
        [
            pltpu.VMEM((z.nrows, z.deep), f32), pltpu.VMEM((3, z.nrows, z.deep), f32),
            pltpu.VMEM(((z.rows + 1) * z.chunks, LANES), f32),
        ],
        [exponent, index, hot], 3 * work,
    )
    if z.cuts == 1:
        stats = [jnp.concatenate(stats, axis=0)]
    stats = gather_pairs(stats)
    dense, other_dense, loss, size, *grads = call(
        z, weight_kernel,
        [shape((z.rows, z.block), bf16)] * 2 + [shape((z.own, LANES), f32)] * 2
        + [shape((z.half, z.width), f32)] * z.side,
        [
            pltpu.VMEM((z.side * z.corpus, z.high, z.packed), f32),
            pltpu.VMEM((LANES, z.packed), f32), pltpu.VMEM((z.packed, LANES), f32),
            pltpu.VMEM((z.rows, LANES), f32),
        ],
        stats + [raw, hot] + blocks, work,
    )
    half = scatter_pairs(grads).astype(jnp.float16)
    half = half.reshape(z.tensor, z.corpus, z.own, z.width).swapaxes(0, 1)
    half = half.reshape(z.groups, z.own, z.width)
    half, other_dense = lax.optimization_barrier((half, other_dense))
    half = lax.all_to_all(half, ("corpus", "tensor"), split_axis=0, concat_axis=0, tiled=True)
    (grad_pass,) = call(
        z, passage_kernel, [shape((z.block, z.width), f32)], [],
        [dense, query_rows, swap(other_dense, "dp", 1), swap(query_rows, "dp", 1)], work,
    )
    half, grad_pass = lax.optimization_barrier((half, grad_pass))
    half = half.astype(f32).reshape(z.corpus, z.tensor, z.own, z.width).sum(axis=0)
    grad_query = half.swapaxes(0, 1).reshape(z.own, z.feat) * (size[:, :1] * z.scale)
    return (grad_query, loss[:, 0], grad_pass)


def solution(mesh):
    spread = ("dp", "tensor", "corpus")
    in_specs = (P(spread, None), P(("dp", "corpus"), "tensor"), P(spread), P(spread, None))
    out_specs = (P(spread, None), P(spread), P(("dp", "corpus"), "tensor"))
    return jax.shard_map(body, mesh=mesh, in_specs=in_specs, out_specs=out_specs, check_vma=False)
```

```python
import jax
import jax.numpy as jnp
from jax import lax
from jax.experimental import pallas as pl
from jax.experimental.pallas import tpu as pltpu
from jax.sharding import PartitionSpec as P

LANES = 128
FAR = -(2**20)
LOW = -1e30
SUM, ZED = [3, 2, 1], [0, 2, 3, 1]


def swap(value, axis, bit):
    size = lax.axis_size(axis)
    return lax.ppermute(value, axis, [(i, i ^ bit) for i in range(size)])


def gather_pairs(pieces):
    bit = 2
    while bit < lax.axis_size("dp"):
        pieces = pieces + [swap(piece, "dp", bit) for piece in pieces]
        bit *= 2
    return pieces


def scatter_pairs(pieces):
    while len(pieces) > 1:
        n = len(pieces) // 2
        pieces = [
            mine + swap(theirs, "dp", 2 * n) for mine, theirs in zip(pieces[:n], pieces[n:])
        ]
    return pieces[0]


class Sizes:
    def __init__(self, queries, passages, neg_ids):
        self.own, self.feat = queries.shape
        self.block, self.width = passages.shape
        self.negs = neg_ids.shape[1]
        self.dp = lax.axis_size("dp")
        self.tensor = lax.axis_size("tensor")
        self.corpus = lax.axis_size("corpus")
        self.side = self.dp // 2
        self.groups = self.tensor * self.corpus
        self.half = self.groups * self.own
        self.rows = self.side * self.half
        self.named = self.dp * self.half
        self.columns = self.dp * self.own
        self.items = self.columns + self.negs
        self.lanes = -(-self.items // LANES) * LANES
        self.pack = max(1, LANES // self.items)
        self.packed = self.rows // self.pack
        self.neg_at = self.columns % LANES
        self.pos_at = 0 if self.neg_at else self.negs
        self.wide = 2 * self.block
        self.chunks = self.wide // LANES
        self.scale = self.feat ** (-0.5)
        self.tensor_order = SUM if self.tensor == 4 else list(range(1, self.tensor))
        self.corpus_order = ZED if self.corpus == 4 else list(range(self.corpus))
        self.cuts = self.corpus if self.side == 1 else 1
        self.deep = 2 * LANES
        self.seats = self.deep // self.negs
        self.nrows = self.rows // self.seats
        self.joint = max(1, self.deep // self.columns)
        self.run = self.joint * self.own
        self.sets = self.groups // self.joint
        self.high = -(-3 * self.pack // 8) * 8
        self.dense_ids = self.block * self.dp * self.corpus <= 2**13 and self.own == 16
        self.fold = self.own // 2 if self.dense_ids else self.own
        self.message = 2 * self.width + LANES if self.dense_ids else self.width + LANES
        self.vmem = min(61, 20 + 20 * self.rows // 1024) * 2**20


def places():
    return [lax.axis_index(axis) for axis in ("dp", "tensor", "corpus")]


def rows_at(start, size):
    return pl.ds(pl.multiple_of(start, size), size)


def message_kernel(z, pos_in, neg_in, query_in, out_ref, pos_ref, neg_ref, query_ref, sems):
    moves = [
        pltpu.make_async_copy(source, target, sems.at[i])
        for i, (source, target) in enumerate(
            [(pos_in, pos_ref), (neg_in, neg_ref), (query_in, query_ref)]
        )
    ]
    for move in moves:
        move.start()
    for move in moves:
        move.wait()
    half = LANES // 2
    row = lax.broadcasted_iota(jnp.int32, (z.own, half), 0)
    pos = jnp.zeros((z.own, half), jnp.int32)
    for i in range(z.own):
        pos = jnp.where(row == i, pos_ref[i], pos)
    ids = [neg_ref[...], pos[:, : half - z.neg_at - z.negs]]
    ids = jnp.concatenate([part for part in [pos[:, : z.neg_at]] + ids if part.shape[1]], axis=1)
    if z.dense_ids:
        code = 1.0 + (ids & 127).astype(jnp.float32) / 128.0
        for bit in range(6):
            code = jnp.where((ids >> (7 + bit)) & 1 == 1, code * 2.0 ** (1 << bit), code)
        code = code * 2.0**-32
        code = jnp.concatenate([code[: z.fold], code[z.fold :]], axis=1)
        for t in range(z.tensor):
            rows = query_ref[:, t * z.width : (t + 1) * z.width].astype(jnp.float32)
            rows = jnp.concatenate([rows[: z.fold], rows[z.fold :], code], axis=1)
            rows = jnp.concatenate([rows, rows], axis=0).astype(jnp.bfloat16)
            for c in range(0, z.corpus, 2):
                k = (t * z.corpus + c + z.groups // 2) % z.groups
                out_ref[pl.ds(k * z.fold, z.own), :] = rows
        return
    ids = jnp.concatenate([ids >> 8, ids & 255], axis=1)
    code = ids.astype(jnp.float32).astype(jnp.bfloat16)
    for k in range(z.groups):
        t = (k + z.groups // 2) % z.groups // z.corpus
        at = pl.ds(k * z.own, z.own)
        out_ref[at, : z.width] = query_ref[:, t * z.width : (t + 1) * z.width]
        out_ref[at, z.width :] = code


def unfold(z, first, second):
    width = first.shape[-1]
    pair = [part.reshape(z.groups, z.fold, width) for part in (first, second)]
    return jnp.concatenate(pair, axis=1).reshape(z.half, width)


def decode(z, code):
    code = code.astype(jnp.float32)
    if not z.dense_ids:
        return code * 256.0 + pltpu.roll(code, LANES // 2, 1)
    code = code * 2.0**32
    high = jnp.zeros_like(code)
    for bit in range(5, -1, -1):
        big = code >= 2.0 ** (1 << bit)
        high = jnp.where(big, high + float(128 << bit), high)
        code = jnp.where(big, code * 2.0 ** -(1 << bit), code)
    ids = high + (code - 1.0) * 128.0
    return unfold(z, ids, pltpu.roll(ids, LANES // 2, 1))


def fetch_kernel(z, block_ref, passage_ref, sem):
    fetch = pltpu.make_async_copy(block_ref, passage_ref, sem)
    fetch.start()
    fetch.wait()


def seat_rows(z, out_ref, source):
    lane = lax.broadcasted_iota(jnp.int32, (z.nrows, LANES), 1)
    per = LANES // z.negs
    for chunk in range(z.deep // LANES):
        packed = None
        for k in range(per):
            ref, row, at = source(chunk * per + k)
            base = at // LANES * LANES
            piece = ref[pl.ds(row, z.nrows), base : base + LANES]
            turn = (k * z.negs - at) % LANES
            piece = pltpu.roll(piece, turn, 1) if turn else piece
            packed = piece if packed is None else jnp.where(lane < k * z.negs, packed, piece)
        out_ref[:, chunk * LANES : (chunk + 1) * LANES] = packed


def score_kernel(z, *refs):
    arrived, block_refs = refs[: z.side], refs[z.side : z.side + 2]
    query_ref, score_ref, own_ref, near_ref = refs[z.side + 2 :]
    d = lax.axis_index("dp")
    localize = localizer(z)
    for su in range(z.side):
        at = rows_at(((d ^ (2 * su)) >> 1) * z.half, z.half)
        rows = arrived[su][:, : z.message - LANES]
        if z.dense_ids:
            rows = rows.astype(jnp.float32)
            rows = unfold(z, rows[:, : z.width], rows[:, z.width :]).astype(jnp.bfloat16)
        query_ref[at, :] = rows
        ids = decode(z, arrived[su][:, z.message - LANES :])
        own_ref[at, :] = ids
        near_ref[at, :] = localize(ids)
    step = min(z.rows, 256)

    def score(i, carry):
        at = rows_at(i * step, step)
        for side, block_ref in enumerate(block_refs):
            score_ref[at, side * z.block : (side + 1) * z.block] = lax.dot_general(
                query_ref[at, :], block_ref[...], (((1,), (1,)), ((), ())),
                preferred_element_type=jnp.float32,
            )
        return carry

    lax.fori_loop(0, z.rows // step, score, 0, unroll=z.rows == step)


def localizer(z):
    d, _, c = places()

    def localize(ids):
        found = jnp.full(ids.shape, float(FAR), jnp.float32)
        for side in range(2):
            local = ids - (((d ^ side) * z.corpus + c) * z.block).astype(jnp.float32)
            inside = (local >= 0.0) & (local < float(z.block))
            found = jnp.where(inside, local + float(side * z.block), found)
        return found

    return localize


def pick_kernel(z, *refs):
    others, (score_ref, own_ref, near_ref) = refs[: z.side], refs[z.side : z.side + 3]
    part_ref, local_ref, id_ref, logit_ref = refs[z.side + 3 :]
    d = lax.axis_index("dp")
    for su in range(z.side):
        from_d = d ^ (2 * su)
        own = own_ref[rows_at((from_d >> 1) * z.half, z.half), :]
        id_ref[rows_at(from_d * z.half, z.half), :] = own
        id_ref[rows_at((from_d ^ 1) * z.half, z.half), :] = decode(z, others[su][...])
    wide = -(-z.columns // LANES) * LANES
    row = lax.broadcasted_iota(jnp.int32, (z.half, wide), 0) & (z.own - 1)
    col = lax.broadcasted_iota(jnp.int32, (z.half, wide), 1)
    group_ids = jnp.zeros((z.groups, wide), jnp.float32)
    for h in range(z.dp):
        at = pl.ds(h * z.half, z.half)
        pos = jnp.broadcast_to(id_ref[at, z.pos_at : z.pos_at + 1], (z.half, wide))
        kept = jnp.where(col == row + h * z.own, pos, 0.0)
        group_ids += jnp.sum(kept.reshape(z.groups, z.own, wide), axis=1)
    batch = jnp.broadcast_to(localizer(z)(group_ids)[:, None, :], (z.groups, z.own, wide))
    batch = batch.reshape(z.half, wide)
    lane = lax.broadcasted_iota(jnp.int32, (z.half, LANES), 1)
    for u in range(z.side):
        near = near_ref[pl.ds(u * z.half, z.half), :]
        for base in range(0, z.lanes, LANES):
            local = near
            if base < z.columns:
                local = jnp.where(lane + base < z.columns, batch[:, base : base + LANES], near)
            local = jnp.where(lane + base < z.items, local, float(FAR))
            local_ref[pl.ds(u * z.half, z.half), base : base + LANES] = local.astype(jnp.int32)
    step = min(z.rows, 256)

    def pick(i, carry):
        at = rows_at(i * step, step)
        for base in range(0, z.lanes, LANES):
            local = local_ref[at, base : base + LANES]
            chunk, within = local >> 7, local & (LANES - 1)
            picked = jnp.zeros((step, LANES), jnp.float32)
            for j in range(z.chunks):
                found = jnp.take_along_axis(
                    score_ref[at, j * LANES : (j + 1) * LANES], within, axis=1
                )
                picked = jnp.where(chunk == j, found, picked)
            logit_ref[at, base : base + LANES] = picked
        return carry

    lax.fori_loop(0, z.rows // step, pick, 0, unroll=z.rows == step)
    pack_rows(z, logit_ref, part_ref)


def pack_rows(z, source_ref, target_ref):
    lane = lax.broadcasted_iota(jnp.int32, (z.packed, z.lanes), 1)
    packed = source_ref[pl.ds(0, z.packed), :]
    for h in range(1, z.pack):
        other = pltpu.roll(source_ref[pl.ds(h * z.packed, z.packed), :], h * z.items, 1)
        packed = jnp.where(lane < h * z.items, packed, other)
    target_ref[...] = packed


def index_kernel(z, local_ref, id_ref, index_ref, inside_ref, hot_ref):
    seat_rows(z, index_ref, lambda j: (local_ref, j * z.nrows, z.columns))
    pack_rows(z, local_ref, inside_ref)
    localize = localizer(z)
    lane = lax.broadcasted_iota(jnp.int32, (z.half, LANES), 1)
    for h in range(z.dp):
        at = pl.ds(h * z.half, z.half)
        pos = localize(jnp.broadcast_to(id_ref[at, z.pos_at : z.pos_at + 1], (z.half, LANES)))
        pos = pos.astype(jnp.int32)
        for j in range(z.chunks):
            same = jnp.where(pos == lane + j * LANES, 1.0, 0.0).astype(jnp.bfloat16)
            hot_ref[at, j * LANES : (j + 1) * LANES] = same


def stat_kernel(z, total_ref, inside_ref, exponent_ref, stat_ref):
    step = min(z.packed, 256)
    side = lax.axis_index("dp") & 1

    def one(i, carry):
        at = rows_at(i * step, step)
        logits = total_ref[at, :] * z.scale
        lane = lax.broadcasted_iota(jnp.int32, logits.shape, 1)
        row = lax.broadcasted_iota(jnp.int32, logits.shape, 0) + i * step
        short = lax.broadcasted_iota(jnp.int32, (step, LANES), 1)
        named = inside_ref[at, :] >= 0
        exponents = jnp.zeros(logits.shape, jnp.float32)
        stats = jnp.zeros((step, LANES), jnp.float32)
        for h in range(z.pack):
            mask = named & (lane >= h * z.items) & (lane < (h + 1) * z.items)
            top = jnp.max(jnp.where(mask, logits, LOW), axis=1, keepdims=True)
            exponent = jnp.where(mask, jnp.exp(logits - top), 0.0)
            query = row + h * z.packed
            own = (2 * (query // z.half) + side) * z.own + (query & (z.own - 1)) + h * z.items
            chosen = jnp.where(mask & (lane == own), logits, 0.0)
            values = (
                top,
                jnp.sum(exponent, axis=1, keepdims=True),
                jnp.sum(chosen, axis=1, keepdims=True),
            )
            for k, value in enumerate(values):
                stats = jnp.where(short == 3 * h + k, value, stats)
            exponents = exponents + exponent
        exponent_ref[at, :] = exponents
        stat_ref[:, at] = stats.T[: z.high, :]
        return carry

    lax.fori_loop(0, z.packed // step, one, 0, unroll=z.packed == step)


def split(values):
    parts = []
    for _ in range(3):
        part = values.astype(jnp.bfloat16)
        parts.append(part)
        values = values - part.astype(jnp.float32)
    return parts


def join(tiles):
    n = tiles.shape[0] // 3
    return tiles[:n] + (tiles[n : 2 * n] + tiles[2 * n :])


def place_kernel(z, exponent_ref, index_ref, hot_ref, raw_ref, seat_ref, part_ref, tile_ref):
    def seat(j):
        h, row = divmod(j * z.nrows, z.packed)
        return exponent_ref, row, h * z.items + z.columns

    seat_rows(z, seat_ref, seat)
    for k, part in enumerate(split(seat_ref[...])):
        part_ref[k] = part.astype(jnp.float32)
    high = z.seats * z.chunks
    shape = (high, z.deep)
    tall = lax.broadcasted_iota(jnp.int32, shape, 0).astype(jnp.bfloat16)
    shift = lax.broadcasted_iota(jnp.int32, (1, z.deep), 1) // z.negs * z.chunks
    spread = lax.broadcasted_iota(jnp.int32, (LANES, z.deep), 0).astype(jnp.bfloat16)
    turns = min(32, z.nrows)
    none, unit = jnp.bfloat16(0), jnp.bfloat16(1)

    def place(i, carry):
        for k in range(turns):
            r = i * turns + k
            local = index_ref[pl.ds(r, 1), :]
            chunk = ((local >> 7) + shift).astype(jnp.bfloat16)
            within = (local & (LANES - 1)).astype(jnp.bfloat16)
            here = jnp.broadcast_to(chunk, shape) == tall
            left = [
                jnp.where(
                    here,
                    jnp.broadcast_to(part_ref[p, pl.ds(r, 1), :].astype(jnp.bfloat16), shape), none,
                )
                for p in range(3)
            ]
            right = jnp.where(jnp.broadcast_to(within, (LANES, z.deep)) == spread, unit, none)
            tiles = join(lax.dot_general(
                jnp.concatenate(left, axis=0), right, (((1,), (1,)), ((), ())),
                preferred_element_type=jnp.float32,
            ))
            for j in range(z.seats):
                at = rows_at((j * z.nrows + r) * z.chunks, z.chunks)
                tile_ref[at, :] = tiles[j * z.chunks : (j + 1) * z.chunks, :]
        return carry

    lax.fori_loop(0, z.nrows // turns, place, 0, unroll=z.nrows == turns)
    lane = lax.broadcasted_iota(jnp.int32, (z.run, LANES), 1)
    group = lax.broadcasted_iota(jnp.int32, (z.run, LANES), 0) // z.own
    for n in range(z.sets):
        hot = [hot_ref[pl.ds(h * z.half + n * z.run, z.run), :] for h in range(z.dp)]
        hot = jnp.concatenate(hot, axis=0)
        for u in range(z.side):
            first_row = u * z.half + n * z.run
            side, row = divmod(first_row, z.packed)
            left = []
            for chunk in range(z.deep // LANES):
                if z.joint == 1:
                    part = exponent_ref[pl.ds(row, z.run), chunk * LANES : (chunk + 1) * LANES]
                else:
                    at = chunk * LANES + lane
                    from_lane = side * z.items + at // z.run * z.own + at % z.own
                    part = jnp.take_along_axis(
                        exponent_ref[pl.ds(row, z.run), :LANES], from_lane, axis=1
                    )
                    part = jnp.where(at // z.own % z.joint == group, part, 0.0)
                left.append(part)
            left = jnp.concatenate(split(jnp.concatenate(left, axis=1)), axis=0)
            shared = join(jnp.dot(left, hot, preferred_element_type=jnp.float32))
            for j in range(z.chunks):
                alone = tile_ref[pl.ds(first_row * z.chunks + j, z.run, stride=z.chunks), :]
                raw_ref[pl.ds(first_row, z.run), j * LANES : (j + 1) * LANES] = (
                    alone + shared[:, j * LANES : (j + 1) * LANES]
                )


def weight_kernel(z, *refs):
    count = z.side * z.cuts
    parts, refs = refs[:count], refs[count:]
    raw_ref, hot_ref, own_ref, other_ref = refs[:4]
    dense_refs, (loss_ref, size_ref) = refs[4:6], refs[6:8]
    grad_refs = refs[8 : 8 + z.side]
    stat_ref, row_ref, back_ref, sizes_ref = refs[8 + z.side :]
    d, t, c = places()
    for su in range(z.side):
        for sc in range(z.corpus):
            part = parts[su * z.cuts + sc % z.cuts][pl.ds(sc // z.cuts * z.high, z.high), :]
            stat_ref[((d >> 1) ^ su) * z.corpus + (c ^ z.corpus_order[sc])] = part
    planes = z.side * z.corpus
    row_ref[...] = jnp.zeros_like(row_ref)
    for h in range(z.pack):
        tops = [stat_ref[b, 3 * h : 3 * h + 1, :] for b in range(planes)]
        top = tops[0]
        for other in tops[1:]:
            top = jnp.maximum(top, other)
        total, chosen = jnp.zeros_like(top), jnp.zeros_like(top)
        for b in range(planes):
            total += stat_ref[b, 3 * h + 1 : 3 * h + 2, :] * jnp.exp(tops[b] - top)
            chosen += stat_ref[b, 3 * h + 2 : 3 * h + 3, :]
        mine = stat_ref[(d >> 1) * z.corpus + c, 3 * h : 3 * h + 1, :]
        rest = 1.0 - jnp.exp(chosen - top) / total
        row_ref[h : h + 1, :] = jnp.exp(mine - top) / total
        row_ref[z.pack + h : z.pack + h + 1, :] = jnp.maximum(rest, 2.0**-24)
        row_ref[2 * z.pack + h : 2 * z.pack + h + 1, :] = jnp.log(total) + top - chosen
    back_ref[...] = row_ref[...].T
    mine = (((d >> 1) * z.tensor + t) * z.corpus + c) * z.own
    place = rows_at(mine % z.packed, z.own)
    for k, target_ref in [(1, size_ref), (2, loss_ref)]:
        value = back_ref[place, k * z.pack : k * z.pack + 1]
        for h in range(1, z.pack):
            other = back_ref[place, k * z.pack + h : k * z.pack + h + 1]
            value = jnp.where(mine // z.packed == h, other, value)
        target_ref[...] = jnp.broadcast_to(value, (z.own, LANES))
    step = min(z.packed, 128)
    for h in range(z.pack):

        def one(i, carry):
            row = i * step
            query = h * z.packed + row
            at = rows_at(query, step)
            named = rows_at((2 * (query // z.half) + (d & 1)) * z.half + query % z.half, step)
            ratio = back_ref[rows_at(row, step), h : h + 1]
            weights = raw_ref[at, :] * ratio - hot_ref[named, :].astype(jnp.float32)
            weights = weights.astype(jnp.bfloat16)
            dense_refs[0][at, :] = weights[:, : z.block]
            dense_refs[1][at, :] = weights[:, z.block :]
            size = back_ref[rows_at(row, step), z.pack + h : z.pack + h + 1]
            sizes_ref[at, :] = jnp.broadcast_to(size, (step, LANES))
            return carry

        lax.fori_loop(0, z.packed // step, one, 0, unroll=z.packed == step)
    for s in range(z.side):
        at = rows_at(((d >> 1) ^ s) * z.half, z.half)
        grads = sum(
            jnp.dot(dense_ref[at, :], block_ref[...], preferred_element_type=jnp.float32)
            for dense_ref, block_ref in zip(dense_refs, (own_ref, other_ref))
        )
        grad_refs[s][...] = grads / sizes_ref[at, :1]


def passage_kernel(z, own_ref, query_ref, other_ref, other_query_ref, out_ref):
    def one(i, carry):
        at = rows_at(i * 256, 256)
        grads = [
            lax.dot_general(
                dense_ref[:, at], rows_ref[...], (((0,), (0,)), ((), ())),
                preferred_element_type=jnp.float32,
            )
            for dense_ref, rows_ref in [(own_ref, query_ref), (other_ref, other_query_ref)]
        ]
        out_ref[at, :] = z.scale * (grads[0] + grads[1])
        return carry

    lax.fori_loop(0, z.block // 256, one, 0)


def call(z, kernel, outs, scratch, args, flops, spaces=None, vmem=None):
    spaces = spaces or [pltpu.VMEM] * len(args)
    moved = sum(a.size * a.dtype.itemsize for a in args)
    moved += sum(o.size * jnp.dtype(o.dtype).itemsize for o in outs)
    return pl.pallas_call(
        lambda *refs: kernel(z, *refs),
        out_shape=outs,
        in_specs=[pl.BlockSpec(memory_space=space) for space in spaces],
        out_specs=[pl.BlockSpec(memory_space=pltpu.VMEM)] * len(outs),
        scratch_shapes=scratch,
        compiler_params=pltpu.CompilerParams(vmem_limit_bytes=vmem or z.vmem),
        cost_estimate=pl.CostEstimate(flops=flops, bytes_accessed=moved, transcendentals=0),
    )(*args)


def body(queries, passages, pos_ids, neg_ids):
    z = Sizes(queries, passages, neg_ids)
    f32, bf16, i32 = jnp.float32, jnp.bfloat16, jnp.int32
    shape = jax.ShapeDtypeStruct

    pieces = call(
        z, message_kernel, [shape((z.groups * z.fold, z.message), bf16)],
        [
            pltpu.SMEM(pos_ids.shape, i32), pltpu.VMEM(neg_ids.shape, i32),
            pltpu.VMEM(queries.shape, bf16), pltpu.SemaphoreType.DMA((3,)),
        ],
        [pos_ids, neg_ids, queries], 0, [pltpu.HBM] * 3, 60 * 2**20,
    )
    passages, pieces = lax.optimization_barrier((passages, pieces))
    (own_block,) = call(
        z, fetch_kernel, [shape(passages.shape, bf16)], [pltpu.SemaphoreType.DMA],
        [passages], 0, [pltpu.HBM],
    )
    other_block = swap(passages, "dp", 1)
    order = list(range(z.groups))
    order = [order[z.groups // 2 :] + order[: z.groups // 2]]
    chip = lax.all_to_all(
        pieces[0], ("tensor", "corpus"), split_axis=0, concat_axis=0, tiled=True,
        axis_index_groups=order,
    )
    chip = jnp.roll(chip, chip.shape[0] // 2, axis=0)
    chip, own_block, other_block = lax.optimization_barrier((chip, own_block, other_block))
    arrived = gather_pairs([chip])
    others = [swap(piece[:, z.message - LANES :], "dp", 1) for piece in arrived]
    blocks = [own_block, other_block]

    work = 2 * z.rows * z.wide * z.width
    query_rows, scores, own_ids, near = call(
        z, score_kernel,
        [shape((z.rows, z.width), bf16), shape((z.rows, z.wide), f32)]
        + [shape((z.rows, LANES), f32)] * 2, [],
        arrived + blocks, work,
    )
    part, local, ids = call(
        z, pick_kernel,
        [
            shape((z.packed, z.lanes), f32), shape((z.rows, z.lanes), i32),
            shape((z.named, LANES), f32),
        ],
        [pltpu.VMEM((z.rows, z.lanes), f32)], others + [scores, own_ids, near], work // 16,
    )
    index, inside, hot = call(
        z, index_kernel,
        [
            shape((z.nrows, z.deep), i32), shape((z.packed, z.lanes), i32),
            shape((z.named, z.wide), bf16),
        ],
        [], [local, ids], work // 64,
    )
    total = sum([swap(part, "tensor", s) for s in z.tensor_order], part)
    exponent, stat = call(
        z, stat_kernel, [shape((z.packed, z.lanes), f32), shape((z.high, z.packed), f32)], [],
        [total, inside], total.size,
    )
    stats = [swap(stat, "corpus", s) if s else stat for s in z.corpus_order]
    (raw,) = call(
        z, place_kernel, [shape((z.rows, z.wide), f32)],
        [
            pltpu.VMEM((z.nrows, z.deep), f32), pltpu.VMEM((3, z.nrows, z.deep), f32),
            pltpu.VMEM(((z.rows + 1) * z.chunks, LANES), f32),
        ],
        [exponent, index, hot], 3 * work,
    )
    if z.cuts == 1:
        stats = [jnp.concatenate(stats, axis=0)]
    stats = gather_pairs(stats)
    dense, other_dense, loss, size, *grads = call(
        z, weight_kernel,
        [shape((z.rows, z.block), bf16)] * 2 + [shape((z.own, LANES), f32)] * 2
        + [shape((z.half, z.width), f32)] * z.side,
        [
            pltpu.VMEM((z.side * z.corpus, z.high, z.packed), f32),
            pltpu.VMEM((LANES, z.packed), f32), pltpu.VMEM((z.packed, LANES), f32),
            pltpu.VMEM((z.rows, LANES), f32),
        ],
        stats + [raw, hot] + blocks, work,
    )
    half = scatter_pairs(grads).astype(jnp.float16)
    half = half.reshape(z.tensor, z.corpus, z.own, z.width).swapaxes(0, 1)
    half = jnp.roll(half, z.corpus // 2, axis=0)
    half = half.reshape(z.groups, z.own, z.width)
    half, other_dense = lax.optimization_barrier((half, other_dense))
    order = list(range(z.groups))
    order = [order[z.groups // 2 :] + order[: z.groups // 2]]
    half = lax.all_to_all(
        half, ("corpus", "tensor"), split_axis=0, concat_axis=0, tiled=True,
        axis_index_groups=order,
    )
    (grad_pass,) = call(
        z, passage_kernel, [shape((z.block, z.width), f32)], [],
        [dense, query_rows, swap(other_dense, "dp", 1), swap(query_rows, "dp", 1)], work,
    )
    half, grad_pass = lax.optimization_barrier((half, grad_pass))
    half = half.astype(f32).reshape(z.corpus, z.tensor, z.own, z.width).sum(axis=0)
    grad_query = half.swapaxes(0, 1).reshape(z.own, z.feat) * (size[:, :1] * z.scale)
    return (grad_query, loss[:, 0], grad_pass)


def solution(mesh):
    spread = ("dp", "tensor", "corpus")
    in_specs = (P(spread, None), P(("dp", "corpus"), "tensor"), P(spread), P(spread, None))
    out_specs = (P(spread, None), P(spread), P(("dp", "corpus"), "tensor"))
    return jax.shard_map(body, mesh=mesh, in_specs=in_specs, out_specs=out_specs, check_vma=False)
```

```python
import jax
import jax.numpy as jnp
from jax import lax
from jax.experimental import pallas as pl
from jax.experimental.pallas import tpu as pltpu
from jax.sharding import PartitionSpec as P

LANES = 128
FAR = -(2**20)
LOW = -1e30
SUM, ZED = [3, 2, 1], [0, 2, 3, 1]


def swap(value, axis, bit):
    size = lax.axis_size(axis)
    return lax.ppermute(value, axis, [(i, i ^ bit) for i in range(size)])


def gather_pairs(pieces):
    bit = 2
    while bit < lax.axis_size("dp"):
        pieces = pieces + [swap(piece, "dp", bit) for piece in pieces]
        bit *= 2
    return pieces


def scatter_pairs(pieces):
    while len(pieces) > 1:
        n = len(pieces) // 2
        pieces = [
            mine + swap(theirs, "dp", 2 * n) for mine, theirs in zip(pieces[:n], pieces[n:])
        ]
    return pieces[0]


class Sizes:
    def __init__(self, queries, passages, neg_ids):
        self.own, self.feat = queries.shape
        self.block, self.width = passages.shape
        self.negs = neg_ids.shape[1]
        self.dp = lax.axis_size("dp")
        self.tensor = lax.axis_size("tensor")
        self.corpus = lax.axis_size("corpus")
        self.side = self.dp // 2
        self.groups = self.tensor * self.corpus
        self.half = self.groups * self.own
        self.rows = self.side * self.half
        self.named = self.dp * self.half
        self.columns = self.dp * self.own
        self.items = self.columns + self.negs
        self.lanes = -(-self.items // LANES) * LANES
        self.pack = max(1, LANES // self.items)
        self.packed = self.rows // self.pack
        self.neg_at = self.columns % LANES
        self.pos_at = 0 if self.neg_at else self.negs
        self.wide = 2 * self.block
        self.chunks = self.wide // LANES
        self.scale = self.feat ** (-0.5)
        self.tensor_order = SUM if self.tensor == 4 else list(range(1, self.tensor))
        self.corpus_order = ZED if self.corpus == 4 else list(range(self.corpus))
        self.cuts = self.corpus if self.side == 1 else 1
        self.deep = 2 * LANES
        self.seats = self.deep // self.negs
        self.nrows = self.rows // self.seats
        self.joint = max(1, self.deep // self.columns)
        self.run = self.joint * self.own
        self.sets = self.groups // self.joint
        self.high = -(-3 * self.pack // 8) * 8
        self.dense_ids = self.block * self.dp * self.corpus <= 2**13 and self.own == 16
        self.fold = self.own // 2 if self.dense_ids else self.own
        self.message = 2 * self.width + LANES if self.dense_ids else self.width + LANES
        self.vmem = min(61, 20 + 20 * self.rows // 1024) * 2**20


def places():
    return [lax.axis_index(axis) for axis in ("dp", "tensor", "corpus")]


def rows_at(start, size):
    return pl.ds(pl.multiple_of(start, size), size)


def message_kernel(z, pos_in, neg_in, query_in, out_ref, pos_ref, neg_ref, query_ref, sems):
    moves = [
        pltpu.make_async_copy(source, target, sems.at[i])
        for i, (source, target) in enumerate(
            [(pos_in, pos_ref), (neg_in, neg_ref), (query_in, query_ref)]
        )
    ]
    for move in moves:
        move.start()
    for move in moves:
        move.wait()
    half = LANES // 2
    row = lax.broadcasted_iota(jnp.int32, (z.own, half), 0)
    pos = jnp.zeros((z.own, half), jnp.int32)
    for i in range(z.own):
        pos = jnp.where(row == i, pos_ref[i], pos)
    ids = [neg_ref[...], pos[:, : half - z.neg_at - z.negs]]
    ids = jnp.concatenate([part for part in [pos[:, : z.neg_at]] + ids if part.shape[1]], axis=1)
    if z.dense_ids:
        code = 1.0 + (ids & 127).astype(jnp.float32) / 128.0
        for bit in range(6):
            code = jnp.where((ids >> (7 + bit)) & 1 == 1, code * 2.0 ** (1 << bit), code)
        code = code * 2.0**-32
        code = jnp.concatenate([code[: z.fold], code[z.fold :]], axis=1)
        for t in range(z.tensor):
            rows = query_ref[:, t * z.width : (t + 1) * z.width].astype(jnp.float32)
            rows = jnp.concatenate([rows[: z.fold], rows[z.fold :], code], axis=1)
            rows = jnp.concatenate([rows, rows], axis=0).astype(jnp.bfloat16)
            for c in range(0, z.corpus, 2):
                k = (t * z.corpus + c + z.groups // 2) % z.groups
                out_ref[pl.ds(k * z.fold, z.own), :] = rows
        return
    ids = jnp.concatenate([ids >> 8, ids & 255], axis=1)
    code = ids.astype(jnp.float32).astype(jnp.bfloat16)
    for k in range(z.groups):
        t = (k + z.groups // 2) % z.groups // z.corpus
        at = pl.ds(k * z.own, z.own)
        out_ref[at, : z.width] = query_ref[:, t * z.width : (t + 1) * z.width]
        out_ref[at, z.width :] = code


def unfold(z, first, second):
    width = first.shape[-1]
    pair = [part.reshape(z.groups, z.fold, width) for part in (first, second)]
    return jnp.concatenate(pair, axis=1).reshape(z.half, width)


def decode(z, code):
    code = code.astype(jnp.float32)
    if not z.dense_ids:
        return code * 256.0 + pltpu.roll(code, LANES // 2, 1)
    code = code * 2.0**32
    high = jnp.zeros_like(code)
    for bit in range(5, -1, -1):
        big = code >= 2.0 ** (1 << bit)
        high = jnp.where(big, high + float(128 << bit), high)
        code = jnp.where(big, code * 2.0 ** -(1 << bit), code)
    ids = high + (code - 1.0) * 128.0
    return unfold(z, ids, pltpu.roll(ids, LANES // 2, 1))


def fetch_kernel(z, block_ref, passage_ref, sem):
    fetch = pltpu.make_async_copy(block_ref, passage_ref, sem)
    fetch.start()
    fetch.wait()


def seat_rows(z, out_ref, source):
    lane = lax.broadcasted_iota(jnp.int32, (z.nrows, LANES), 1)
    per = LANES // z.negs
    for chunk in range(z.deep // LANES):
        packed = None
        for k in range(per):
            ref, row, at = source(chunk * per + k)
            base = at // LANES * LANES
            piece = ref[pl.ds(row, z.nrows), base : base + LANES]
            turn = (k * z.negs - at) % LANES
            piece = pltpu.roll(piece, turn, 1) if turn else piece
            packed = piece if packed is None else jnp.where(lane < k * z.negs, packed, piece)
        out_ref[:, chunk * LANES : (chunk + 1) * LANES] = packed


def score_kernel(z, *refs):
    arrived, block_refs = refs[: z.side], refs[z.side : z.side + 2]
    query_ref, score_ref, own_ref, near_ref = refs[z.side + 2 :]
    d = lax.axis_index("dp")
    localize = localizer(z)
    for su in range(z.side):
        at = rows_at(((d ^ (2 * su)) >> 1) * z.half, z.half)
        rows = arrived[su][:, : z.message - LANES]
        if z.dense_ids:
            rows = rows.astype(jnp.float32)
            rows = unfold(z, rows[:, : z.width], rows[:, z.width :]).astype(jnp.bfloat16)
        query_ref[at, :] = rows
        ids = decode(z, arrived[su][:, z.message - LANES :])
        own_ref[at, :] = ids
        near_ref[at, :] = localize(ids)
    step = min(z.rows, 256)

    def score(i, carry):
        at = rows_at(i * step, step)
        for side, block_ref in enumerate(block_refs):
            score_ref[at, side * z.block : (side + 1) * z.block] = lax.dot_general(
                query_ref[at, :], block_ref[...], (((1,), (1,)), ((), ())),
                preferred_element_type=jnp.float32,
            )
        return carry

    lax.fori_loop(0, z.rows // step, score, 0, unroll=z.rows == step)


def localizer(z):
    d, _, c = places()

    def localize(ids):
        found = jnp.full(ids.shape, float(FAR), jnp.float32)
        for side in range(2):
            local = ids - (((d ^ side) * z.corpus + c) * z.block).astype(jnp.float32)
            inside = (local >= 0.0) & (local < float(z.block))
            found = jnp.where(inside, local + float(side * z.block), found)
        return found

    return localize


def pick_kernel(z, *refs):
    others, (score_ref, own_ref, near_ref) = refs[: z.side], refs[z.side : z.side + 3]
    part_ref, local_ref, id_ref, logit_ref = refs[z.side + 3 :]
    d = lax.axis_index("dp")
    for su in range(z.side):
        from_d = d ^ (2 * su)
        own = own_ref[rows_at((from_d >> 1) * z.half, z.half), :]
        id_ref[rows_at(from_d * z.half, z.half), :] = own
        id_ref[rows_at((from_d ^ 1) * z.half, z.half), :] = decode(z, others[su][...])
    wide = -(-z.columns // LANES) * LANES
    row = lax.broadcasted_iota(jnp.int32, (z.half, wide), 0) & (z.own - 1)
    col = lax.broadcasted_iota(jnp.int32, (z.half, wide), 1)
    group_ids = jnp.zeros((z.groups, wide), jnp.float32)
    for h in range(z.dp):
        at = pl.ds(h * z.half, z.half)
        pos = jnp.broadcast_to(id_ref[at, z.pos_at : z.pos_at + 1], (z.half, wide))
        kept = jnp.where(col == row + h * z.own, pos, 0.0)
        group_ids += jnp.sum(kept.reshape(z.groups, z.own, wide), axis=1)
    batch = jnp.broadcast_to(localizer(z)(group_ids)[:, None, :], (z.groups, z.own, wide))
    batch = batch.reshape(z.half, wide)
    lane = lax.broadcasted_iota(jnp.int32, (z.half, LANES), 1)
    for u in range(z.side):
        near = near_ref[pl.ds(u * z.half, z.half), :]
        for base in range(0, z.lanes, LANES):
            local = near
            if base < z.columns:
                local = jnp.where(lane + base < z.columns, batch[:, base : base + LANES], near)
            local = jnp.where(lane + base < z.items, local, float(FAR))
            local_ref[pl.ds(u * z.half, z.half), base : base + LANES] = local.astype(jnp.int32)
    step = min(z.rows, 256)

    def pick(i, carry):
        at = rows_at(i * step, step)
        for base in range(0, z.lanes, LANES):
            local = local_ref[at, base : base + LANES]
            chunk, within = local >> 7, local & (LANES - 1)
            picked = jnp.zeros((step, LANES), jnp.float32)
            for j in range(z.chunks):
                found = jnp.take_along_axis(
                    score_ref[at, j * LANES : (j + 1) * LANES], within, axis=1
                )
                picked = jnp.where(chunk == j, found, picked)
            logit_ref[at, base : base + LANES] = picked
        return carry

    lax.fori_loop(0, z.rows // step, pick, 0, unroll=z.rows == step)
    pack_rows(z, logit_ref, part_ref)


def pack_rows(z, source_ref, target_ref):
    lane = lax.broadcasted_iota(jnp.int32, (z.packed, z.lanes), 1)
    packed = source_ref[pl.ds(0, z.packed), :]
    for h in range(1, z.pack):
        other = pltpu.roll(source_ref[pl.ds(h * z.packed, z.packed), :], h * z.items, 1)
        packed = jnp.where(lane < h * z.items, packed, other)
    target_ref[...] = packed


def index_kernel(z, local_ref, id_ref, index_ref, inside_ref, hot_ref):
    seat_rows(z, index_ref, lambda j: (local_ref, j * z.nrows, z.columns))
    pack_rows(z, local_ref, inside_ref)
    localize = localizer(z)
    lane = lax.broadcasted_iota(jnp.int32, (z.half, LANES), 1)
    for h in range(z.dp):
        at = pl.ds(h * z.half, z.half)
        pos = localize(jnp.broadcast_to(id_ref[at, z.pos_at : z.pos_at + 1], (z.half, LANES)))
        pos = pos.astype(jnp.int32)
        for j in range(z.chunks):
            same = jnp.where(pos == lane + j * LANES, 1.0, 0.0).astype(jnp.bfloat16)
            hot_ref[at, j * LANES : (j + 1) * LANES] = same


def stat_kernel(z, total_ref, inside_ref, exponent_ref, stat_ref):
    step = min(z.packed, 256)
    side = lax.axis_index("dp") & 1

    def one(i, carry):
        at = rows_at(i * step, step)
        logits = total_ref[at, :] * z.scale
        lane = lax.broadcasted_iota(jnp.int32, logits.shape, 1)
        row = lax.broadcasted_iota(jnp.int32, logits.shape, 0) + i * step
        short = lax.broadcasted_iota(jnp.int32, (step, LANES), 1)
        named = inside_ref[at, :] >= 0
        exponents = jnp.zeros(logits.shape, jnp.float32)
        stats = jnp.zeros((step, LANES), jnp.float32)
        for h in range(z.pack):
            mask = named & (lane >= h * z.items) & (lane < (h + 1) * z.items)
            top = jnp.max(jnp.where(mask, logits, LOW), axis=1, keepdims=True)
            exponent = jnp.where(mask, jnp.exp(logits - top), 0.0)
            query = row + h * z.packed
            own = (2 * (query // z.half) + side) * z.own + (query & (z.own - 1)) + h * z.items
            chosen = jnp.where(mask & (lane == own), logits, 0.0)
            values = (
                top,
                jnp.sum(exponent, axis=1, keepdims=True),
                jnp.sum(chosen, axis=1, keepdims=True),
            )
            for k, value in enumerate(values):
                stats = jnp.where(short == 3 * h + k, value, stats)
            exponents = exponents + exponent
        exponent_ref[at, :] = exponents
        stat_ref[:, at] = stats.T[: z.high, :]
        return carry

    lax.fori_loop(0, z.packed // step, one, 0, unroll=z.packed == step)


def split(values):
    parts = []
    for _ in range(3):
        part = values.astype(jnp.bfloat16)
        parts.append(part)
        values = values - part.astype(jnp.float32)
    return parts


def join(tiles):
    n = tiles.shape[0] // 3
    return tiles[:n] + (tiles[n : 2 * n] + tiles[2 * n :])


def place_kernel(z, exponent_ref, index_ref, hot_ref, raw_ref, seat_ref, part_ref, tile_ref):
    def seat(j):
        h, row = divmod(j * z.nrows, z.packed)
        return exponent_ref, row, h * z.items + z.columns

    seat_rows(z, seat_ref, seat)
    for k, part in enumerate(split(seat_ref[...])):
        part_ref[k] = part.astype(jnp.float32)
    high = z.seats * z.chunks
    shape = (high, z.deep)
    tall = lax.broadcasted_iota(jnp.int32, shape, 0).astype(jnp.bfloat16)
    shift = lax.broadcasted_iota(jnp.int32, (1, z.deep), 1) // z.negs * z.chunks
    spread = lax.broadcasted_iota(jnp.int32, (LANES, z.deep), 0).astype(jnp.bfloat16)
    turns = min(32, z.nrows)
    none, unit = jnp.bfloat16(0), jnp.bfloat16(1)

    def place(i, carry):
        for k in range(turns):
            r = i * turns + k
            local = index_ref[pl.ds(r, 1), :]
            chunk = ((local >> 7) + shift).astype(jnp.bfloat16)
            within = (local & (LANES - 1)).astype(jnp.bfloat16)
            here = jnp.broadcast_to(chunk, shape) == tall
            left = [
                jnp.where(
                    here,
                    jnp.broadcast_to(part_ref[p, pl.ds(r, 1), :].astype(jnp.bfloat16), shape), none,
                )
                for p in range(3)
            ]
            right = jnp.where(jnp.broadcast_to(within, (LANES, z.deep)) == spread, unit, none)
            tiles = join(lax.dot_general(
                jnp.concatenate(left, axis=0), right, (((1,), (1,)), ((), ())),
                preferred_element_type=jnp.float32,
            ))
            for j in range(z.seats):
                at = rows_at((j * z.nrows + r) * z.chunks, z.chunks)
                tile_ref[at, :] = tiles[j * z.chunks : (j + 1) * z.chunks, :]
        return carry

    lax.fori_loop(0, z.nrows // turns, place, 0, unroll=z.nrows == turns)
    lane = lax.broadcasted_iota(jnp.int32, (z.run, LANES), 1)
    group = lax.broadcasted_iota(jnp.int32, (z.run, LANES), 0) // z.own
    for n in range(z.sets):
        hot = [hot_ref[pl.ds(h * z.half + n * z.run, z.run), :] for h in range(z.dp)]
        hot = jnp.concatenate(hot, axis=0)
        for u in range(z.side):
            first_row = u * z.half + n * z.run
            side, row = divmod(first_row, z.packed)
            left = []
            for chunk in range(z.deep // LANES):
                if z.joint == 1:
                    part = exponent_ref[pl.ds(row, z.run), chunk * LANES : (chunk + 1) * LANES]
                else:
                    at = chunk * LANES + lane
                    from_lane = side * z.items + at // z.run * z.own + at % z.own
                    part = jnp.take_along_axis(
                        exponent_ref[pl.ds(row, z.run), :LANES], from_lane, axis=1
                    )
                    part = jnp.where(at // z.own % z.joint == group, part, 0.0)
                left.append(part)
            left = jnp.concatenate(split(jnp.concatenate(left, axis=1)), axis=0)
            shared = join(jnp.dot(left, hot, preferred_element_type=jnp.float32))
            for j in range(z.chunks):
                alone = tile_ref[pl.ds(first_row * z.chunks + j, z.run, stride=z.chunks), :]
                raw_ref[pl.ds(first_row, z.run), j * LANES : (j + 1) * LANES] = (
                    alone + shared[:, j * LANES : (j + 1) * LANES]
                )


def weight_kernel(z, *refs):
    count = z.side * z.cuts
    parts, refs = refs[:count], refs[count:]
    raw_ref, hot_ref, own_ref, other_ref = refs[:4]
    dense_refs, (loss_ref, size_ref) = refs[4:6], refs[6:8]
    grad_refs = refs[8 : 8 + z.side]
    stat_ref, row_ref, back_ref, sizes_ref = refs[8 + z.side :]
    d, t, c = places()
    for su in range(z.side):
        for sc in range(z.corpus):
            part = parts[su * z.cuts + sc % z.cuts][pl.ds(sc // z.cuts * z.high, z.high), :]
            stat_ref[((d >> 1) ^ su) * z.corpus + (c ^ z.corpus_order[sc])] = part
    planes = z.side * z.corpus
    row_ref[...] = jnp.zeros_like(row_ref)
    for h in range(z.pack):
        tops = [stat_ref[b, 3 * h : 3 * h + 1, :] for b in range(planes)]
        top = tops[0]
        for other in tops[1:]:
            top = jnp.maximum(top, other)
        total, chosen = jnp.zeros_like(top), jnp.zeros_like(top)
        for b in range(planes):
            total += stat_ref[b, 3 * h + 1 : 3 * h + 2, :] * jnp.exp(tops[b] - top)
            chosen += stat_ref[b, 3 * h + 2 : 3 * h + 3, :]
        mine = stat_ref[(d >> 1) * z.corpus + c, 3 * h : 3 * h + 1, :]
        rest = 1.0 - jnp.exp(chosen - top) / total
        row_ref[h : h + 1, :] = jnp.exp(mine - top) / total
        row_ref[z.pack + h : z.pack + h + 1, :] = jnp.maximum(rest, 2.0**-24)
        row_ref[2 * z.pack + h : 2 * z.pack + h + 1, :] = jnp.log(total) + top - chosen
    back_ref[...] = row_ref[...].T
    mine = (((d >> 1) * z.tensor + t) * z.corpus + c) * z.own
    place = rows_at(mine % z.packed, z.own)
    for k, target_ref in [(1, size_ref), (2, loss_ref)]:
        value = back_ref[place, k * z.pack : k * z.pack + 1]
        for h in range(1, z.pack):
            other = back_ref[place, k * z.pack + h : k * z.pack + h + 1]
            value = jnp.where(mine // z.packed == h, other, value)
        target_ref[...] = jnp.broadcast_to(value, (z.own, LANES))
    step = min(z.packed, 128)
    for h in range(z.pack):

        def one(i, carry):
            row = i * step
            query = h * z.packed + row
            at = rows_at(query, step)
            named = rows_at((2 * (query // z.half) + (d & 1)) * z.half + query % z.half, step)
            ratio = back_ref[rows_at(row, step), h : h + 1]
            weights = raw_ref[at, :] * ratio - hot_ref[named, :].astype(jnp.float32)
            weights = weights.astype(jnp.bfloat16)
            dense_refs[0][at, :] = weights[:, : z.block]
            dense_refs[1][at, :] = weights[:, z.block :]
            size = back_ref[rows_at(row, step), z.pack + h : z.pack + h + 1]
            sizes_ref[at, :] = jnp.broadcast_to(size, (step, LANES))
            return carry

        lax.fori_loop(0, z.packed // step, one, 0, unroll=z.packed == step)
    for s in range(z.side):
        at = rows_at(((d >> 1) ^ s) * z.half, z.half)
        grads = sum(
            jnp.dot(dense_ref[at, :], block_ref[...], preferred_element_type=jnp.float32)
            for dense_ref, block_ref in zip(dense_refs, (own_ref, other_ref))
        )
        grad_refs[s][...] = grads / sizes_ref[at, :1]


def passage_kernel(z, own_ref, query_ref, other_ref, other_query_ref, out_ref):
    def one(i, carry):
        at = rows_at(i * 256, 256)
        grads = [
            lax.dot_general(
                dense_ref[:, at], rows_ref[...], (((0,), (0,)), ((), ())),
                preferred_element_type=jnp.float32,
            )
            for dense_ref, rows_ref in [(own_ref, query_ref), (other_ref, other_query_ref)]
        ]
        out_ref[at, :] = z.scale * (grads[0] + grads[1])
        return carry

    lax.fori_loop(0, z.block // 256, one, 0)


def call(z, kernel, outs, scratch, args, flops, spaces=None, vmem=None):
    spaces = spaces or [pltpu.VMEM] * len(args)
    moved = sum(a.size * a.dtype.itemsize for a in args)
    moved += sum(o.size * jnp.dtype(o.dtype).itemsize for o in outs)
    return pl.pallas_call(
        lambda *refs: kernel(z, *refs),
        out_shape=outs,
        in_specs=[pl.BlockSpec(memory_space=space) for space in spaces],
        out_specs=[pl.BlockSpec(memory_space=pltpu.VMEM)] * len(outs),
        scratch_shapes=scratch,
        compiler_params=pltpu.CompilerParams(vmem_limit_bytes=vmem or z.vmem),
        cost_estimate=pl.CostEstimate(flops=flops, bytes_accessed=moved, transcendentals=0),
    )(*args)


def body(queries, passages, pos_ids, neg_ids):
    z = Sizes(queries, passages, neg_ids)
    f32, bf16, i32 = jnp.float32, jnp.bfloat16, jnp.int32
    shape = jax.ShapeDtypeStruct

    pieces = call(
        z, message_kernel, [shape((z.groups * z.fold, z.message), bf16)],
        [
            pltpu.SMEM(pos_ids.shape, i32), pltpu.VMEM(neg_ids.shape, i32),
            pltpu.VMEM(queries.shape, bf16), pltpu.SemaphoreType.DMA((3,)),
        ],
        [pos_ids, neg_ids, queries], 0, [pltpu.HBM] * 3, 60 * 2**20,
    )
    passages, pieces = lax.optimization_barrier((passages, pieces))
    (own_block,) = call(
        z, fetch_kernel, [shape(passages.shape, bf16)], [pltpu.SemaphoreType.DMA],
        [passages], 0, [pltpu.HBM],
    )
    other_block = swap(passages, "dp", 1)
    order = list(range(z.groups))
    order = [order[z.groups // 2 :] + order[: z.groups // 2]]
    chip = lax.all_to_all(
        pieces[0], ("tensor", "corpus"), split_axis=0, concat_axis=0, tiled=True,
        axis_index_groups=order,
    )
    chip = jnp.roll(chip, chip.shape[0] // 2, axis=0)
    chip, own_block, other_block = lax.optimization_barrier((chip, own_block, other_block))
    arrived = gather_pairs([chip])
    others = [swap(piece[:, z.message - LANES :], "dp", 1) for piece in arrived]
    blocks = [own_block, other_block]

    work = 2 * z.rows * z.wide * z.width
    query_rows, scores, own_ids, near = call(
        z, score_kernel,
        [shape((z.rows, z.width), bf16), shape((z.rows, z.wide), f32)]
        + [shape((z.rows, LANES), f32)] * 2, [],
        arrived + blocks, work,
    )
    part, local, ids = call(
        z, pick_kernel,
        [
            shape((z.packed, z.lanes), f32), shape((z.rows, z.lanes), i32),
            shape((z.named, LANES), f32),
        ],
        [pltpu.VMEM((z.rows, z.lanes), f32)], others + [scores, own_ids, near], work // 16,
    )
    index, inside, hot = call(
        z, index_kernel,
        [
            shape((z.nrows, z.deep), i32), shape((z.packed, z.lanes), i32),
            shape((z.named, z.wide), bf16),
        ],
        [], [local, ids], work // 64,
    )
    total = sum([swap(part, "tensor", s) for s in z.tensor_order], part)
    exponent, stat = call(
        z, stat_kernel, [shape((z.packed, z.lanes), f32), shape((z.high, z.packed), f32)], [],
        [total, inside], total.size,
    )
    stats = [swap(stat, "corpus", s) if s else stat for s in z.corpus_order]
    (raw,) = call(
        z, place_kernel, [shape((z.rows, z.wide), f32)],
        [
            pltpu.VMEM((z.nrows, z.deep), f32), pltpu.VMEM((3, z.nrows, z.deep), f32),
            pltpu.VMEM(((z.rows + 1) * z.chunks, LANES), f32),
        ],
        [exponent, index, hot], 3 * work,
    )
    if z.cuts == 1:
        stats = [jnp.concatenate(stats, axis=0)]
    stats = gather_pairs(stats)
    dense, other_dense, loss, size, *grads = call(
        z, weight_kernel,
        [shape((z.rows, z.block), bf16)] * 2 + [shape((z.own, LANES), f32)] * 2
        + [shape((z.half, z.width), f32)] * z.side,
        [
            pltpu.VMEM((z.side * z.corpus, z.high, z.packed), f32),
            pltpu.VMEM((LANES, z.packed), f32), pltpu.VMEM((z.packed, LANES), f32),
            pltpu.VMEM((z.rows, LANES), f32),
        ],
        stats + [raw, hot] + blocks, work,
    )
    half = scatter_pairs(grads).astype(jnp.float16)
    half = half.reshape(z.tensor, z.corpus, z.own, z.width).swapaxes(0, 1)
    half = jnp.roll(half, (z.corpus // 2, z.tensor // 2), axis=(0, 1))
    half = half.reshape(z.groups, z.own, z.width)
    half, other_dense = lax.optimization_barrier((half, other_dense))
    turned = [(c + z.corpus // 2) % z.corpus for c in range(z.corpus)]
    order = [[c * z.tensor + (t + z.tensor // 2) % z.tensor for c in turned for t in range(z.tensor)]]
    half = lax.all_to_all(
        half, ("corpus", "tensor"), split_axis=0, concat_axis=0, tiled=True,
        axis_index_groups=order,
    )
    (grad_pass,) = call(
        z, passage_kernel, [shape((z.block, z.width), f32)], [],
        [dense, query_rows, swap(other_dense, "dp", 1), swap(query_rows, "dp", 1)], work,
    )
    half, grad_pass = lax.optimization_barrier((half, grad_pass))
    half = half.astype(f32).reshape(z.corpus, z.tensor, z.own, z.width).sum(axis=0)
    half = jnp.roll(half, z.tensor // 2, axis=0)
    grad_query = half.swapaxes(0, 1).reshape(z.own, z.feat) * (size[:, :1] * z.scale)
    return (grad_query, loss[:, 0], grad_pass)


def solution(mesh):
    spread = ("dp", "tensor", "corpus")
    in_specs = (P(spread, None), P(("dp", "corpus"), "tensor"), P(spread), P(spread, None))
    out_specs = (P(spread, None), P(spread), P(("dp", "corpus"), "tensor"))
    return jax.shard_map(body, mesh=mesh, in_specs=in_specs, out_specs=out_specs, check_vma=False)
```
